32 devices in a mesh: frames: 16 (over z, x, core), pos: 2 (over y).
Axes of the slice: x: 2, y: 2, z: 4, core: 2. Of those that a mesh axis runs over, the one named last changes fastest.
Arguments:
- frames_in: bfloat16 [3584, 2, 1024], P('frames', 'pos'), may hold values from -6 to 6
- code_table: bfloat16 [2, 2048, 1024], P('pos', 'frames'), may hold values from -6 to 6
- code_ids: int32 [3584, 2], P('frames', 'pos'), may hold values from 0 to 2047
- delays: int32 [3, 2], P(None, 'pos'), may hold values from 1 to 2, as said below
- item_lengths: int32 [3], replicated, may hold values from 1 to 3360, as said below
- w_qkv: bfloat16 [2, 2, 1024, 3072], P(None, 'pos', 'frames'), may hold values from -0.1875 to 0.1875
- w_out: bfloat16 [2, 2, 1024, 1024], P(None, 'pos', 'frames'), may hold values from -0.25 to 0.25
- w_gate: bfloat16 [2, 2, 1024, 4096], P(None, 'pos', 'frames'), may hold values from -0.1875 to 0.1875
- w_up: bfloat16 [2, 2, 1024, 4096], P(None, 'pos', 'frames'), may hold values from -0.1875 to 0.1875
- w_down: bfloat16 [2, 2, 4096, 1024], P(None, 'pos', 'frames'), may hold values from -0.1875 to 0.1875
- gain_attn: bfloat16 [2, 2, 1024], P(None, 'pos', 'frames'), may hold values from 0.099609375 to 1.8984375
- gain_ffn: bfloat16 [2, 2, 1024], P(None, 'pos', 'frames'), may hold values from 0.099609375 to 1.8984375
- cotangent: bfloat16 [3584, 2, 1024], P('frames', 'pos'), may hold values from -6 to 6
Outputs:
- activations: bfloat16 [3584, 2, 1024], P('frames', 'pos')
- input_grad: float32 [3584, 2, 1024], P('frames', 'pos')
- table_grad: float32 [2, 2048, 1024], P('pos', 'frames')
- qkv_grad: float32 [2, 2, 1024, 3072], P(None, 'pos', 'frames')
- out_grad: float32 [2, 2, 1024, 1024], P(None, 'pos', 'frames')
- gate_grad: float32 [2, 2, 1024, 4096], P(None, 'pos', 'frames')
- up_grad: float32 [2, 2, 1024, 4096], P(None, 'pos', 'frames')
- down_grad: float32 [2, 2, 4096, 1024], P(None, 'pos', 'frames')
- attn_gain_grad: float32 [2, 2, 1024], P(None, 'pos', 'frames')
- ffn_gain_grad: float32 [2, 2, 1024], P(None, 'pos', 'frames')
The draws below stay inside these ranges and needn't reach their ends.
Inputs may be any that keep to these rules, and one draw needn't show every extreme that they name: delays in frames; both values occur in every draw. `item_lengths`: 3 item lengths, each at least 1, summing to 3584; the longest has exactly 3360 frames.
All inputs are finite; a program needn't handle non-finite values.
Results may differ from the reference program's by a relative error of at most 0.017.
Values may be sent and summed in bfloat16 or wider, within the bound.
A program may use at most 320 MiB of HBM per device.

```python
import math
import jax
import jax.numpy as jnp
import numpy as np
from jax import lax

D = 1024
HEADS = 16
HD = 64
FF = 4096
V = 2048
LAYERS = 2
ITEMS = 3
FR_DEV = 224
P_SIZE = 2
FRAMES = 3584
N_FRAMES = 16


def draw_delays(key, part):
    key = jax.random.fold_in(key, 12)
    flat = jax.random.randint(key, (ITEMS * P_SIZE,), 0, 2).astype(jnp.int32)
    flat = flat.at[0].set(1 - flat[1])
    return (flat + 1).reshape(ITEMS, P_SIZE).astype(jnp.int32)


def draw_item_lengths(key, part):
    key = jax.random.fold_in(key, 11)
    first_len = jax.random.randint(key, (), 1, FR_DEV).astype(jnp.int32)
    middle_len = jnp.asarray(FR_DEV * N_FRAMES - FR_DEV, jnp.int32)
    return jnp.stack([first_len, middle_len, FR_DEV - first_len]).astype(jnp.int32)


def set_ends(values, stream_key, low, high):
    shape = values.shape
    place = [jax.random.randint(jax.random.fold_in(stream_key, axis), (), 0, shape[axis]) for axis in range(len(shape))]
    values = values.at[tuple(place)].set(low)
    longest = shape.index(max(shape))
    place[longest] = (place[longest] + 1) % shape[longest]
    return values.at[tuple(place)].set(high)


def shard_levels(stream_key, extent, pieces, low, top_value):
    def one(dim, shards_of):
        steps = jax.random.uniform(jax.random.fold_in(jax.random.fold_in(stream_key, 6), dim), (shards_of,), jnp.float32, low / len(pieces), top_value / len(pieces))
        return jnp.repeat(jnp.exp(steps), extent[dim] // shards_of).reshape((-1,) + (1,) * (len(extent) - dim - 1))

    loudness = one(*pieces[0])
    for cut in pieces[1:]:
        loudness = loudness * one(*cut)
    return loudness


def rank_table(number_of, lean):
    loads = [(1 << 20) // math.isqrt(rank ** lean) + 1 for rank in range(1, number_of + 1)]
    width = 1 + sum(loads) // (1 << 30)
    return np.cumsum(np.array([max(1, weight // width) for weight in loads]))


def ranked_ids(own_key, extent, number_of, slope):
    listing = rank_table(number_of, slope)
    ticket = jax.random.randint(jax.random.fold_in(own_key, 1), extent, 0, int(listing[number_of - 1]))
    rank = jnp.searchsorted(jnp.asarray(listing, jnp.int32), ticket, side="right")
    return jax.random.permutation(jax.random.fold_in(own_key, 2), number_of)[rank].astype(jnp.int32)


def normal_values(key, extent, scale, bound, cuts=(), kind=jnp.bfloat16):
    factor_of = shard_levels(key, extent, cuts, -0.22, 0.18) if cuts else 1.0
    result = jax.random.normal(key, extent, jnp.float32) * scale * factor_of
    return jnp.minimum(jnp.maximum(result, -bound), bound).astype(kind)


def setup_inputs(seed: int = 0) -> dict:
    key_of = jax.random.split(jax.random.key(seed), 14)
    frames_in = normal_values(key_of[0], (FRAMES, P_SIZE, D), 1.0, 6.0, ((0, 16), (1, 2)))
    code_table = normal_values(key_of[1], (P_SIZE, V, D), 1.0, 6.0, ((0, 2), (1, 16)))
    code_ids = set_ends(ranked_ids(key_of[2], (FRAMES, P_SIZE), V, 2), jax.random.fold_in(key_of[2], 3), 0, V - 1).astype(jnp.int32)
    delays = draw_delays(jax.random.fold_in(key_of[13], 71), 0)
    item_lengths = draw_item_lengths(jax.random.fold_in(key_of[13], 71), 0)
    w_qkv = normal_values(key_of[5], (LAYERS, P_SIZE, D, 3 * D), D ** -0.5, 0.1875, ((1, 2), (2, 16)))
    w_out = normal_values(key_of[6], (LAYERS, P_SIZE, D, D), (D // 2) ** -0.5, 0.25, ((1, 2), (2, 16)))
    w_gate = normal_values(key_of[7], (LAYERS, P_SIZE, D, FF), D ** -0.5, 0.1875, ((1, 2), (2, 16)))
    w_up = normal_values(key_of[8], (LAYERS, P_SIZE, D, FF), D ** -0.5, 0.1875, ((1, 2), (2, 16)))
    w_down = normal_values(key_of[9], (LAYERS, P_SIZE, FF, D), (FF // 4) ** -0.5, 0.1875, ((1, 2), (2, 16)))
    gain_attn = jnp.clip(1.0 + 0.18 * jax.random.normal(key_of[10], (LAYERS, P_SIZE, D), jnp.float32), 0.099609375, 1.8984375).astype(jnp.bfloat16)
    gain_ffn = jnp.clip(1.0 + 0.18 * jax.random.normal(key_of[11], (LAYERS, P_SIZE, D), jnp.float32), 0.099609375, 1.8984375).astype(jnp.bfloat16)
    cotangent = normal_values(key_of[12], (FRAMES, P_SIZE, D), 1.0, 6.0, ((0, 16), (1, 2)))
    return dict(frames_in=frames_in, code_table=code_table, code_ids=code_ids, delays=delays, item_lengths=item_lengths, w_qkv=w_qkv, w_out=w_out, w_gate=w_gate, w_up=w_up, w_down=w_down, gain_attn=gain_attn, gain_ffn=gain_ffn, cotangent=cotangent)


EPSILON = 1e-06

@jax.custom_vjp
def low(v):
    return lax.optimization_barrier(v.astype(jnp.bfloat16)).astype(jnp.float32)

@jax.custom_vjp
def low_back(v):
    return v

def low_keep(v):
    return (low(v), None)

def low_pass(kept, grad):
    return (grad,)

def back_keep(v):
    return (v, None)

def back_low(kept, grad):
    return (low(grad),)
low.defvjp(low_keep, low_pass)
low_back.defvjp(back_keep, back_low)

def inverse_rms(stream):
    return lax.rsqrt(lax.optimization_barrier(jnp.mean(stream * stream, axis=-1, keepdims=True)) + EPSILON)

def project(left, weight):
    return jnp.einsum('tpd,pde->tpe', left, weight, precision=lax.Precision.HIGHEST)

def delayed_codes(code_ids, delays, item_lengths):
    frame_count = code_ids.shape[0]
    item_ends = jnp.cumsum(item_lengths).astype(jnp.int32)
    starts = (item_ends - item_lengths).astype(jnp.int32)
    global_frame = jnp.arange(frame_count, dtype=jnp.int32)
    item_index = (lax.optimization_barrier(jnp.sum((starts[None, :] <= global_frame[:, None]).astype(jnp.int32), axis=1)) - 1).astype(jnp.int32)
    item_begin = starts[item_index]
    delay_rows = delays[item_index].astype(jnp.int32)
    source = (global_frame[:, None] - delay_rows).astype(jnp.int32)
    is_valid = source >= item_begin[:, None]
    source_rows = jnp.maximum(source, 0).astype(jnp.int32)
    code_rows = jnp.take_along_axis(code_ids, source_rows, axis=0)
    return (code_rows, is_valid)

def one_layer(stream, qkv_all, out_all, gate_all, up_all, down_all, attn_gain, ffn_gain):
    frame_count, positions, model_width = stream.shape
    normed_attn = low(stream * inverse_rms(stream) * attn_gain[None])
    qkv_rows = low_back(low(project(normed_attn, qkv_all)))
    queries = qkv_rows[..., :model_width].reshape(frame_count, positions, HEADS, HD)
    key_rows = qkv_rows[..., model_width:2 * model_width].reshape(frame_count, positions, HEADS, HD)
    value_rows = qkv_rows[..., 2 * model_width:].reshape(frame_count, positions, HEADS, HD)
    scores = jnp.einsum('tihe,tjhe->thij', queries, key_rows, precision=lax.Precision.HIGHEST) / math.sqrt(HD)
    causal = jnp.arange(positions)[:, None] >= jnp.arange(positions)[None, :]
    scores = jnp.where(causal, scores, -1e+30)
    scores = scores - lax.optimization_barrier(jnp.max(scores, axis=-1, keepdims=True))
    expon = jnp.exp(scores)
    attention_probs = expon / lax.optimization_barrier(jnp.sum(expon, axis=-1, keepdims=True))
    attended = jnp.einsum('thij,tjhe->tihe', attention_probs, value_rows, precision=lax.Precision.HIGHEST)
    attended = low_back(low(attended.reshape(frame_count, positions, model_width)))
    middle = stream + low_back(project(attended, out_all))
    normed_ffn = low(middle * inverse_rms(middle) * ffn_gain[None])
    gate_pre = low_back(project(normed_ffn, gate_all))
    up_pre = low_back(project(normed_ffn, up_all))
    gated_rows = low(jax.nn.silu(gate_pre) * up_pre)
    return middle + low_back(project(gated_rows, down_all))

def reference(frames_in, code_table, code_ids, delays, item_lengths, w_qkv, w_out, w_gate, w_up, w_down, gain_attn, gain_ffn, cotangent):
    code_rows, is_valid = delayed_codes(code_ids, delays, item_lengths)
    valid_scale = is_valid.astype(jnp.float32)[..., None]

    def forward(stream_in, table_all, qkv_all, out_all, gate_all, up_all, down_all, attn_all, ffn_all):
        embedded = jax.vmap(lambda one_table, one_code: one_table[one_code], in_axes=(0, 1), out_axes=1)(table_all, code_rows)
        stream = stream_in + low_back(embedded * valid_scale)
        for layer_index in range(LAYERS):
            stream = one_layer(stream, qkv_all[layer_index], out_all[layer_index], gate_all[layer_index], up_all[layer_index], down_all[layer_index], attn_all[layer_index], ffn_all[layer_index])
        return stream
    floats = (frames_in, code_table, w_qkv, w_out, w_gate, w_up, w_down, gain_attn, gain_ffn)
    floats = tuple((item.astype(jnp.float32) for item in floats))
    output, pull_back = jax.vjp(forward, *floats)
    grads = pull_back(cotangent.astype(jnp.float32))
    return (output.astype(jnp.bfloat16), grads[0], grads[1], grads[2], grads[3], grads[4], grads[5], grads[6], grads[7], grads[8])
```

```python
import math

import jax
import jax.numpy as jnp
from jax import lax
from jax.sharding import PartitionSpec as P

HEADS = 16
HD = 64
LAYERS = 2
EPSILON = 1e-06
HIGHEST = lax.Precision.HIGHEST
BF = jnp.bfloat16
F32 = jnp.float32


def plain(left, right):
    return jnp.dot(left, right, preferred_element_type=F32)


def left_trans(left, right):
    return lax.dot_general(left, right, (((0,), (0,)), ((), ())), preferred_element_type=F32)


def right_trans(left, right):
    return lax.dot_general(left, right, (((1,), (1,)), ((), ())), preferred_element_type=F32)


def inverse_rms(stream):
    return lax.rsqrt(jnp.mean(stream * stream, axis=-1, keepdims=True) + EPSILON)


def norm_back(gradient, stream, inverse, gain_row):
    scaled = gradient * gain_row
    gain_grad = jnp.sum(gradient * stream * inverse, axis=0)
    inner_sum = jnp.mean(scaled * stream, axis=-1, keepdims=True)
    return (inverse * scaled - stream * inverse * inverse * inverse * inner_sum, gain_grad)


def head_matrix():
    rows = lax.broadcasted_iota(jnp.int32, (HEADS * HD, HEADS), 0) // HD
    cols = lax.broadcasted_iota(jnp.int32, (HEADS * HD, HEADS), 1)
    return (rows == cols).astype(F32)


def head_sum(values):
    return jnp.dot(values, head_matrix(), precision=HIGHEST)


def head_spread(values):
    return jnp.dot(values, head_matrix().T, precision=HIGHEST)


class Plan:
    def __init__(self, count):
        self.count = count
        self.team = 8 if count % 8 == 0 else count
        self.teams = count // self.team
        self.inside = [[g * self.team + t for t in range(self.team)] for g in range(self.teams)]
        self.across = [[g * self.team + t for g in range(self.teams)] for t in range(self.team)]

    def gather_inside(self, rows):
        return lax.all_gather(rows, "frames", axis=0, tiled=True, axis_index_groups=self.inside)

    def scatter_inside(self, rows):
        return lax.psum_scatter(
            rows, "frames", scatter_dimension=0, tiled=True, axis_index_groups=self.inside
        )

    def gather_across(self, rows):
        return lax.all_gather(rows, "frames", axis=0, tiled=True, axis_index_groups=self.across)

    def scatter_across(self, rows):
        return lax.psum_scatter(
            rows, "frames", scatter_dimension=0, tiled=True, axis_index_groups=self.across
        )

    def swap_inside(self, parts):
        return lax.all_to_all(
            parts, "frames", split_axis=0, concat_axis=0, tiled=True, axis_index_groups=self.inside
        )

    def ffn_weights(self, gate, up, down):
        rows = gate.shape[0]
        both = jnp.stack([gate, up], axis=1).reshape(rows, 2, self.teams, self.team, -1)
        parts = both.transpose(3, 0, 1, 2, 4).reshape(self.team * rows, -1)
        mine = self.swap_inside(parts)
        return self.gather_across(mine), self.gather_across(down)

    def ffn_grads(self, both_part, down_part):
        down = self.scatter_across(down_part.astype(BF)).astype(F32)
        both = self.scatter_across(both_part.astype(BF))
        parts = self.swap_inside(both)
        rows = parts.shape[0] // self.team
        parts = parts.astype(F32).reshape(self.team, rows, 2, self.teams, -1)
        both = parts.transpose(1, 2, 3, 0, 4).reshape(rows, 2, -1)
        return both[:, 0], both[:, 1], down


def attend(qkv, other):
    width = HEADS * HD
    position = lax.axis_index("pos")
    q, k, v = (qkv[:, i * width : (i + 1) * width].astype(F32) for i in range(3))
    k0, v0 = (other[:, i * width : (i + 1) * width].astype(F32) for i in range(2))
    own = head_sum(q * k) / math.sqrt(HD)
    past = jnp.where(position > 0, head_sum(q * k0) / math.sqrt(HD), -1e30)
    largest = jnp.maximum(own, past)
    own, past = jnp.exp(own - largest), jnp.exp(past - largest)
    total = own + past
    own, past = own / total, past / total
    attended = head_spread(own) * v + head_spread(past) * v0
    return attended.astype(BF), own, past


def attend_back(grad, qkv, other, own, past):
    width = HEADS * HD
    q, k, v = (qkv[:, i * width : (i + 1) * width].astype(F32) for i in range(3))
    k0, v0 = (other[:, i * width : (i + 1) * width].astype(F32) for i in range(2))
    grad = grad.astype(F32)
    d_own, d_past = head_sum(grad * v), head_sum(grad * v0)
    inner = own * d_own + past * d_past
    s_own = head_spread(own * (d_own - inner) / math.sqrt(HD))
    s_past = head_spread(past * (d_past - inner) / math.sqrt(HD))
    own, past = head_spread(own), head_spread(past)
    d_q = s_own * k + s_past * k0
    d_k = s_own * q
    d_v = own * grad
    d_other = jnp.concatenate([s_past * q, past * grad], axis=1)
    return d_q, d_k, d_v, d_other


def body(
    frames_in,
    code_table,
    code_ids,
    delays,
    item_lengths,
    w_qkv,
    w_out,
    w_gate,
    w_up,
    w_down,
    gain_attn,
    gain_ffn,
    cotangent,
):
    count = lax.axis_size("frames")
    plan = Plan(count)
    positions = lax.axis_size("pos")
    onward = [(i, i + 1) for i in range(positions - 1)]
    backward = [(i + 1, i) for i in range(positions - 1)]
    local_frames = frames_in.shape[0]
    item_count = item_lengths.shape[0]
    width = frames_in.shape[-1]

    neighbours = [(i, i + 1) for i in range(count - 1)]
    earlier = lax.ppermute(code_ids[local_frames - 2 :], "frames", neighbours)
    extended = jnp.concatenate([earlier, code_ids], axis=0)[:, 0]
    global_frame = lax.axis_index("frames") * local_frames + jnp.arange(
        local_frames, dtype=jnp.int32
    )
    item_ends = jnp.cumsum(item_lengths)
    starts = item_ends - item_lengths
    item_index = jnp.sum((starts[None, :] <= global_frame[:, None]).astype(jnp.int32), axis=1) - 1
    chosen = item_index[:, None] == jnp.arange(item_count, dtype=jnp.int32)[None, :]
    item_begin = jnp.sum(jnp.where(chosen, starts[None, :], 0), axis=1)
    delay_rows = jnp.sum(jnp.where(chosen, delays[:, 0][None, :], 0), axis=1)
    one_back = extended[1 : local_frames + 1]
    two_back = extended[:local_frames]
    code_rows = jnp.where(delay_rows == 1, one_back, two_back)
    is_valid = global_frame - delay_rows >= item_begin
    vocab_size = code_table.shape[1] * count
    matches = code_rows[:, None] == jnp.arange(vocab_size, dtype=jnp.int32)[None, :]
    onehot = (matches & is_valid[:, None]).astype(BF)

    gains = jnp.stack([gain_attn[0, 0], gain_attn[1, 0], gain_ffn[0, 0], gain_ffn[1, 0]], axis=1)
    gains = jnp.pad(gains, ((0, 0), (0, 124)))
    full_table = lax.all_gather(code_table[0], "frames", axis=0, tiled=True)
    first_qkv = lax.all_gather(
        jnp.concatenate([w_qkv[0, 0], gains], axis=1), "frames", axis=0, tiled=True
    )
    gain_rows = first_qkv[:, 3 * width : 3 * width + 4].astype(F32).T
    qkv_all = [first_qkv[:, : 3 * width], None]
    out_all = [lax.all_gather(w_out[0, 0], "frames", axis=0, tiled=True), None]
    ffn_all = [plan.ffn_weights(w_gate[0, 0], w_up[0, 0], w_down[0, 0]), None]
    qkv_all[1] = lax.all_gather(w_qkv[1, 0], "frames", axis=0, tiled=True)
    out_all[1] = lax.all_gather(w_out[1, 0], "frames", axis=0, tiled=True)
    ffn_all[1] = plan.ffn_weights(w_gate[1, 0], w_up[1, 0], w_down[1, 0])

    stream = frames_in[:, 0].astype(F32) + plain(onehot, full_table)
    kept = []
    for layer in range(LAYERS):
        inv_attn = inverse_rms(stream)
        normed_attn = (stream * inv_attn * gain_rows[layer]).astype(BF)
        qkv = plain(normed_attn, qkv_all[layer]).astype(BF)
        other = lax.ppermute(qkv[:, width:], "pos", onward)
        attended, own, past = attend(qkv, other)
        middle = stream + plain(attended, out_all[layer])
        inv_ffn = inverse_rms(middle)
        normed_ffn = (middle * inv_ffn * gain_rows[2 + layer]).astype(BF)
        team_normed = plan.gather_inside(normed_ffn)
        both_all, down_all = ffn_all[layer]
        pre = plain(team_normed, both_all)
        half = pre.shape[1] // 2
        gate_pre, up_pre = pre[:, :half], pre[:, half:]
        gated = (jax.nn.silu(gate_pre) * up_pre).astype(BF)
        result = plain(gated, down_all).astype(BF)
        new_stream = middle + plan.scatter_inside(result).astype(F32)
        kept.append(
            (
                stream,
                inv_attn,
                normed_attn,
                qkv,
                other,
                own,
                past,
                attended,
                middle,
                inv_ffn,
                team_normed,
                gate_pre,
                up_pre,
                gated,
            )
        )
        stream = new_stream
    output = stream.astype(BF)[:, None, :]

    gradient = cotangent[:, 0].astype(F32)
    collected = [None] * LAYERS
    gain_parts = [None] * (2 * LAYERS)
    for layer in reversed(range(LAYERS)):
        (
            stream,
            inv_attn,
            normed_attn,
            qkv,
            other,
            own,
            past,
            attended,
            middle,
            inv_ffn,
            team_normed,
            gate_pre,
            up_pre,
            gated,
        ) = kept[layer]
        both_all, down_all = ffn_all[layer]
        grad_out = plan.gather_inside(gradient.astype(BF))
        grad_gated = right_trans(grad_out, down_all)
        sig = jax.nn.sigmoid(gate_pre)
        grad_gate = (grad_gated * up_pre * sig * (1.0 + gate_pre * (1.0 - sig))).astype(BF)
        grad_up = (grad_gated * gate_pre * sig).astype(BF)
        grad_both = jnp.concatenate([grad_gate, grad_up], axis=1)
        grad_normed = plan.scatter_inside(right_trans(grad_both, both_all).astype(BF)).astype(F32)
        down_part = left_trans(gated, grad_out)
        both_part = left_trans(team_normed, grad_both)
        ffn_shares = plan.ffn_grads(both_part, down_part)
        grad_middle, gain_parts[2 + layer] = norm_back(
            grad_normed, middle, inv_ffn, gain_rows[2 + layer]
        )
        grad_middle = gradient + grad_middle
        grad_attn = grad_middle.astype(BF)
        grad_attended = right_trans(grad_attn, out_all[layer]).astype(BF)
        d_q, d_k, d_v, d_other = attend_back(grad_attended, qkv, other, own, past)
        arrived = lax.ppermute(d_other.astype(BF), "pos", backward).astype(F32)
        grad_qkv = jnp.concatenate([d_q, d_k + arrived[:, :width], d_v + arrived[:, width:]], axis=1)
        grad_qkv = grad_qkv.astype(BF)
        out_part = left_trans(attended, grad_attn).astype(BF)
        out_share = lax.psum_scatter(out_part, "frames", scatter_dimension=0, tiled=True)
        grad_normed_attn = right_trans(grad_qkv, qkv_all[layer])
        grad_stream, gain_parts[layer] = norm_back(
            grad_normed_attn, stream, inv_attn, gain_rows[layer]
        )
        gradient = grad_middle + grad_stream
        qkv_part = left_trans(normed_attn, grad_qkv).astype(BF)
        if layer == 0:
            tail = jnp.stack(gain_parts, axis=1).astype(BF)
            qkv_part = jnp.concatenate([qkv_part, jnp.pad(tail, ((0, 0), (0, 124)))], axis=1)
        qkv_share = lax.psum_scatter(qkv_part, "frames", scatter_dimension=0, tiled=True)
        collected[layer] = (qkv_share.astype(F32), out_share.astype(F32)) + ffn_shares
    table_part = left_trans(onehot, gradient.astype(BF)).astype(BF)
    table_share = lax.psum_scatter(table_part, "frames", scatter_dimension=0, tiled=True)
    gain_shares = collected[0][0][:, 3 * width : 3 * width + 4].T
    collected[0] = (collected[0][0][:, : 3 * width],) + collected[0][1:]
    stacked = [
        jnp.stack([collected[layer][slot] for layer in range(LAYERS)], axis=0)[:, None]
        for slot in range(5)
    ]
    return (
        output,
        gradient[:, None, :],
        table_share.astype(F32)[None],
        stacked[0],
        stacked[1],
        stacked[2],
        stacked[3],
        stacked[4],
        gain_shares[:2][:, None],
        gain_shares[2:][:, None],
    )


def solution(mesh):
    return jax.shard_map(
        body,
        mesh=mesh,
        in_specs=(
            P("frames", "pos", None),
            P("pos", "frames", None),
            P("frames", "pos"),
            P(None, "pos"),
            P(),
            P(None, "pos", "frames", None),
            P(None, "pos", "frames", None),
            P(None, "pos", "frames", None),
            P(None, "pos", "frames", None),
            P(None, "pos", "frames", None),
            P(None, "pos", "frames"),
            P(None, "pos", "frames"),
            P("frames", "pos", None),
        ),
        out_specs=(
            P("frames", "pos", None),
            P("frames", "pos", None),
            P("pos", "frames", None),
            P(None, "pos", "frames", None),
            P(None, "pos", "frames", None),
            P(None, "pos", "frames", None),
            P(None, "pos", "frames", None),
            P(None, "pos", "frames", None),
            P(None, "pos", "frames"),
            P(None, "pos", "frames"),
        ),
        check_vma=False,
    )
```

```python
import math

import jax
import jax.numpy as jnp
from jax import lax
from jax.experimental import pallas as pl
from jax.experimental.pallas import tpu as pltpu
from jax.sharding import PartitionSpec as P

HEADS = 16
HD = 64
LAYERS = 2
EPSILON = 1e-06
HIGHEST = lax.Precision.HIGHEST
BF = jnp.bfloat16
F32 = jnp.float32


def plain(left, right):
    return jnp.dot(left, right, preferred_element_type=F32)


def left_trans(left, right):
    return lax.dot_general(left, right, (((0,), (0,)), ((), ())), preferred_element_type=F32)


def right_trans(left, right):
    return lax.dot_general(left, right, (((1,), (1,)), ((), ())), preferred_element_type=F32)


def inverse_rms(stream):
    return lax.rsqrt(jnp.mean(stream * stream, axis=-1, keepdims=True) + EPSILON)


def norm_back(gradient, stream, inverse, gain_row):
    scaled = gradient * gain_row
    gain_grad = jnp.sum(gradient * stream * inverse, axis=0)
    inner_sum = jnp.mean(scaled * stream, axis=-1, keepdims=True)
    return (inverse * scaled - stream * inverse * inverse * inverse * inner_sum, gain_grad)


def head_matrix():
    rows = lax.broadcasted_iota(jnp.int32, (HEADS * HD, HEADS), 0) // HD
    cols = lax.broadcasted_iota(jnp.int32, (HEADS * HD, HEADS), 1)
    return (rows == cols).astype(F32)


def head_sum(values):
    return jnp.dot(values, head_matrix(), precision=HIGHEST)


def head_spread(values):
    return jnp.dot(values, head_matrix().T, precision=HIGHEST)


MESH = pl.DeviceIdType.MESH
VMEM_LIMIT = 60 * 2**20


def in_vmem(count):
    return [pl.BlockSpec(memory_space=pltpu.VMEM)] * count


class Team:
    SCRATCH_COPIES = 19

    def __init__(self, rows, mine, everyone, sums, scratch):
        (self.part, self.from_core, self.from_across, self.from_x, self.from_z) = scratch[:5]
        (self.to_x, self.to_z, self.to_across, self.sent, self.got) = scratch[5:10]
        self.rows, self.half = rows, rows // 2
        self.mine, self.everyone, self.sums = mine, everyone, sums
        index = lax.axis_index("frames")
        self.place = lax.axis_index("pos")
        member = lax.rem(index, 8)
        self.core = lax.rem(member, 2)
        self.x = lax.rem(member // 2, 2)
        self.z = member // 4
        self.core_peer = index + 1 - 2 * self.core
        self.x_peer = index + 2 - 4 * self.x
        self.z_peer = index + 4 - 8 * self.z

    @staticmethod
    def scratch(rows, width):
        half = rows // 2
        return [
            pltpu.VMEM((4, rows, width), BF),
            pltpu.VMEM((4, rows, width), BF),
            pltpu.VMEM((2, half, width), BF),
            pltpu.VMEM((rows, width), BF),
            pltpu.VMEM((rows, width), BF),
            pltpu.VMEM((rows, width), BF),
            pltpu.VMEM((rows, width), BF),
            pltpu.VMEM((rows, width), BF),
            pltpu.SemaphoreType.DMA((Team.SCRATCH_COPIES,)),
            pltpu.SemaphoreType.DMA((Team.SCRATCH_COPIES,)),
        ]

    def greet(self):
        barrier = pltpu.get_barrier_semaphore()
        for peer in (self.core_peer, self.x_peer, self.z_peer):
            pl.semaphore_signal(barrier, inc=1, device_id=(peer, self.place), device_id_type=MESH)
        pl.semaphore_wait(barrier, 3)

    def copy(self, number, source, target, peer):
        return pltpu.make_async_remote_copy(
            src_ref=source,
            dst_ref=target,
            send_sem=self.sent.at[number],
            recv_sem=self.got.at[number],
            device_id=(peer, self.place),
            device_id_type=MESH,
        )

    def pair_start(self, m):
        x = self.x + (m % 2) * (1 - 2 * self.x)
        z = self.z + (m // 2) * (1 - 2 * self.z)
        return pl.multiple_of((z * 2 + x) * (2 * self.rows), 2 * self.rows)

    def shard(self, m, part=None, core=None):
        core = self.core if core is None else core
        start = self.pair_start(m) + core * self.rows
        size = self.rows
        if part is not None:
            start, size = start + part * self.half, self.half
        return self.everyone.at[pl.ds(pl.multiple_of(start, 16), size)]

    def gather_copies(self):
        own = self.shard(0)
        x_rows, z_rows = self.shard(1), self.shard(2)
        x_low, z_high = self.shard(1, 1), self.shard(2, 0)
        high, low = self.shard(3, 0), self.shard(3, 1)
        return [
            self.copy(0, self.mine, own, self.core_peer),
            self.copy(1, self.mine, own, self.x_peer),
            self.copy(2, self.mine, own, self.z_peer),
            self.copy(3, x_rows, x_rows, self.core_peer),
            self.copy(4, x_low, x_low, self.z_peer),
            self.copy(5, z_rows, z_rows, self.core_peer),
            self.copy(6, z_high, z_high, self.x_peer),
            self.copy(7, high, high, self.core_peer),
            self.copy(8, low, low, self.core_peer),
        ]

    def arrived(self, number):
        other = 1 - self.core
        target = [
            self.shard(0, core=other),
            self.shard(1),
            self.shard(2),
            self.shard(1, core=other),
            self.shard(3, 1),
            self.shard(2, core=other),
            self.shard(3, 0),
            self.shard(3, 0, core=other),
            self.shard(3, 1, core=other),
        ][number]
        self.copy(number, target, target, self.core_peer).wait_recv()

    def sum_copies(self):
        half = self.half
        high, low = pl.ds(0, half), pl.ds(half, half)
        copies = [
            self.copy(9 + m, self.part.at[m], self.from_core.at[m], self.core_peer)
            for m in range(4)
        ]
        copies += [
            self.copy(13, self.to_across.at[high], self.from_across.at[0], self.x_peer),
            self.copy(14, self.to_across.at[low], self.from_across.at[1], self.z_peer),
            self.copy(15, self.to_x.at[high], self.from_x.at[high], self.x_peer),
            self.copy(16, self.to_x.at[low], self.from_x.at[low], self.x_peer),
            self.copy(17, self.to_z.at[low], self.from_z.at[low], self.z_peer),
            self.copy(18, self.to_z.at[high], self.from_z.at[high], self.z_peer),
        ]
        return copies

    def run(self, compute, between, result):
        half, rows = self.half, self.rows
        self.greet()
        gather = self.gather_copies()
        adds = self.sum_copies()
        for copy in gather[:3]:
            copy.start()
        start = self.pair_start(0) + self.core * rows
        self.everyone[pl.ds(pl.multiple_of(start, 16), rows), :] = self.mine[...]

        def total(m, first):
            return self.sums[m, first : first + half, :] + self.from_core[
                m, first : first + half, :
            ].astype(F32)

        def step(m, carry):
            @pl.when(m == 0)
            def _():
                self.arrived(0)

            @pl.when(m == 1)
            def _():
                self.arrived(1)
                gather[4].start()
                gather[3].start()
                self.arrived(2)
                gather[6].start()
                gather[5].start()
                self.arrived(3)

            @pl.when(m == 2)
            def _():
                self.arrived(5)

            @pl.when(m == 3)
            def _():
                self.arrived(6)
                gather[7].start()
                self.arrived(4)
                gather[8].start()
                self.arrived(7)
                self.arrived(8)

            compute(m, self.pair_start(m))
            self.copy(9 + m, self.part.at[m], self.from_core.at[m], self.core_peer).start()

            @pl.when(m == 2)
            def _():
                adds[1].wait_recv()
                self.to_x[:half, :] = total(1, 0).astype(BF)
                adds[6].start()

            return carry

        lax.fori_loop(0, 4, step, 0)
        adds[3].wait_recv()
        self.to_across[:half, :] = total(3, 0).astype(BF)
        adds[4].start()
        self.to_across[half:, :] = total(3, half).astype(BF)
        adds[5].start()
        adds[2].wait_recv()
        self.to_z[half:, :] = total(2, half).astype(BF)
        adds[8].start()
        between()
        adds[5].wait_recv()
        self.to_x[half:, :] = (total(1, half) + self.from_across[1].astype(F32)).astype(BF)
        adds[7].start()
        adds[4].wait_recv()
        self.to_z[:half, :] = (total(2, 0) + self.from_across[0].astype(F32)).astype(BF)
        adds[9].start()
        adds[0].wait_recv()
        for number in (6, 7, 8, 9):
            adds[number].wait_recv()
        for first in (0, half):
            rows_here = slice(first, first + half)
            result[rows_here, :] = (
                total(0, first)
                + self.from_x[rows_here, :].astype(F32)
                + self.from_z[rows_here, :].astype(F32)
            )
        for copy in gather + adds:
            copy.wait_send()


def split_pair(team, m, value, sums, part):
    rows = team.rows

    @pl.when(team.core == 0)
    def _():
        sums[m] = value[:rows]
        part[m] = value[rows:].astype(BF)

    @pl.when(team.core == 1)
    def _():
        sums[m] = value[rows:]
        part[m] = value[:rows].astype(BF)


def ffn_forward_kernel(normed, both, down, everyone, pre, gated, result, sums, *scratch):
    rows = normed.shape[0]
    hidden = down.shape[0]
    tile = min(hidden, 256)
    team = Team(rows, normed, everyone, sums, scratch)

    def compute(m, start):
        here = pl.ds(start, 2 * rows)
        block = everyone[here, :]
        for first in range(0, hidden, tile):
            g = plain(block, both[:, first : first + tile])
            u = plain(block, both[:, hidden + first : hidden + first + tile])
            pre[here, first : first + tile] = g
            pre[here, hidden + first : hidden + first + tile] = u
            gated[here, first : first + tile] = (g * jax.nn.sigmoid(g) * u).astype(BF)
        split_pair(team, m, plain(gated[here, :], down[...]), sums, team.part)

    team.run(compute, lambda: None, result)


def ffn_backward_kernel(
    grad, both, down, pre, gated, normed, result, both_part, down_part, everyone, d_both, sums, *scratch
):
    rows = grad.shape[0]
    hidden = down.shape[0]
    tile = min(hidden, 256)
    team = Team(rows, grad, everyone, sums, scratch)

    def compute(m, start):
        here = pl.ds(start, 2 * rows)
        block = everyone[here, :]
        for first in range(0, hidden, tile):
            d_gated = right_trans(block, down[first : first + tile, :])
            g = pre[here, first : first + tile]
            u = pre[here, hidden + first : hidden + first + tile]
            sig = jax.nn.sigmoid(g)
            d_both[here, first : first + tile] = (
                d_gated * u * sig * (1.0 + g * (1.0 - sig))
            ).astype(BF)
            d_both[here, hidden + first : hidden + first + tile] = (d_gated * g * sig).astype(BF)
        split_pair(team, m, right_trans(d_both[here, :], both[...]), sums, team.part)

    def between():
        def down_step(i, carry):
            cols = pl.ds(pl.multiple_of(i * 256, 256), 256)
            down_part[:, cols] = left_trans(gated[...], everyone[:, cols])
            return carry

        def both_step(i, carry):
            cols = pl.ds(pl.multiple_of(i * 256, 256), 256)
            both_part[:, cols] = left_trans(normed[...], d_both[:, cols]).astype(BF)
            return carry

        lax.fori_loop(0, down_part.shape[1] // 256, down_step, 0)
        lax.fori_loop(0, both_part.shape[1] // 256, both_step, 0)

    team.run(compute, between, result)


def ffn_forward(normed, both, down):
    rows, width = normed.shape
    hidden = down.shape[0]
    return pl.pallas_call(
        ffn_forward_kernel,
        out_shape=(
            jax.ShapeDtypeStruct((8 * rows, width), BF),
            jax.ShapeDtypeStruct((8 * rows, 2 * hidden), F32),
            jax.ShapeDtypeStruct((8 * rows, hidden), BF),
            jax.ShapeDtypeStruct((rows, width), F32),
        ),
        in_specs=in_vmem(3),
        out_specs=in_vmem(4),
        scratch_shapes=[pltpu.VMEM((4, rows, width), F32)] + Team.scratch(rows, width),
        compiler_params=pltpu.CompilerParams(
            collective_id=1, has_side_effects=True, vmem_limit_bytes=VMEM_LIMIT
        ),
        name="ffn_forward",
    )(normed, both, down)


def ffn_backward(grad, both, down, pre, gated, normed):
    rows, width = grad.shape
    hidden = down.shape[0]
    return pl.pallas_call(
        ffn_backward_kernel,
        out_shape=(
            jax.ShapeDtypeStruct((rows, width), F32),
            jax.ShapeDtypeStruct((width, 2 * hidden), BF),
            jax.ShapeDtypeStruct((hidden, width), F32),
        ),
        in_specs=in_vmem(6),
        out_specs=in_vmem(3),
        scratch_shapes=[
            pltpu.VMEM((8 * rows, width), BF),
            pltpu.VMEM((8 * rows, 2 * hidden), BF),
            pltpu.VMEM((4, rows, width), F32),
        ]
        + Team.scratch(rows, width),
        compiler_params=pltpu.CompilerParams(
            collective_id=2, has_side_effects=True, vmem_limit_bytes=VMEM_LIMIT
        ),
        name="ffn_backward",
    )(grad, both, down, pre, gated, normed)


class Plan:
    def __init__(self, count):
        self.count = count
        self.team = 8
        self.teams = count // self.team
        self.across = [[g * self.team + t for g in range(self.teams)] for t in range(self.team)]

    def ffn_weights(self, gate, up, down):
        rows = gate.shape[0]
        both = jnp.stack([gate, up], axis=1).reshape(rows, 2, self.teams, self.team, -1)
        parts = both.transpose(3, 0, 1, 2, 4).reshape(self.team, rows, -1)
        parts = jnp.broadcast_to(parts[None], (self.teams,) + parts.shape)
        parts = parts.reshape((self.count,) + parts.shape[2:])
        mine = lax.all_to_all(parts, "frames", split_axis=0, concat_axis=0, tiled=True)
        return mine.reshape(self.count * rows, -1), self.gather_across(down)

    def gather_across(self, rows):
        if self.teams != 2:
            return lax.all_gather(rows, "frames", axis=0, tiled=True, axis_index_groups=self.across)
        theirs = lax.ppermute(rows, "frames", self.partners())
        first = lax.axis_index("frames") < self.team
        return jnp.concatenate([jnp.where(first, rows, theirs), jnp.where(first, theirs, rows)])

    def scatter_across(self, rows):
        if self.teams != 2:
            part = lax.psum_scatter(
                rows.astype(BF),
                "frames",
                scatter_dimension=0,
                tiled=True,
                axis_index_groups=self.across,
            )
            return part.astype(F32)
        half = rows.shape[0] // 2
        first = lax.axis_index("frames") < self.team
        mine = jnp.where(first, rows[:half], rows[half:])
        sent = jnp.where(first, rows[half:], rows[:half]).astype(BF)
        return mine + lax.ppermute(sent, "frames", self.partners()).astype(F32)

    def partners(self):
        return [(i, (i + self.team) % self.count) for i in range(self.count)]

    def ffn_grads(self, both_part, down_part):
        down = self.scatter_across(down_part)
        parts = both_part.astype(BF).reshape(self.count, -1, both_part.shape[1])
        parts = lax.all_to_all(parts, "frames", split_axis=0, concat_axis=0, tiled=True)
        rows = parts.shape[1]
        parts = parts.astype(F32).reshape(self.teams, self.team, rows, 2, self.teams, -1).sum(axis=0)
        both = parts.transpose(1, 2, 3, 0, 4).reshape(rows, 2, -1)
        return both[:, 0], both[:, 1], down


def attend(qkv, other):
    width = HEADS * HD
    position = lax.axis_index("pos")
    q, k, v = (qkv[:, i * width : (i + 1) * width].astype(F32) for i in range(3))
    k0, v0 = (other[:, i * width : (i + 1) * width].astype(F32) for i in range(2))
    own = head_sum(q * k) / math.sqrt(HD)
    past = jnp.where(position > 0, head_sum(q * k0) / math.sqrt(HD), -1e30)
    largest = jnp.maximum(own, past)
    own, past = jnp.exp(own - largest), jnp.exp(past - largest)
    total = own + past
    own, past = own / total, past / total
    attended = head_spread(own) * v + head_spread(past) * v0
    return attended.astype(BF), own, past


def attend_back(grad, qkv, other, own, past):
    width = HEADS * HD
    q, k, v = (qkv[:, i * width : (i + 1) * width].astype(F32) for i in range(3))
    k0, v0 = (other[:, i * width : (i + 1) * width].astype(F32) for i in range(2))
    grad = grad.astype(F32)
    d_own, d_past = head_sum(grad * v), head_sum(grad * v0)
    inner = own * d_own + past * d_past
    s_own = head_spread(own * (d_own - inner) / math.sqrt(HD))
    s_past = head_spread(past * (d_past - inner) / math.sqrt(HD))
    own, past = head_spread(own), head_spread(past)
    d_q = s_own * k + s_past * k0
    d_k = s_own * q
    d_v = own * grad
    d_other = jnp.concatenate([s_past * q, past * grad], axis=1)
    return d_q, d_k, d_v, d_other


def body(
    frames_in,
    code_table,
    code_ids,
    delays,
    item_lengths,
    w_qkv,
    w_out,
    w_gate,
    w_up,
    w_down,
    gain_attn,
    gain_ffn,
    cotangent,
):
    count = lax.axis_size("frames")
    plan = Plan(count)
    positions = lax.axis_size("pos")
    onward = [(i, i + 1) for i in range(positions - 1)]
    backward = [(i + 1, i) for i in range(positions - 1)]
    local_frames = frames_in.shape[0]
    item_count = item_lengths.shape[0]
    width = frames_in.shape[-1]

    neighbours = [(i, i + 1) for i in range(count - 1)]
    earlier = lax.ppermute(code_ids[local_frames - 2 :], "frames", neighbours)
    extended = jnp.concatenate([earlier, code_ids], axis=0)[:, 0]
    global_frame = lax.axis_index("frames") * local_frames + jnp.arange(
        local_frames, dtype=jnp.int32
    )
    item_ends = jnp.cumsum(item_lengths)
    starts = item_ends - item_lengths
    item_index = jnp.sum((starts[None, :] <= global_frame[:, None]).astype(jnp.int32), axis=1) - 1
    chosen = item_index[:, None] == jnp.arange(item_count, dtype=jnp.int32)[None, :]
    item_begin = jnp.sum(jnp.where(chosen, starts[None, :], 0), axis=1)
    delay_rows = jnp.sum(jnp.where(chosen, delays[:, 0][None, :], 0), axis=1)
    one_back = extended[1 : local_frames + 1]
    two_back = extended[:local_frames]
    code_rows = jnp.where(delay_rows == 1, one_back, two_back)
    is_valid = global_frame - delay_rows >= item_begin
    vocab_size = code_table.shape[1] * count
    matches = code_rows[:, None] == jnp.arange(vocab_size, dtype=jnp.int32)[None, :]
    onehot = (matches & is_valid[:, None]).astype(BF)

    gains = jnp.stack([gain_attn[0, 0], gain_attn[1, 0], gain_ffn[0, 0], gain_ffn[1, 0]], axis=1)
    gains = jnp.pad(gains, ((0, 0), (0, 124)))
    full_table = lax.all_gather(code_table[0], "frames", axis=0, tiled=True)
    first_qkv = lax.all_gather(
        jnp.concatenate([w_qkv[0, 0], gains], axis=1), "frames", axis=0, tiled=True
    )
    gain_rows = first_qkv[:, 3 * width : 3 * width + 4].astype(F32).T
    qkv_all = [first_qkv[:, : 3 * width], None]
    out_all = [lax.all_gather(w_out[0, 0], "frames", axis=0, tiled=True), None]
    ffn_all = [plan.ffn_weights(w_gate[0, 0], w_up[0, 0], w_down[0, 0]), None]
    qkv_all[1] = lax.all_gather(w_qkv[1, 0], "frames", axis=0, tiled=True)
    out_all[1] = lax.all_gather(w_out[1, 0], "frames", axis=0, tiled=True)
    ffn_all[1] = plan.ffn_weights(w_gate[1, 0], w_up[1, 0], w_down[1, 0])

    stream = frames_in[:, 0].astype(F32) + plain(onehot, full_table)
    kept = []
    for layer in range(LAYERS):
        inv_attn = inverse_rms(stream)
        normed_attn = (stream * inv_attn * gain_rows[layer]).astype(BF)
        qkv = plain(normed_attn, qkv_all[layer]).astype(BF)
        other = lax.ppermute(qkv[:, width:], "pos", onward)
        attended, own, past = attend(qkv, other)
        middle = stream + plain(attended, out_all[layer])
        inv_ffn = inverse_rms(middle)
        normed_ffn = (middle * inv_ffn * gain_rows[2 + layer]).astype(BF)
        both_all, down_all = ffn_all[layer]
        team_normed, pre, gated, summed = ffn_forward(normed_ffn, both_all, down_all)
        new_stream = middle + summed
        kept.append(
            (
                stream,
                inv_attn,
                normed_attn,
                qkv,
                other,
                own,
                past,
                attended,
                middle,
                inv_ffn,
                team_normed,
                pre,
                gated,
            )
        )
        stream = new_stream
    output = stream.astype(BF)[:, None, :]

    gradient = cotangent[:, 0].astype(F32)
    collected = [None] * LAYERS
    gain_parts = [None] * (2 * LAYERS)
    for layer in reversed(range(LAYERS)):
        (
            stream,
            inv_attn,
            normed_attn,
            qkv,
            other,
            own,
            past,
            attended,
            middle,
            inv_ffn,
            team_normed,
            pre,
            gated,
        ) = kept[layer]
        both_all, down_all = ffn_all[layer]
        grad_normed, both_part, down_part = ffn_backward(
            gradient.astype(BF), both_all, down_all, pre, gated, team_normed
        )
        ffn_shares = plan.ffn_grads(both_part, down_part)
        grad_middle, gain_parts[2 + layer] = norm_back(
            grad_normed, middle, inv_ffn, gain_rows[2 + layer]
        )
        grad_middle = gradient + grad_middle
        grad_attn = grad_middle.astype(BF)
        grad_attended = right_trans(grad_attn, out_all[layer]).astype(BF)
        d_q, d_k, d_v, d_other = attend_back(grad_attended, qkv, other, own, past)
        arrived = lax.ppermute(d_other.astype(BF), "pos", backward).astype(F32)
        grad_qkv = jnp.concatenate([d_q, d_k + arrived[:, :width], d_v + arrived[:, width:]], axis=1)
        grad_qkv = grad_qkv.astype(BF)
        out_part = left_trans(attended, grad_attn).astype(BF)
        out_share = lax.psum_scatter(out_part, "frames", scatter_dimension=0, tiled=True)
        grad_normed_attn = right_trans(grad_qkv, qkv_all[layer])
        grad_stream, gain_parts[layer] = norm_back(
            grad_normed_attn, stream, inv_attn, gain_rows[layer]
        )
        gradient = grad_middle + grad_stream
        qkv_part = left_trans(normed_attn, grad_qkv).astype(BF)
        if layer == 0:
            tail = jnp.stack(gain_parts, axis=1).astype(BF)
            qkv_part = jnp.concatenate([qkv_part, jnp.pad(tail, ((0, 0), (0, 124)))], axis=1)
        qkv_share = lax.psum_scatter(qkv_part, "frames", scatter_dimension=0, tiled=True)
        collected[layer] = (qkv_share.astype(F32), out_share.astype(F32)) + ffn_shares
    table_part = left_trans(onehot, gradient.astype(BF)).astype(BF)
    table_share = lax.psum_scatter(table_part, "frames", scatter_dimension=0, tiled=True)
    gain_shares = collected[0][0][:, 3 * width : 3 * width + 4].T
    collected[0] = (collected[0][0][:, : 3 * width],) + collected[0][1:]
    stacked = [
        jnp.stack([collected[layer][slot] for layer in range(LAYERS)], axis=0)[:, None]
        for slot in range(5)
    ]
    return (
        output,
        gradient[:, None, :],
        table_share.astype(F32)[None],
        stacked[0],
        stacked[1],
        stacked[2],
        stacked[3],
        stacked[4],
        gain_shares[:2][:, None],
        gain_shares[2:][:, None],
    )


def solution(mesh):
    return jax.shard_map(
        body,
        mesh=mesh,
        in_specs=(
            P("frames", "pos", None),
            P("pos", "frames", None),
            P("frames", "pos"),
            P(None, "pos"),
            P(),
            P(None, "pos", "frames", None),
            P(None, "pos", "frames", None),
            P(None, "pos", "frames", None),
            P(None, "pos", "frames", None),
            P(None, "pos", "frames", None),
            P(None, "pos", "frames"),
            P(None, "pos", "frames"),
            P("frames", "pos", None),
        ),
        out_specs=(
            P("frames", "pos", None),
            P("frames", "pos", None),
            P("pos", "frames", None),
            P(None, "pos", "frames", None),
            P(None, "pos", "frames", None),
            P(None, "pos", "frames", None),
            P(None, "pos", "frames", None),
            P(None, "pos", "frames", None),
            P(None, "pos", "frames"),
            P(None, "pos", "frames"),
        ),
        check_vma=False,
    )
```

```python
import math

import jax
import jax.numpy as jnp
from jax import lax
from jax.experimental import pallas as pl
from jax.experimental.pallas import tpu as pltpu
from jax.sharding import PartitionSpec as P

HEADS = 16
HD = 64
LAYERS = 2
EPSILON = 1e-06
HIGHEST = lax.Precision.HIGHEST
BF = jnp.bfloat16
F32 = jnp.float32


def plain(left, right):
    return jnp.dot(left, right, preferred_element_type=F32)


def left_trans(left, right):
    return lax.dot_general(left, right, (((0,), (0,)), ((), ())), preferred_element_type=F32)


def right_trans(left, right):
    return lax.dot_general(left, right, (((1,), (1,)), ((), ())), preferred_element_type=F32)


def inverse_rms(stream):
    return lax.rsqrt(jnp.mean(stream * stream, axis=-1, keepdims=True) + EPSILON)


def norm_back(gradient, stream, inverse, gain_row):
    scaled = gradient * gain_row
    gain_grad = jnp.sum(gradient * stream * inverse, axis=0)
    inner_sum = jnp.mean(scaled * stream, axis=-1, keepdims=True)
    return (inverse * scaled - stream * inverse * inverse * inverse * inner_sum, gain_grad)


def head_matrix():
    rows = lax.broadcasted_iota(jnp.int32, (HEADS * HD, HEADS), 0) // HD
    cols = lax.broadcasted_iota(jnp.int32, (HEADS * HD, HEADS), 1)
    return (rows == cols).astype(F32)


def head_sum(values):
    return jnp.dot(values, head_matrix(), precision=HIGHEST)


def head_spread(values):
    return jnp.dot(values, head_matrix().T, precision=HIGHEST)


MESH = pl.DeviceIdType.MESH
VMEM_LIMIT = 60 * 2**20


def in_vmem(count):
    return [pl.BlockSpec(memory_space=pltpu.VMEM)] * count


class Team:
    SCRATCH_COPIES = 19

    def __init__(self, rows, mine, everyone, sums, scratch):
        (self.part, self.from_core, self.from_across, self.from_x, self.from_z) = scratch[:5]
        (self.to_x, self.to_z, self.to_across, self.sent, self.got) = scratch[5:10]
        self.rows, self.half = rows, rows // 2
        self.mine, self.everyone, self.sums = mine, everyone, sums
        index = lax.axis_index("frames")
        self.place = lax.axis_index("pos")
        member = lax.rem(index, 8)
        self.core = lax.rem(member, 2)
        self.x = lax.rem(member // 2, 2)
        self.z = member // 4
        self.core_peer = index + 1 - 2 * self.core
        self.x_peer = index + 2 - 4 * self.x
        self.z_peer = index + 4 - 8 * self.z

    @staticmethod
    def scratch(rows, width):
        half = rows // 2
        return [
            pltpu.VMEM((4, rows, width), BF),
            pltpu.VMEM((4, rows, width), BF),
            pltpu.VMEM((2, half, width), BF),
            pltpu.VMEM((rows, width), BF),
            pltpu.VMEM((rows, width), BF),
            pltpu.VMEM((rows, width), BF),
            pltpu.VMEM((rows, width), BF),
            pltpu.VMEM((rows, width), BF),
            pltpu.SemaphoreType.DMA((Team.SCRATCH_COPIES,)),
            pltpu.SemaphoreType.DMA((Team.SCRATCH_COPIES,)),
        ]

    def greet(self):
        barrier = pltpu.get_barrier_semaphore()
        for peer in (self.core_peer, self.x_peer, self.z_peer):
            pl.semaphore_signal(barrier, inc=1, device_id=(peer, self.place), device_id_type=MESH)
        pl.semaphore_wait(barrier, 3)

    def copy(self, number, source, target, peer):
        return pltpu.make_async_remote_copy(
            src_ref=source,
            dst_ref=target,
            send_sem=self.sent.at[number],
            recv_sem=self.got.at[number],
            device_id=(peer, self.place),
            device_id_type=MESH,
        )

    def pair_start(self, m):
        x = self.x + (m % 2) * (1 - 2 * self.x)
        z = self.z + (m // 2) * (1 - 2 * self.z)
        return pl.multiple_of((z * 2 + x) * (2 * self.rows), 2 * self.rows)

    def shard(self, m, part=None, core=None):
        core = self.core if core is None else core
        start = self.pair_start(m) + core * self.rows
        size = self.rows
        if part is not None:
            start, size = start + part * self.half, self.half
        return self.everyone.at[pl.ds(pl.multiple_of(start, 16), size)]

    def gather_copies(self):
        own = self.shard(0)
        x_rows, z_rows = self.shard(1), self.shard(2)
        x_low, z_high = self.shard(1, 1), self.shard(2, 0)
        high, low = self.shard(3, 0), self.shard(3, 1)
        return [
            self.copy(0, self.mine, own, self.core_peer),
            self.copy(1, self.mine, own, self.x_peer),
            self.copy(2, self.mine, own, self.z_peer),
            self.copy(3, x_rows, x_rows, self.core_peer),
            self.copy(4, x_low, x_low, self.z_peer),
            self.copy(5, z_rows, z_rows, self.core_peer),
            self.copy(6, z_high, z_high, self.x_peer),
            self.copy(7, high, high, self.core_peer),
            self.copy(8, low, low, self.core_peer),
        ]

    def arrived(self, number):
        other = 1 - self.core
        target = [
            self.shard(0, core=other),
            self.shard(1),
            self.shard(2),
            self.shard(1, core=other),
            self.shard(3, 1),
            self.shard(2, core=other),
            self.shard(3, 0),
            self.shard(3, 0, core=other),
            self.shard(3, 1, core=other),
        ][number]
        self.copy(number, target, target, self.core_peer).wait_recv()

    def sum_copies(self):
        half = self.half
        high, low = pl.ds(0, half), pl.ds(half, half)
        copies = [
            self.copy(9 + m, self.part.at[m], self.from_core.at[m], self.core_peer)
            for m in range(4)
        ]
        copies += [
            self.copy(13, self.to_across.at[high], self.from_across.at[0], self.x_peer),
            self.copy(14, self.to_across.at[low], self.from_across.at[1], self.z_peer),
            self.copy(15, self.to_x.at[high], self.from_x.at[high], self.x_peer),
            self.copy(16, self.to_x.at[low], self.from_x.at[low], self.x_peer),
            self.copy(17, self.to_z.at[low], self.from_z.at[low], self.z_peer),
            self.copy(18, self.to_z.at[high], self.from_z.at[high], self.z_peer),
        ]
        return copies

    def run(self, compute, between, result, later=None):
        half, rows = self.half, self.rows
        self.greet()
        gather = self.gather_copies()
        adds = self.sum_copies()
        for copy in gather[:3]:
            copy.start()
        start = self.pair_start(0) + self.core * rows
        self.everyone[pl.ds(pl.multiple_of(start, 16), rows), :] = self.mine[...]

        def total(m, first):
            return self.sums[m, first : first + half, :] + self.from_core[
                m, first : first + half, :
            ].astype(F32)

        def step(m, carry):
            @pl.when(m == 0)
            def _():
                self.arrived(0)

            @pl.when(m == 1)
            def _():
                self.arrived(1)
                gather[4].start()
                gather[3].start()
                self.arrived(2)
                gather[6].start()
                gather[5].start()
                self.arrived(3)

            @pl.when(m == 2)
            def _():
                self.arrived(5)

            @pl.when(m == 3)
            def _():
                self.arrived(6)
                gather[7].start()
                self.arrived(4)
                gather[8].start()
                self.arrived(7)
                self.arrived(8)

            compute(m, self.pair_start(m))
            self.copy(9 + m, self.part.at[m], self.from_core.at[m], self.core_peer).start()
            if later is not None:
                later(m)

            @pl.when(m == 2)
            def _():
                adds[1].wait_recv()
                self.to_x[:half, :] = total(1, 0).astype(BF)
                adds[6].start()

            return carry

        lax.fori_loop(0, 4, step, 0)
        adds[3].wait_recv()
        self.to_across[:half, :] = total(3, 0).astype(BF)
        adds[4].start()
        self.to_across[half:, :] = total(3, half).astype(BF)
        adds[5].start()
        adds[2].wait_recv()
        self.to_z[half:, :] = total(2, half).astype(BF)
        adds[8].start()
        between()
        adds[5].wait_recv()
        self.to_x[half:, :] = (total(1, half) + self.from_across[1].astype(F32)).astype(BF)
        adds[7].start()
        adds[4].wait_recv()
        self.to_z[:half, :] = (total(2, 0) + self.from_across[0].astype(F32)).astype(BF)
        adds[9].start()
        adds[0].wait_recv()
        for number in (6, 7, 8, 9):
            adds[number].wait_recv()
        for first in (0, half):
            rows_here = slice(first, first + half)
            result[rows_here, :] = (
                total(0, first)
                + self.from_x[rows_here, :].astype(F32)
                + self.from_z[rows_here, :].astype(F32)
            )
        for copy in gather + adds:
            copy.wait_send()


def split_pair(team, m, value, sums, part):
    rows = team.rows

    @pl.when(team.core == 0)
    def _():
        sums[m] = value[:rows]
        part[m] = value[rows:].astype(BF)

    @pl.when(team.core == 1)
    def _():
        sums[m] = value[rows:]
        part[m] = value[:rows].astype(BF)


def hidden_units(block, both, hidden, first):
    gate = plain(block, both[:, first : first + 256])
    return gate, plain(block, both[:, hidden + first : hidden + first + 256])


def ffn_rows(block, both, down):
    hidden = down.shape[0]
    parts = []
    for first in range(0, hidden, 256):
        gate, up = hidden_units(block, both, hidden, first)
        parts.append((gate * jax.nn.sigmoid(gate) * up).astype(BF))
    return plain(jnp.concatenate(parts, axis=1), down[...])


def ffn_forward_kernel(normed, both, down, everyone, result, sums, *scratch):
    rows = normed.shape[0]
    team = Team(rows, normed, everyone, sums, scratch)

    def compute(m, start):
        block = everyone[pl.ds(start, 2 * rows), :]
        split_pair(team, m, ffn_rows(block, both, down), sums, team.part)

    team.run(compute, lambda: None, result)


def ffn_back_rows(block, normed, both, down, gated, d_both, here):
    hidden = down.shape[0]
    before = normed[here, :]
    for first in range(0, hidden, 256):
        columns = slice(first, first + 256)
        gate, up = hidden_units(before, both, hidden, first)
        d_gated = right_trans(block, down[columns, :])
        sig = jax.nn.sigmoid(gate)
        act = gate * sig
        gated[here, columns] = (act * up).astype(BF)
        d_both[here, columns] = (d_gated * up * sig * (1.0 + gate * (1.0 - sig))).astype(BF)
        d_both[here, hidden + first : hidden + first + 256] = (d_gated * act).astype(BF)


def ffn_backward_kernel(
    grad, both, down, normed, result, both_part, down_part, everyone, gated, d_both, sums, *scratch
):
    rows = grad.shape[0]
    team = Team(rows, grad, everyone, sums, scratch)

    def compute(m, start):
        here = pl.ds(start, 2 * rows)
        ffn_back_rows(everyone[here, :], normed, both, down, gated, d_both, here)
        split_pair(team, m, right_trans(d_both[here, :], both[...]), sums, team.part)

    def between():
        def down_step(i, carry):
            cols = pl.ds(pl.multiple_of(i * 256, 256), 256)
            down_part[:, cols] = left_trans(gated[...], everyone[:, cols])
            return carry

        def both_step(i, carry):
            cols = pl.ds(pl.multiple_of(i * 256, 256), 256)
            both_part[:, cols] = left_trans(normed[...], d_both[:, cols]).astype(BF)
            return carry

        lax.fori_loop(0, down_part.shape[1] // 256, down_step, 0)
        lax.fori_loop(0, both_part.shape[1] // 256, both_step, 0)

    team.run(compute, between, result)


def ffn_forward(normed, both, down):
    rows, width = normed.shape
    return pl.pallas_call(
        ffn_forward_kernel,
        out_shape=(
            jax.ShapeDtypeStruct((8 * rows, width), BF),
            jax.ShapeDtypeStruct((rows, width), F32),
        ),
        in_specs=in_vmem(3),
        out_specs=in_vmem(2),
        scratch_shapes=[pltpu.VMEM((4, rows, width), F32)] + Team.scratch(rows, width),
        compiler_params=pltpu.CompilerParams(
            collective_id=1, has_side_effects=True, vmem_limit_bytes=VMEM_LIMIT
        ),
        name="ffn_forward",
    )(normed, both, down)


def ffn_backward(grad, both, down, normed):
    rows, width = grad.shape
    hidden = down.shape[0]
    return pl.pallas_call(
        ffn_backward_kernel,
        out_shape=(
            jax.ShapeDtypeStruct((rows, width), F32),
            jax.ShapeDtypeStruct((width, 2 * hidden), BF),
            jax.ShapeDtypeStruct((hidden, width), F32),
        ),
        in_specs=in_vmem(4),
        out_specs=in_vmem(3),
        scratch_shapes=[
            pltpu.VMEM((8 * rows, width), BF),
            pltpu.VMEM((8 * rows, hidden), BF),
            pltpu.VMEM((8 * rows, 2 * hidden), BF),
            pltpu.VMEM((4, rows, width), F32),
        ]
        + Team.scratch(rows, width),
        compiler_params=pltpu.CompilerParams(
            collective_id=2, has_side_effects=True, vmem_limit_bytes=VMEM_LIMIT
        ),
        name="ffn_backward",
    )(grad, both, down, normed)


class Place:
    def __init__(self):
        self.index = lax.axis_index("frames")
        self.place = lax.axis_index("pos")
        self.core = lax.rem(self.index, 2)
        self.x = lax.rem(self.index // 2, 2)
        self.z = self.index // 4
        self.core_peer = self.index + 1 - 2 * self.core
        self.x_peer = self.index + 2 - 4 * self.x

    def greet_all(self):
        barrier = pltpu.get_barrier_semaphore()

        def signal(step, carry):
            peer = lax.rem(self.index + step, 16)
            pl.semaphore_signal(barrier, inc=1, device_id=(peer, self.place), device_id_type=MESH)
            return carry

        lax.fori_loop(1, 16, signal, 0)
        pl.semaphore_signal(
            barrier, inc=1, device_id=(self.index, 1 - self.place), device_id_type=MESH
        )
        pl.semaphore_wait(barrier, 16)


class Gather:
    def __init__(self, where, number, source, full, sent, got):
        self.where, self.source, self.full = where, source, full
        self.sent, self.got = sent.at[number], got.at[number]
        self.rows = source.shape[0]

    def shard(self, z, x, core):
        start = (z * 4 + x * 2 + core) * self.rows
        return self.full.at[pl.ds(pl.multiple_of(start, self.rows), self.rows)]

    def copy(self, source, target, sent, got, peer):
        return pltpu.make_async_remote_copy(
            src_ref=source,
            dst_ref=target,
            send_sem=self.sent.at[sent],
            recv_sem=self.got.at[got],
            device_id=(peer, self.where.place),
            device_id_type=MESH,
        )

    def z_copy(self, z, up, own=False):
        w = self.where
        target = self.shard(z, w.x, w.core)
        source = self.source if own else target
        if up:
            return self.copy(source, target, z, z, jnp.minimum(w.index + 4, 15))
        return self.copy(source, target, 4 + z, z, jnp.maximum(w.index - 4, 0))

    def x_copy(self, z, own=False):
        w = self.where
        target = self.shard(z, w.x, w.core)
        return self.copy(self.source if own else target, target, 8 + z, 4 + z, w.x_peer)

    def core_copy(self, z, other_x, own=False):
        w = self.where
        x = 1 - w.x if other_x else w.x
        target = self.shard(z, x, w.core)
        number = z * 2 + other_x
        return self.copy(
            self.source if own else target, target, 12 + number, 8 + number, w.core_peer
        )

    def local(self):
        w = self.where
        return pltpu.make_async_copy(
            self.source, self.shard(w.z, w.x, w.core), self.got.at[w.z]
        )

    def start(self):
        w = self.where
        pl.when(w.z < 3)(lambda: self.z_copy(w.z, True, True).start())
        pl.when(w.z > 0)(lambda: self.z_copy(w.z, False, True).start())
        self.x_copy(w.z, True).start()
        self.core_copy(w.z, 0, True).start()
        self.local().start()

    def pass_z(self, distance):
        w = self.where

        @pl.when(w.z >= distance)
        def _():
            z = w.z - distance
            self.z_copy(z, True).wait_recv()
            pl.when(w.z < 3)(lambda: self.z_copy(z, True).start())
            self.x_copy(z).start()
            self.core_copy(z, 0).start()

        @pl.when(w.z + distance <= 3)
        def _():
            z = w.z + distance
            self.z_copy(z, False).wait_recv()
            pl.when(w.z > 0)(lambda: self.z_copy(z, False).start())
            self.x_copy(z).start()
            self.core_copy(z, 0).start()

    def pass_x(self):
        w = self.where

        def hand(z):
            target = self.shard(z, 1 - w.x, w.core)
            self.copy(target, target, 8 + z, 4 + z, w.x_peer).wait_recv()
            self.core_copy(z, 1).start()

        hand(w.z)
        for distance in (1, 2, 3):
            pl.when(w.z >= distance)(lambda: hand(w.z - distance))
            pl.when(w.z + distance <= 3)(lambda: hand(w.z + distance))

    def finish(self):
        w = self.where
        for z in range(4):
            for other_x in (0, 1):
                x = 1 - w.x if other_x else w.x
                target = self.shard(z, x, 1 - w.core)
                number = z * 2 + other_x
                self.copy(target, target, 12 + number, 8 + number, w.core_peer).wait_recv()
        self.local().wait()

    def drain(self):
        w = self.where
        for z in range(4):
            pl.when((z <= w.z) & (w.z < 3))(lambda: self.z_copy(z, True).wait_send())
            pl.when((z >= w.z) & (w.z > 0))(lambda: self.z_copy(z, False).wait_send())
            self.x_copy(z).wait_send()
            self.core_copy(z, 0).wait_send()
            self.core_copy(z, 1).wait_send()

    def all_steps(self):
        for distance in (1, 2, 3):
            self.pass_z(distance)
        self.pass_x()


class Slices:
    def __init__(self, where, layer, gate, up, down, both, down_all, sent, got):
        self.where, self.both, self.down_all = where, both.at[layer], down_all.at[layer]
        self.gate, self.up, self.down = gate.at[layer], up.at[layer], down.at[layer]
        self.sent, self.got = sent.at[layer], got.at[layer]
        self.rows = self.gate.shape[0]
        self.hidden = self.down_all.shape[0]

    def piece(self, source, side, member):
        here = pl.ds(pl.multiple_of(self.where.index * self.rows, self.rows), self.rows)
        columns = pl.ds(pl.multiple_of(member * self.hidden, self.hidden), self.hidden)
        return source.at[:, columns], self.both.at[
            here, side * self.hidden : (side + 1) * self.hidden
        ]

    def remote(self, source, target, number, peer):
        return pltpu.make_async_remote_copy(
            src_ref=source,
            dst_ref=target,
            send_sem=self.sent.at[number],
            recv_sem=self.got.at[number],
            device_id=(peer, self.where.place),
            device_id_type=MESH,
        )

    def down_target(self):
        half = self.hidden // 2
        start = lax.rem(self.where.index, 2) * half
        return self.down_all.at[pl.ds(pl.multiple_of(start, half), half)]

    def start(self):
        index = self.where.index

        def send(step, carry):
            peer = lax.rem(index + step, 16)
            for side, source in ((0, self.gate), (1, self.up)):
                part, target = self.piece(source, side, lax.rem(peer, 8))
                self.remote(part, target, 0, peer).start()
            return carry

        lax.fori_loop(1, 16, send, 0)
        for side, source in ((0, self.gate), (1, self.up)):
            part, target = self.piece(source, side, lax.rem(index, 8))
            pltpu.make_async_copy(part, target, self.got.at[0]).start()
        for team in (0, 1):
            peer = team * 8 + index // 2

            @pl.when(peer != index)
            def _():
                self.remote(self.down, self.down_target(), 1, peer).start()

            @pl.when(peer == index)
            def _():
                pltpu.make_async_copy(self.down, self.down_target(), self.got.at[1]).start()

    def finish(self):
        pltpu.make_async_copy(self.both, self.both, self.got.at[0]).wait()
        pltpu.make_async_copy(self.down_all, self.down_all, self.got.at[1]).wait()

    def drain(self):
        index = self.where.index
        most = self.both.at[pl.ds(0, 15 * self.rows)]
        pltpu.make_async_copy(most, most, self.sent.at[0]).wait()
        ends = (index == 0) | (index == 15)
        half = self.down_all.at[pl.ds(0, self.hidden // 2)]

        @pl.when(ends)
        def _():
            pltpu.make_async_copy(half, half, self.sent.at[1]).wait()

        @pl.when(jnp.logical_not(ends))
        def _():
            pltpu.make_async_copy(self.down_all, self.down_all, self.sent.at[1]).wait()


def two_parts(values):
    high = values.astype(BF)
    return high, (values - high.astype(F32)).astype(BF)


def heads_summed(values, heads):
    high, low = two_parts(values)
    return plain(high, heads[...]) + plain(low, heads[...])


def heads_spread(values, heads):
    high, low = two_parts(values)
    return right_trans(high, heads[...]) + right_trans(low, heads[...])


def fill_heads(heads):
    rows = lax.broadcasted_iota(jnp.int32, heads.shape, 0) // HD
    columns = lax.broadcasted_iota(jnp.int32, heads.shape, 1)
    heads[...] = jnp.where(rows == columns, 1.0, 0.0).astype(BF)


def probabilities(q, k, k0, heads, place):
    own = heads_summed(q * k, heads) / math.sqrt(HD)
    past = jnp.where(place > 0, heads_summed(q * k0, heads) / math.sqrt(HD), -1e30)
    largest = jnp.maximum(own, past)
    own, past = jnp.exp(own - largest), jnp.exp(past - largest)
    total = own + past
    return own / total, past / total


def forward_kernel(
    frames, onehot, gain_shard, table, qkv0, qkv1, out0, out1, gate, up, down, *refs
):
    (act, stream, middle, qkv, other, attended, everyone, gain_rows) = refs[:8]
    (qkv0_out, qkv1_out, outs_out, both_out, down_out) = refs[8:13]
    (gains, table_all, qkv0_all, qkv1_all, outs_all, both, down_all) = refs[13:20]
    (heads, normed, result, sums, gather_sent, gather_got, slice_sent, slice_got) = refs[20:28]
    (y_sent, y_got, saved) = refs[28:31]
    team_scratch = refs[31:39]
    team_sent, team_got = refs[39:41]
    rows, width = frames.shape
    where = Place()

    def gather(number, source, full):
        return Gather(where, number, source, full, gather_sent, gather_got)

    gain_gather = gather(0, gain_shard, gains)
    table_gather = gather(1, table, table_all)
    qkv_gathers = [gather(2, qkv0, qkv0_all), gather(3, qkv1, qkv1_all)]
    out_gathers = [gather(4, out0, outs_all.at[0]), gather(5, out1, outs_all.at[1])]
    slices = [
        Slices(where, layer, gate, up, down, both, down_all, slice_sent, slice_got)
        for layer in range(LAYERS)
    ]
    where.greet_all()
    for item in (gain_gather, table_gather, qkv_gathers[0], out_gathers[0]):
        item.start()
    slices[0].start()
    fill_heads(heads)
    gain_gather.all_steps()
    table_gather.all_steps()
    qkv_gathers[0].all_steps()
    out_gathers[0].all_steps()
    gain_gather.finish()
    for block in range(8):
        first, second = block * 16, block * 16 + 8
        gain_rows[:, block * 128 : (block + 1) * 128] = (
            gains[first : first + 8, :] + gains[second : second + 8, :]
        )
    table_gather.finish()
    for first in range(0, width, 256):
        columns = slice(first, first + 256)
        stream[0, :, columns] = frames[:, columns].astype(F32) + plain(
            onehot[...], table_all[:, columns]
        )
    saves = []

    def save(source, target, number):
        copy = pltpu.make_async_copy(source, target, saved.at[number])
        copy.start()
        saves.append(copy)

    for layer in range(LAYERS):
        value = stream[layer]
        normed[...] = (value * inverse_rms(value) * gain_rows[layer : layer + 1, :]).astype(BF)
        qkv_gathers[layer].finish()
        weights = (qkv0_all, qkv1_all)[layer]
        save(weights, (qkv0_out, qkv1_out)[layer], layer)
        exchange = pltpu.make_async_remote_copy(
            src_ref=qkv.at[layer, :, pl.ds(width, 2 * width)],
            dst_ref=other.at[layer],
            send_sem=y_sent.at[layer],
            recv_sem=y_got.at[layer],
            device_id=(where.index, 1 - where.place),
            device_id_type=MESH,
        )
        for first in list(range(width, 3 * width, 512)) + list(range(0, width, 512)):
            if first == 0:
                exchange.start()
            columns = slice(first, first + 512)
            qkv[layer, :, columns] = plain(normed[...], weights[:, columns]).astype(BF)
        exchange.wait_recv()
        q = qkv[layer, :, :width].astype(F32)
        k = qkv[layer, :, width : 2 * width].astype(F32)
        k0 = other[layer, :, :width].astype(F32)
        own, past = probabilities(q, k, k0, heads, where.place)
        attended[layer] = (
            heads_spread(own, heads) * qkv[layer, :, 2 * width :].astype(F32)
            + heads_spread(past, heads) * other[layer, :, width:].astype(F32)
        ).astype(BF)
        out_gathers[layer].finish()
        for first in range(0, width, 512):
            columns = slice(first, first + 512)
            middle[layer, :, columns] = stream[layer, :, columns] + plain(
                attended[layer], outs_all[layer, :, columns]
            )
        value = middle[layer]
        normed[...] = (value * inverse_rms(value) * gain_rows[2 + layer : 3 + layer, :]).astype(BF)
        slices[layer].finish()
        save(both.at[layer], both_out.at[layer], 2 + layer)
        save(down_all.at[layer], down_out.at[layer], 4 + layer)
        team = Team(
            rows,
            normed,
            everyone.at[layer],
            sums,
            tuple(team_scratch) + (team_sent.at[layer], team_got.at[layer]),
        )

        def compute(m, start):
            block = everyone[layer, pl.ds(start, 2 * rows), :]
            rows_out = ffn_rows(block, both.at[layer], down_all.at[layer])
            split_pair(team, m, rows_out, sums, team.part)

        later = None
        if layer == 0:
            for item in (qkv_gathers[1], out_gathers[1]):
                item.start()
            slices[1].start()

            def later(m):
                for step in (1, 2, 3):

                    @pl.when(m == step)
                    def _():
                        for item in (qkv_gathers[1], out_gathers[1]):
                            item.pass_z(step)

        def between():
            if layer == 0:
                for item in (qkv_gathers[1], out_gathers[1]):
                    item.pass_x()

        team.run(compute, lambda: None, result, later)
        between()
        if layer == 0:
            stream[1] = middle[0] + result[...]
        else:
            act[...] = (middle[1] + result[...]).astype(BF)
        exchange.wait_send()
    save(outs_all, outs_out, 6)
    for item in [gain_gather, table_gather] + qkv_gathers + out_gathers + slices:
        item.drain()
    for copy in saves:
        copy.wait()


def forward(frames, onehot, gain_shard, table, w_qkv, w_out, gate, up, down):
    rows, width = frames.shape
    hidden = gate.shape[2] // 8
    vocab = table.shape[0] * 16
    shape = jax.ShapeDtypeStruct
    hbm = pl.BlockSpec(memory_space=pl.ANY)
    return pl.pallas_call(
        forward_kernel,
        out_shape=(
            shape((rows, width), BF),
            shape((2, rows, width), F32),
            shape((2, rows, width), F32),
            shape((2, rows, 3 * width), BF),
            shape((2, rows, 2 * width), BF),
            shape((2, rows, width), BF),
            shape((2, 8 * rows, width), BF),
            shape((8, width), F32),
            shape((width, 3 * width), BF),
            shape((width, 3 * width), BF),
            shape((2, width, width), BF),
            shape((2, width, 2 * hidden), BF),
            shape((2, hidden, width), BF),
        ),
        in_specs=in_vmem(2) + [hbm] * 9,
        out_specs=tuple(in_vmem(8) + [hbm] * 5),
        scratch_shapes=[
            pltpu.VMEM((8 * 16, 128), F32),
            pltpu.VMEM((vocab, width), BF),
            pltpu.VMEM((width, 3 * width), BF),
            pltpu.VMEM((width, 3 * width), BF),
            pltpu.VMEM((2, width, width), BF),
            pltpu.VMEM((2, width, 2 * hidden), BF),
            pltpu.VMEM((2, hidden, width), BF),
            pltpu.VMEM((width, 128), BF),
            pltpu.VMEM((rows, width), BF),
            pltpu.VMEM((rows, width), F32),
            pltpu.VMEM((4, rows, width), F32),
            pltpu.SemaphoreType.DMA((6, 20)),
            pltpu.SemaphoreType.DMA((6, 16)),
            pltpu.SemaphoreType.DMA((2, 2)),
            pltpu.SemaphoreType.DMA((2, 2)),
            pltpu.SemaphoreType.DMA((2,)),
            pltpu.SemaphoreType.DMA((2,)),
            pltpu.SemaphoreType.DMA((7,)),
        ]
        + Team.scratch(rows, width)[:8]
        + [
            pltpu.SemaphoreType.DMA((2, Team.SCRATCH_COPIES)),
            pltpu.SemaphoreType.DMA((2, Team.SCRATCH_COPIES)),
        ],
        compiler_params=pltpu.CompilerParams(
            collective_id=3, has_side_effects=True, vmem_limit_bytes=63 * 2**20
        ),
        name="forward_pass",
    )(
        frames,
        onehot,
        gain_shard,
        table,
        w_qkv[0],
        w_qkv[1],
        w_out[0],
        w_out[1],
        gate,
        up,
        down,
    )


class Plan:
    def __init__(self, count):
        self.count = count
        self.team = 8
        self.teams = count // self.team
        self.across = [[g * self.team + t for g in range(self.teams)] for t in range(self.team)]

    def ffn_weights(self, gate, up, down):
        rows = gate.shape[0]
        both = jnp.stack([gate, up], axis=1).reshape(rows, 2, self.teams, self.team, -1)
        parts = both.transpose(3, 0, 1, 2, 4).reshape(self.team, rows, -1)
        parts = jnp.broadcast_to(parts[None], (self.teams,) + parts.shape)
        parts = parts.reshape((self.count,) + parts.shape[2:])
        mine = lax.all_to_all(parts, "frames", split_axis=0, concat_axis=0, tiled=True)
        return mine.reshape(self.count * rows, -1), self.gather_across(down)

    def gather_across(self, rows):
        if self.teams != 2:
            return lax.all_gather(rows, "frames", axis=0, tiled=True, axis_index_groups=self.across)
        theirs = lax.ppermute(rows, "frames", self.partners())
        first = lax.axis_index("frames") < self.team
        return jnp.concatenate([jnp.where(first, rows, theirs), jnp.where(first, theirs, rows)])

    def scatter_across(self, rows):
        if self.teams != 2:
            part = lax.psum_scatter(
                rows.astype(BF),
                "frames",
                scatter_dimension=0,
                tiled=True,
                axis_index_groups=self.across,
            )
            return part.astype(F32)
        half = rows.shape[0] // 2
        first = lax.axis_index("frames") < self.team
        mine = jnp.where(first, rows[:half], rows[half:])
        sent = jnp.where(first, rows[half:], rows[:half]).astype(BF)
        return mine + lax.ppermute(sent, "frames", self.partners()).astype(F32)

    def partners(self):
        return [(i, (i + self.team) % self.count) for i in range(self.count)]

    def ffn_grads(self, both_part, down_part):
        parts = both_part.astype(BF).reshape(self.count, -1, both_part.shape[1])
        parts = lax.all_to_all(parts, "frames", split_axis=0, concat_axis=0, tiled=True)
        rows = parts.shape[1]
        parts = parts.astype(F32).reshape(self.teams, self.team, rows, -1).sum(axis=0)
        if self.count == 16:
            half = down_part.shape[0] // 2
            first = lax.axis_index("frames") < 8
            one, two = down_part[:half].astype(BF), down_part[half:].astype(BF)
            straight = [(i, 2 * (i % 8) + i // 8) for i in range(16)]
            crossed = [(i, 2 * (i % 8) + 1 - i // 8) for i in range(16)]
            one, two = jnp.where(first, one, two), jnp.where(first, two, one)
            down = lax.ppermute(one, "frames", straight).astype(F32)
            down = down + lax.ppermute(two, "frames", crossed).astype(F32)
            parts = parts.reshape(self.team, rows, 2, -1)
            both = parts.transpose(1, 2, 0, 3).reshape(rows, 2, -1)
            return both[:, 0], both[:, 1], down
        down = self.scatter_across(down_part)
        parts = parts.reshape(self.team, rows, 2, self.teams, -1)
        both = parts.transpose(1, 2, 3, 0, 4).reshape(rows, 2, -1)
        return both[:, 0], both[:, 1], down


def attend(qkv, other):
    width = HEADS * HD
    position = lax.axis_index("pos")
    q, k, v = (qkv[:, i * width : (i + 1) * width].astype(F32) for i in range(3))
    k0, v0 = (other[:, i * width : (i + 1) * width].astype(F32) for i in range(2))
    own = head_sum(q * k) / math.sqrt(HD)
    past = jnp.where(position > 0, head_sum(q * k0) / math.sqrt(HD), -1e30)
    largest = jnp.maximum(own, past)
    own, past = jnp.exp(own - largest), jnp.exp(past - largest)
    total = own + past
    own, past = own / total, past / total
    attended = head_spread(own) * v + head_spread(past) * v0
    return attended.astype(BF), own, past


def attend_back(grad, qkv, other, own, past):
    width = HEADS * HD
    q, k, v = (qkv[:, i * width : (i + 1) * width].astype(F32) for i in range(3))
    k0, v0 = (other[:, i * width : (i + 1) * width].astype(F32) for i in range(2))
    grad = grad.astype(F32)
    d_own, d_past = head_sum(grad * v), head_sum(grad * v0)
    inner = own * d_own + past * d_past
    s_own = head_spread(own * (d_own - inner) / math.sqrt(HD))
    s_past = head_spread(past * (d_past - inner) / math.sqrt(HD))
    own, past = head_spread(own), head_spread(past)
    d_q = s_own * k + s_past * k0
    d_k = s_own * q
    d_v = own * grad
    d_other = jnp.concatenate([s_past * q, past * grad], axis=1)
    return d_q, d_k, d_v, d_other


def plain_forward(
    plan, onward, frames_in, onehot, code_table, w_qkv, w_out, w_gate, w_up, w_down, gain_attn, gain_ffn
):
    width = frames_in.shape[-1]
    gains = jnp.stack([gain_attn[0, 0], gain_attn[1, 0], gain_ffn[0, 0], gain_ffn[1, 0]], axis=1)
    gains = jnp.pad(gains, ((0, 0), (0, 124)))
    full_table = lax.all_gather(code_table[0], "frames", axis=0, tiled=True)
    first_qkv = lax.all_gather(
        jnp.concatenate([w_qkv[0, 0], gains], axis=1), "frames", axis=0, tiled=True
    )
    gain_rows = first_qkv[:, 3 * width : 3 * width + 4].astype(F32).T
    qkv_all = [first_qkv[:, : 3 * width], None]
    out_all = [lax.all_gather(w_out[0, 0], "frames", axis=0, tiled=True), None]
    ffn_all = [plan.ffn_weights(w_gate[0, 0], w_up[0, 0], w_down[0, 0]), None]
    qkv_all[1] = lax.all_gather(w_qkv[1, 0], "frames", axis=0, tiled=True)
    out_all[1] = lax.all_gather(w_out[1, 0], "frames", axis=0, tiled=True)
    ffn_all[1] = plan.ffn_weights(w_gate[1, 0], w_up[1, 0], w_down[1, 0])

    stream = frames_in[:, 0].astype(F32) + plain(onehot, full_table)
    kept = []
    for layer in range(LAYERS):
        inv_attn = inverse_rms(stream)
        normed_attn = (stream * inv_attn * gain_rows[layer]).astype(BF)
        qkv = plain(normed_attn, qkv_all[layer]).astype(BF)
        other = lax.ppermute(qkv[:, width:], "pos", onward)
        attended, own, past = attend(qkv, other)
        middle = stream + plain(attended, out_all[layer])
        inv_ffn = inverse_rms(middle)
        normed_ffn = (middle * inv_ffn * gain_rows[2 + layer]).astype(BF)
        both_all, down_all = ffn_all[layer]
        team_normed, summed = ffn_forward(normed_ffn, both_all, down_all)
        new_stream = middle + summed
        kept.append(
            (
                stream,
                inv_attn,
                normed_attn,
                qkv,
                other,
                own,
                past,
                attended,
                middle,
                inv_ffn,
                team_normed,
            )
        )
        stream = new_stream
    return kept, stream, gain_rows, qkv_all, out_all, ffn_all


def fused_forward(
    frames_in, onehot, code_table, w_qkv, w_out, w_gate, w_up, w_down, gain_attn, gain_ffn
):
    share = gain_attn.shape[-1]
    gains = jnp.concatenate([gain_attn[:, 0], gain_ffn[:, 0]], axis=0).astype(F32)
    gains = jnp.pad(gains, ((0, 4), (0, share)))
    odd = lax.rem(lax.axis_index("frames"), 2) == 1
    gains = jnp.where(odd, jnp.roll(gains, share, axis=1), gains)
    (act, stream, middle, qkv, other, attended, normed, gain_rows, qkv0, qkv1, outs, both, down) = (
        forward(
            frames_in[:, 0],
            onehot,
            gains,
            code_table[0],
            w_qkv[:, 0],
            w_out[:, 0],
            w_gate[:, 0],
            w_up[:, 0],
            w_down[:, 0],
        )
    )
    kept = []
    for layer in range(LAYERS):
        inv_attn = inverse_rms(stream[layer])
        normed_attn = (stream[layer] * inv_attn * gain_rows[layer]).astype(BF)
        unused, own, past = attend(qkv[layer], other[layer])
        inv_ffn = inverse_rms(middle[layer])
        kept.append(
            (
                stream[layer],
                inv_attn,
                normed_attn,
                qkv[layer],
                other[layer],
                own,
                past,
                attended[layer],
                middle[layer],
                inv_ffn,
                normed[layer],
            )
        )
    ffn_all = [(both[layer], down[layer]) for layer in range(LAYERS)]
    return kept, act, gain_rows, [qkv0, qkv1], outs, ffn_all


def body(
    frames_in,
    code_table,
    code_ids,
    delays,
    item_lengths,
    w_qkv,
    w_out,
    w_gate,
    w_up,
    w_down,
    gain_attn,
    gain_ffn,
    cotangent,
):
    count = lax.axis_size("frames")
    plan = Plan(count)
    positions = lax.axis_size("pos")
    onward = [(i, i + 1) for i in range(positions - 1)]
    backward = [(i + 1, i) for i in range(positions - 1)]
    local_frames = frames_in.shape[0]
    item_count = item_lengths.shape[0]
    width = frames_in.shape[-1]

    neighbours = [(i, i + 1) for i in range(count - 1)]
    earlier = lax.ppermute(code_ids[local_frames - 2 :], "frames", neighbours)
    extended = jnp.concatenate([earlier, code_ids], axis=0)[:, 0]
    global_frame = lax.axis_index("frames") * local_frames + jnp.arange(
        local_frames, dtype=jnp.int32
    )
    item_ends = jnp.cumsum(item_lengths)
    starts = item_ends - item_lengths
    item_index = jnp.sum((starts[None, :] <= global_frame[:, None]).astype(jnp.int32), axis=1) - 1
    chosen = item_index[:, None] == jnp.arange(item_count, dtype=jnp.int32)[None, :]
    item_begin = jnp.sum(jnp.where(chosen, starts[None, :], 0), axis=1)
    delay_rows = jnp.sum(jnp.where(chosen, delays[:, 0][None, :], 0), axis=1)
    one_back = extended[1 : local_frames + 1]
    two_back = extended[:local_frames]
    code_rows = jnp.where(delay_rows == 1, one_back, two_back)
    is_valid = global_frame - delay_rows >= item_begin
    vocab_size = code_table.shape[1] * count
    matches = code_rows[:, None] == jnp.arange(vocab_size, dtype=jnp.int32)[None, :]
    onehot = (matches & is_valid[:, None]).astype(BF)

    if count == 16:
        kept, stream, gain_rows, qkv_all, out_all, ffn_all = fused_forward(
            frames_in, onehot, code_table, w_qkv, w_out, w_gate, w_up, w_down, gain_attn, gain_ffn
        )
    else:
        kept, stream, gain_rows, qkv_all, out_all, ffn_all = plain_forward(
            plan, onward, frames_in, onehot, code_table, w_qkv, w_out, w_gate, w_up, w_down,
            gain_attn, gain_ffn,
        )
    output = stream.astype(BF)[:, None, :]

    gradient = cotangent[:, 0].astype(F32)
    collected = [None] * LAYERS
    gain_parts = [None] * (2 * LAYERS)
    for layer in reversed(range(LAYERS)):
        (
            stream,
            inv_attn,
            normed_attn,
            qkv,
            other,
            own,
            past,
            attended,
            middle,
            inv_ffn,
            team_normed,
        ) = kept[layer]
        both_all, down_all = ffn_all[layer]
        grad_normed, both_part, down_part = ffn_backward(
            gradient.astype(BF), both_all, down_all, team_normed
        )
        ffn_shares = plan.ffn_grads(both_part, down_part)
        grad_middle, gain_parts[2 + layer] = norm_back(
            grad_normed, middle, inv_ffn, gain_rows[2 + layer]
        )
        grad_middle = gradient + grad_middle
        grad_attn = grad_middle.astype(BF)
        grad_attended = right_trans(grad_attn, out_all[layer]).astype(BF)
        d_q, d_k, d_v, d_other = attend_back(grad_attended, qkv, other, own, past)
        arrived = lax.ppermute(d_other.astype(BF), "pos", backward).astype(F32)
        grad_qkv = jnp.concatenate([d_q, d_k + arrived[:, :width], d_v + arrived[:, width:]], axis=1)
        grad_qkv = grad_qkv.astype(BF)
        out_part = left_trans(attended, grad_attn).astype(BF)
        out_share = lax.psum_scatter(out_part, "frames", scatter_dimension=0, tiled=True)
        grad_normed_attn = right_trans(grad_qkv, qkv_all[layer])
        grad_stream, gain_parts[layer] = norm_back(
            grad_normed_attn, stream, inv_attn, gain_rows[layer]
        )
        gradient = grad_middle + grad_stream
        qkv_part = left_trans(normed_attn, grad_qkv).astype(BF)
        if layer == 0:
            tail = jnp.stack(gain_parts, axis=1).astype(BF)
            qkv_part = jnp.concatenate([qkv_part, jnp.pad(tail, ((0, 0), (0, 124)))], axis=1)
        qkv_share = lax.psum_scatter(qkv_part, "frames", scatter_dimension=0, tiled=True)
        collected[layer] = (qkv_share.astype(F32), out_share.astype(F32)) + ffn_shares
    table_part = left_trans(onehot, gradient.astype(BF)).astype(BF)
    table_share = lax.psum_scatter(table_part, "frames", scatter_dimension=0, tiled=True)
    gain_shares = collected[0][0][:, 3 * width : 3 * width + 4].T
    collected[0] = (collected[0][0][:, : 3 * width],) + collected[0][1:]
    stacked = [
        jnp.stack([collected[layer][slot] for layer in range(LAYERS)], axis=0)[:, None]
        for slot in range(5)
    ]
    return (
        output,
        gradient[:, None, :],
        table_share.astype(F32)[None],
        stacked[0],
        stacked[1],
        stacked[2],
        stacked[3],
        stacked[4],
        gain_shares[:2][:, None],
        gain_shares[2:][:, None],
    )


def solution(mesh):
    return jax.shard_map(
        body,
        mesh=mesh,
        in_specs=(
            P("frames", "pos", None),
            P("pos", "frames", None),
            P("frames", "pos"),
            P(None, "pos"),
            P(),
            P(None, "pos", "frames", None),
            P(None, "pos", "frames", None),
            P(None, "pos", "frames", None),
            P(None, "pos", "frames", None),
            P(None, "pos", "frames", None),
            P(None, "pos", "frames"),
            P(None, "pos", "frames"),
            P("frames", "pos", None),
        ),
        out_specs=(
            P("frames", "pos", None),
            P("frames", "pos", None),
            P("pos", "frames", None),
            P(None, "pos", "frames", None),
            P(None, "pos", "frames", None),
            P(None, "pos", "frames", None),
            P(None, "pos", "frames", None),
            P(None, "pos", "frames", None),
            P(None, "pos", "frames"),
            P(None, "pos", "frames"),
        ),
        check_vma=False,
    )
```

```python
import math

import jax
import jax.numpy as jnp
from jax import lax
from jax.experimental import pallas as pl
from jax.experimental.pallas import tpu as pltpu
from jax.sharding import PartitionSpec as P

HEADS = 16
HD = 64
LAYERS = 2
EPSILON = 1e-06
HIGHEST = lax.Precision.HIGHEST
BF = jnp.bfloat16
F32 = jnp.float32


def plain(left, right):
    return jnp.dot(left, right, preferred_element_type=F32)


def left_trans(left, right):
    return lax.dot_general(left, right, (((0,), (0,)), ((), ())), preferred_element_type=F32)


def right_trans(left, right):
    return lax.dot_general(left, right, (((1,), (1,)), ((), ())), preferred_element_type=F32)


def inverse_rms(stream):
    return lax.rsqrt(jnp.mean(stream * stream, axis=-1, keepdims=True) + EPSILON)


def norm_back(gradient, stream, inverse, gain_row):
    scaled = gradient * gain_row
    gain_grad = jnp.sum(gradient * stream * inverse, axis=0)
    inner_sum = jnp.mean(scaled * stream, axis=-1, keepdims=True)
    return (inverse * scaled - stream * inverse * inverse * inverse * inner_sum, gain_grad)


def head_matrix():
    rows = lax.broadcasted_iota(jnp.int32, (HEADS * HD, HEADS), 0) // HD
    cols = lax.broadcasted_iota(jnp.int32, (HEADS * HD, HEADS), 1)
    return (rows == cols).astype(F32)


def head_sum(values):
    return jnp.dot(values, head_matrix(), precision=HIGHEST)


def head_spread(values):
    return jnp.dot(values, head_matrix().T, precision=HIGHEST)


MESH = pl.DeviceIdType.MESH
VMEM_LIMIT = 60 * 2**20


def in_vmem(count):
    return [pl.BlockSpec(memory_space=pltpu.VMEM)] * count


class Team:
    SCRATCH_COPIES = 19

    def __init__(self, rows, mine, everyone, sums, scratch):
        (self.part, self.from_core, self.from_across, self.from_x, self.from_z) = scratch[:5]
        (self.to_x, self.to_z, self.to_across, self.sent, self.got) = scratch[5:10]
        self.rows, self.half = rows, rows // 2
        self.mine, self.everyone, self.sums = mine, everyone, sums
        index = lax.axis_index("frames")
        self.place = lax.axis_index("pos")
        member = lax.rem(index, 8)
        self.core = lax.rem(member, 2)
        self.x = lax.rem(member // 2, 2)
        self.z = member // 4
        self.core_peer = index + 1 - 2 * self.core
        self.x_peer = index + 2 - 4 * self.x
        self.z_peer = index + 4 - 8 * self.z

    @staticmethod
    def scratch(rows, width):
        half = rows // 2
        return [
            pltpu.VMEM((4, rows, width), BF),
            pltpu.VMEM((4, rows, width), BF),
            pltpu.VMEM((2, half, width), BF),
            pltpu.VMEM((rows, width), BF),
            pltpu.VMEM((rows, width), BF),
            pltpu.VMEM((rows, width), BF),
            pltpu.VMEM((rows, width), BF),
            pltpu.VMEM((rows, width), BF),
            pltpu.SemaphoreType.DMA((Team.SCRATCH_COPIES,)),
            pltpu.SemaphoreType.DMA((Team.SCRATCH_COPIES,)),
        ]

    def greet(self):
        barrier = pltpu.get_barrier_semaphore()
        for peer in (self.core_peer, self.x_peer, self.z_peer):
            pl.semaphore_signal(barrier, inc=1, device_id=(peer, self.place), device_id_type=MESH)
        pl.semaphore_wait(barrier, 3)

    def copy(self, number, source, target, peer):
        return pltpu.make_async_remote_copy(
            src_ref=source,
            dst_ref=target,
            send_sem=self.sent.at[number],
            recv_sem=self.got.at[number],
            device_id=(peer, self.place),
            device_id_type=MESH,
        )

    def pair_start(self, m):
        x = self.x + (m % 2) * (1 - 2 * self.x)
        z = self.z + (m // 2) * (1 - 2 * self.z)
        return pl.multiple_of((z * 2 + x) * (2 * self.rows), 2 * self.rows)

    def shard(self, m, part=None, core=None):
        core = self.core if core is None else core
        start = self.pair_start(m) + core * self.rows
        size = self.rows
        if part is not None:
            start, size = start + part * self.half, self.half
        return self.everyone.at[pl.ds(pl.multiple_of(start, 16), size)]

    def gather_copies(self):
        own = self.shard(0)
        x_rows, z_rows = self.shard(1), self.shard(2)
        x_low, z_high = self.shard(1, 1), self.shard(2, 0)
        high, low = self.shard(3, 0), self.shard(3, 1)
        return [
            self.copy(0, self.mine, own, self.core_peer),
            self.copy(1, self.mine, own, self.x_peer),
            self.copy(2, self.mine, own, self.z_peer),
            self.copy(3, x_rows, x_rows, self.core_peer),
            self.copy(4, x_low, x_low, self.z_peer),
            self.copy(5, z_rows, z_rows, self.core_peer),
            self.copy(6, z_high, z_high, self.x_peer),
            self.copy(7, high, high, self.core_peer),
            self.copy(8, low, low, self.core_peer),
        ]

    def arrived(self, number):
        other = 1 - self.core
        target = [
            self.shard(0, core=other),
            self.shard(1),
            self.shard(2),
            self.shard(1, core=other),
            self.shard(3, 1),
            self.shard(2, core=other),
            self.shard(3, 0),
            self.shard(3, 0, core=other),
            self.shard(3, 1, core=other),
        ][number]
        self.copy(number, target, target, self.core_peer).wait_recv()

    def sum_copies(self):
        half = self.half
        high, low = pl.ds(0, half), pl.ds(half, half)
        copies = [
            self.copy(9 + m, self.part.at[m], self.from_core.at[m], self.core_peer)
            for m in range(4)
        ]
        copies += [
            self.copy(13, self.to_across.at[high], self.from_across.at[0], self.x_peer),
            self.copy(14, self.to_across.at[low], self.from_across.at[1], self.z_peer),
            self.copy(15, self.to_x.at[high], self.from_x.at[high], self.x_peer),
            self.copy(16, self.to_x.at[low], self.from_x.at[low], self.x_peer),
            self.copy(17, self.to_z.at[low], self.from_z.at[low], self.z_peer),
            self.copy(18, self.to_z.at[high], self.from_z.at[high], self.z_peer),
        ]
        return copies

    def run(self, compute, between, result, later=None, early=None):
        half, rows = self.half, self.rows
        gather = self.gather_copies()
        adds = self.sum_copies()
        for copy in gather[:3]:
            copy.start()
        start = self.pair_start(0) + self.core * rows
        self.everyone[pl.ds(pl.multiple_of(start, 16), rows), :] = self.mine[...]
        if early is not None:
            early()

        def total(m, first):
            return self.sums[m, first : first + half, :] + self.from_core[
                m, first : first + half, :
            ].astype(F32)

        def step(m, carry):
            @pl.when(m == 0)
            def _():
                self.arrived(0)

            @pl.when(m == 1)
            def _():
                self.arrived(1)
                gather[4].start()
                gather[3].start()
                self.arrived(2)
                gather[6].start()
                gather[5].start()
                self.arrived(3)

            @pl.when(m == 2)
            def _():
                self.arrived(5)

            @pl.when(m == 3)
            def _():
                self.arrived(6)
                gather[7].start()
                self.arrived(4)
                gather[8].start()
                self.arrived(7)
                self.arrived(8)

            compute(m, self.pair_start(m))
            self.copy(9 + m, self.part.at[m], self.from_core.at[m], self.core_peer).start()
            if later is not None:
                later(m)

            @pl.when(m == 2)
            def _():
                adds[1].wait_recv()
                self.to_x[:half, :] = total(1, 0).astype(BF)
                adds[6].start()

            return carry

        lax.fori_loop(0, 4, step, 0)
        adds[3].wait_recv()
        self.to_across[:half, :] = total(3, 0).astype(BF)
        adds[4].start()
        self.to_across[half:, :] = total(3, half).astype(BF)
        adds[5].start()
        adds[2].wait_recv()
        self.to_z[half:, :] = total(2, half).astype(BF)
        adds[8].start()
        between()
        for copy in gather:
            copy.wait_send()
        adds[5].wait_recv()
        self.to_x[half:, :] = (total(1, half) + self.from_across[1].astype(F32)).astype(BF)
        adds[7].start()
        adds[4].wait_recv()
        self.to_z[:half, :] = (total(2, 0) + self.from_across[0].astype(F32)).astype(BF)
        adds[9].start()
        adds[0].wait_recv()
        for number in (6, 7, 8, 9):
            adds[number].wait_recv()
        for first in (0, half):
            rows_here = slice(first, first + half)
            result[rows_here, :] = (
                total(0, first)
                + self.from_x[rows_here, :].astype(F32)
                + self.from_z[rows_here, :].astype(F32)
            )
        for copy in adds:
            copy.wait_send()


def split_pair(team, m, product, sums, part):
    rows = team.rows
    for first in range(0, sums.shape[2], 256):
        columns = slice(first, first + 256)
        value = product(columns)
        low, high = value[:rows], value[rows:]
        sums[m, :, columns] = jnp.where(team.core == 0, low, high)
        part[m, :, columns] = jnp.where(team.core == 0, high, low).astype(BF)


def hidden_units(block, both, hidden, first):
    gate = plain(block, both[:, first : first + 256])
    return gate, plain(block, both[:, hidden + first : hidden + first + 256])


def ffn_rows(block, both, down):
    hidden = down.shape[0]
    parts = []
    for first in range(0, hidden, 256):
        gate, up = hidden_units(block, both, hidden, first)
        parts.append((gate * jax.nn.sigmoid(gate) * up).astype(BF))
    gated = jnp.concatenate(parts, axis=1)
    return lambda columns: plain(gated, down[:, columns])


def ffn_forward_kernel(normed, both, down, everyone, result, sums, *scratch):
    rows = normed.shape[0]
    team = Team(rows, normed, everyone, sums, scratch)
    team.greet()

    def compute(m, start):
        block = everyone[pl.ds(start, 2 * rows), :]
        split_pair(team, m, ffn_rows(block, both, down), sums, team.part)

    team.run(compute, lambda: None, result)


def ffn_back_rows(block, normed, both, down, gated, d_both, here):
    hidden = down.shape[0]
    before = normed[here, :]
    for first in range(0, hidden, 256):
        columns = slice(first, first + 256)
        gate, up = hidden_units(before, both, hidden, first)
        d_gated = right_trans(block, down[columns, :])
        sig = jax.nn.sigmoid(gate)
        act = gate * sig
        gated[here, columns] = (act * up).astype(BF)
        d_both[here, columns] = (d_gated * up * sig * (1.0 + gate * (1.0 - sig))).astype(BF)
        d_both[here, hidden + first : hidden + first + 256] = (d_gated * act).astype(BF)


def ffn_backward_kernel(
    grad, both, down, normed, result, both_part, down_part, everyone, gated, d_both, sums, *scratch
):
    rows = grad.shape[0]
    team = Team(rows, grad, everyone, sums, scratch)
    team.greet()

    def compute(m, start):
        here = pl.ds(start, 2 * rows)
        ffn_back_rows(everyone[here, :], normed, both, down, gated, d_both, here)
        split_pair(team, m, lambda c: right_trans(d_both[here, :], both[c, :]), sums, team.part)

    def between():
        def down_step(i, carry):
            cols = pl.ds(pl.multiple_of(i * 256, 256), 256)
            down_part[:, cols] = left_trans(gated[...], everyone[:, cols])
            return carry

        def both_step(i, carry):
            cols = pl.ds(pl.multiple_of(i * 256, 256), 256)
            both_part[:, cols] = left_trans(normed[...], d_both[:, cols]).astype(BF)
            return carry

        lax.fori_loop(0, down_part.shape[1] // 256, down_step, 0)
        lax.fori_loop(0, both_part.shape[1] // 256, both_step, 0)

    team.run(compute, between, result)


def ffn_forward(normed, both, down):
    rows, width = normed.shape
    return pl.pallas_call(
        ffn_forward_kernel,
        out_shape=(
            jax.ShapeDtypeStruct((8 * rows, width), BF),
            jax.ShapeDtypeStruct((rows, width), F32),
        ),
        in_specs=in_vmem(3),
        out_specs=in_vmem(2),
        scratch_shapes=[pltpu.VMEM((4, rows, width), F32)] + Team.scratch(rows, width),
        compiler_params=pltpu.CompilerParams(
            collective_id=1, has_side_effects=True, vmem_limit_bytes=VMEM_LIMIT
        ),
        name="ffn_forward",
    )(normed, both, down)


def ffn_backward(grad, both, down, normed):
    rows, width = grad.shape
    hidden = down.shape[0]
    return pl.pallas_call(
        ffn_backward_kernel,
        out_shape=(
            jax.ShapeDtypeStruct((rows, width), F32),
            jax.ShapeDtypeStruct((width, 2 * hidden), BF),
            jax.ShapeDtypeStruct((hidden, width), F32),
        ),
        in_specs=in_vmem(4),
        out_specs=in_vmem(3),
        scratch_shapes=[
            pltpu.VMEM((8 * rows, width), BF),
            pltpu.VMEM((8 * rows, hidden), BF),
            pltpu.VMEM((8 * rows, 2 * hidden), BF),
            pltpu.VMEM((4, rows, width), F32),
        ]
        + Team.scratch(rows, width),
        compiler_params=pltpu.CompilerParams(
            collective_id=2, has_side_effects=True, vmem_limit_bytes=VMEM_LIMIT
        ),
        name="ffn_backward",
    )(grad, both, down, normed)


class Place:
    def __init__(self):
        self.index = lax.axis_index("frames")
        self.place = lax.axis_index("pos")
        self.core = lax.rem(self.index, 2)
        self.x = lax.rem(self.index // 2, 2)
        self.z = self.index // 4
        self.core_peer = self.index + 1 - 2 * self.core
        self.x_peer = self.index + 2 - 4 * self.x

    def greet_all(self):
        barrier = pltpu.get_barrier_semaphore()

        def signal(step, carry):
            peer = lax.rem(self.index + step, 16)
            pl.semaphore_signal(barrier, inc=1, device_id=(peer, self.place), device_id_type=MESH)
            return carry

        lax.fori_loop(1, 16, signal, 0)
        pl.semaphore_signal(
            barrier, inc=1, device_id=(self.index, 1 - self.place), device_id_type=MESH
        )
        pl.semaphore_wait(barrier, 16)


class Gather:
    def __init__(self, where, number, source, full, sent, got):
        self.where, self.source, self.full = where, source, full
        self.sent, self.got = sent.at[number], got.at[number]
        self.rows = source.shape[0]

    def shard(self, z, x, core):
        start = (z * 4 + x * 2 + core) * self.rows
        return self.full.at[pl.ds(pl.multiple_of(start, self.rows), self.rows)]

    def copy(self, source, target, sent, got, peer):
        return pltpu.make_async_remote_copy(
            src_ref=source,
            dst_ref=target,
            send_sem=self.sent.at[sent],
            recv_sem=self.got.at[got],
            device_id=(peer, self.where.place),
            device_id_type=MESH,
        )

    def z_copy(self, z, up, own=False):
        w = self.where
        target = self.shard(z, w.x, w.core)
        source = self.source if own else target
        if up:
            return self.copy(source, target, z, z, jnp.minimum(w.index + 4, 15))
        return self.copy(source, target, 4 + z, z, jnp.maximum(w.index - 4, 0))

    def x_copy(self, z, own=False):
        w = self.where
        target = self.shard(z, w.x, w.core)
        return self.copy(self.source if own else target, target, 8 + z, 4 + z, w.x_peer)

    def core_copy(self, z, other_x, own=False):
        w = self.where
        x = 1 - w.x if other_x else w.x
        target = self.shard(z, x, w.core)
        number = z * 2 + other_x
        return self.copy(
            self.source if own else target, target, 12 + number, 8 + number, w.core_peer
        )

    def local(self):
        w = self.where
        return pltpu.make_async_copy(
            self.source, self.shard(w.z, w.x, w.core), self.got.at[w.z]
        )

    def start(self):
        w = self.where
        pl.when(w.z < 3)(lambda: self.z_copy(w.z, True, True).start())
        pl.when(w.z > 0)(lambda: self.z_copy(w.z, False, True).start())
        self.x_copy(w.z, True).start()
        self.core_copy(w.z, 0, True).start()
        self.local().start()

    def pass_z(self, distance):
        w = self.where

        @pl.when(w.z >= distance)
        def _():
            z = w.z - distance
            self.z_copy(z, True).wait_recv()
            pl.when(w.z < 3)(lambda: self.z_copy(z, True).start())
            self.x_copy(z).start()
            self.core_copy(z, 0).start()

        @pl.when(w.z + distance <= 3)
        def _():
            z = w.z + distance
            self.z_copy(z, False).wait_recv()
            pl.when(w.z > 0)(lambda: self.z_copy(z, False).start())
            self.x_copy(z).start()
            self.core_copy(z, 0).start()

    def pass_x(self):
        w = self.where

        def hand(z):
            target = self.shard(z, 1 - w.x, w.core)
            self.copy(target, target, 8 + z, 4 + z, w.x_peer).wait_recv()
            self.core_copy(z, 1).start()

        hand(w.z)
        for distance in (1, 2, 3):
            pl.when(w.z >= distance)(lambda: hand(w.z - distance))
            pl.when(w.z + distance <= 3)(lambda: hand(w.z + distance))

    def finish(self):
        w = self.where
        for z in range(4):
            for other_x in (0, 1):
                x = 1 - w.x if other_x else w.x
                target = self.shard(z, x, 1 - w.core)
                number = z * 2 + other_x
                self.copy(target, target, 12 + number, 8 + number, w.core_peer).wait_recv()
        self.local().wait()

    def drain(self):
        w = self.where
        for z in range(4):
            pl.when((z <= w.z) & (w.z < 3))(lambda: self.z_copy(z, True).wait_send())
            pl.when((z >= w.z) & (w.z > 0))(lambda: self.z_copy(z, False).wait_send())
            self.x_copy(z).wait_send()
            self.core_copy(z, 0).wait_send()
            self.core_copy(z, 1).wait_send()


class Slices:
    def __init__(self, where, layer, gate, up, down, both, down_all, sent, got):
        self.where, self.both, self.down_all = where, both.at[layer], down_all.at[layer]
        self.gate, self.up, self.down = gate.at[layer], up.at[layer], down.at[layer]
        self.sent, self.got = sent.at[layer], got.at[layer]
        self.rows = self.gate.shape[0]
        self.hidden = self.down_all.shape[0]

    def piece(self, source, side, member):
        here = pl.ds(pl.multiple_of(self.where.index * self.rows, self.rows), self.rows)
        columns = pl.ds(pl.multiple_of(member * self.hidden, self.hidden), self.hidden)
        return source.at[:, columns], self.both.at[
            here, side * self.hidden : (side + 1) * self.hidden
        ]

    def remote(self, source, target, number, peer):
        return pltpu.make_async_remote_copy(
            src_ref=source,
            dst_ref=target,
            send_sem=self.sent.at[number],
            recv_sem=self.got.at[number],
            device_id=(peer, self.where.place),
            device_id_type=MESH,
        )

    def down_target(self):
        half = self.hidden // 2
        start = lax.rem(self.where.index, 2) * half
        return self.down_all.at[pl.ds(pl.multiple_of(start, half), half)]

    def start(self):
        index = self.where.index
        base = index - lax.rem(index, 8)

        def send(step, carry):
            member = lax.rem(index + step, 8)
            for side, source in ((0, self.gate), (1, self.up)):
                part, target = self.piece(source, side, member)
                self.remote(part, target, 0, base + member).start()
            return carry

        lax.fori_loop(1, 8, send, 0)
        for side, source in ((0, self.gate), (1, self.up)):
            part, target = self.piece(source, side, lax.rem(index, 8))
            pltpu.make_async_copy(part, target, self.got.at[0]).start()
        for team in (0, 1):
            peer = team * 8 + index // 2

            @pl.when(peer != index)
            def _():
                self.remote(self.down, self.down_target(), 1, peer).start()

            @pl.when(peer == index)
            def _():
                pltpu.make_async_copy(self.down, self.down_target(), self.got.at[1]).start()

    def team_rows(self, team):
        size = 8 * self.rows
        return self.both.at[pl.ds(pl.multiple_of(team * size, size), size)]

    def swap(self):
        mine = self.team_rows(self.where.index // 8)
        return self.remote(mine, mine, 2, lax.rem(self.where.index + 8, 16))

    def pass_on(self):
        mine = self.team_rows(self.where.index // 8)
        pltpu.make_async_copy(mine, mine, self.got.at[0]).wait()
        self.swap().start()

    def finish(self):
        theirs = self.team_rows(1 - self.where.index // 8)
        pltpu.make_async_copy(theirs, theirs, self.got.at[2]).wait()
        pltpu.make_async_copy(self.down_all, self.down_all, self.got.at[1]).wait()

    def drain(self):
        index = self.where.index
        most = self.both.at[pl.ds(0, 7 * self.rows)]
        pltpu.make_async_copy(most, most, self.sent.at[0]).wait()
        self.swap().wait_send()
        ends = (index == 0) | (index == 15)
        half = self.down_all.at[pl.ds(0, self.hidden // 2)]

        @pl.when(ends)
        def _():
            pltpu.make_async_copy(half, half, self.sent.at[1]).wait()

        @pl.when(jnp.logical_not(ends))
        def _():
            pltpu.make_async_copy(self.down_all, self.down_all, self.sent.at[1]).wait()


def two_parts(values):
    high = values.astype(BF)
    return high, (values - high.astype(F32)).astype(BF)


def heads_summed(values, heads):
    high, low = two_parts(values)
    return plain(high, heads[...]) + plain(low, heads[...])


def heads_spread(values, heads):
    high, low = two_parts(values)
    return right_trans(high, heads[...]) + right_trans(low, heads[...])


def fill_heads(heads):
    rows = lax.broadcasted_iota(jnp.int32, heads.shape, 0) // HD
    columns = lax.broadcasted_iota(jnp.int32, heads.shape, 1)
    heads[...] = jnp.where(rows == columns, 1.0, 0.0).astype(BF)


def probabilities(q, k, k0, heads, place):
    own = heads_summed(q * k, heads) / math.sqrt(HD)
    past = jnp.where(place > 0, heads_summed(q * k0, heads) / math.sqrt(HD), -1e30)
    largest = jnp.maximum(own, past)
    own, past = jnp.exp(own - largest), jnp.exp(past - largest)
    total = own + past
    return own / total, past / total


def forward_kernel(
    frames, onehot, gain_shard, table, qkv0, qkv1, out0, out1, gate, up, down, *refs
):
    (act, stream, middle, qkv, other, attended, everyone, gain_rows) = refs[:8]
    (qkv0_out, qkv1_out, outs_out, both_out, down_out) = refs[8:13]
    (gains, table_all, qkv0_all, qkv1_all, outs_all, both, down_all) = refs[13:20]
    (heads, normed, result, sums, gather_sent, gather_got, slice_sent, slice_got) = refs[20:28]
    (y_sent, y_got, saved) = refs[28:31]
    team_scratch = refs[31:39]
    team_sent, team_got = refs[39:41]
    rows, width = frames.shape
    where = Place()

    def gather(number, source, full):
        return Gather(where, number, source, full, gather_sent, gather_got)

    gain_gather = gather(0, gain_shard, gains)
    table_gather = gather(1, table, table_all)
    qkv_gathers = [gather(2, qkv0, qkv0_all), gather(3, qkv1, qkv1_all)]
    out_gathers = [gather(4, out0, outs_all.at[0]), gather(5, out1, outs_all.at[1])]
    slices = [
        Slices(where, layer, gate, up, down, both, down_all, slice_sent, slice_got)
        for layer in range(LAYERS)
    ]
    where.greet_all()
    for item in (gain_gather, table_gather, qkv_gathers[0], out_gathers[0]):
        item.start()
    slices[0].start()
    fill_heads(heads)
    first = (gain_gather, table_gather, qkv_gathers[0], out_gathers[0])
    for item in first:
        for distance in (1, 2, 3):
            item.pass_z(distance)
    slices[0].pass_on()
    for item in first:
        item.pass_x()
    gain_gather.finish()
    for block in range(8):
        first, second = block * 16, block * 16 + 8
        gain_rows[:, block * 128 : (block + 1) * 128] = (
            gains[first : first + 8, :] + gains[second : second + 8, :]
        )
    table_gather.finish()
    for first in range(0, width, 256):
        columns = slice(first, first + 256)
        stream[0, :, columns] = frames[:, columns].astype(F32) + plain(
            onehot[...], table_all[:, columns]
        )
    saves = []
    second = (qkv_gathers[1], out_gathers[1])

    def save(source, target, number):
        copy = pltpu.make_async_copy(source, target, saved.at[number])
        copy.start()
        saves.append(copy)

    for layer in range(LAYERS):
        value = stream[layer]
        normed[...] = (value * inverse_rms(value) * gain_rows[layer : layer + 1, :]).astype(BF)
        qkv_gathers[layer].finish()
        weights = (qkv0_all, qkv1_all)[layer]
        if layer == 0:
            for item in second:
                item.start()
        save(weights, (qkv0_out, qkv1_out)[layer], layer)
        exchange = pltpu.make_async_remote_copy(
            src_ref=qkv.at[layer, :, pl.ds(width, 2 * width)],
            dst_ref=other.at[layer],
            send_sem=y_sent.at[layer],
            recv_sem=y_got.at[layer],
            device_id=(where.index, 1 - where.place),
            device_id_type=MESH,
        )
        for first in list(range(width, 3 * width, 512)) + list(range(0, width, 512)):
            if first == 0:
                exchange.start()
            columns = slice(first, first + 512)
            qkv[layer, :, columns] = plain(normed[...], weights[:, columns]).astype(BF)
        if layer == 0:
            slices[1].start()
        exchange.wait_recv()
        q = qkv[layer, :, :width].astype(F32)
        k = qkv[layer, :, width : 2 * width].astype(F32)
        k0 = other[layer, :, :width].astype(F32)
        own, past = probabilities(q, k, k0, heads, where.place)
        attended[layer] = (
            heads_spread(own, heads) * qkv[layer, :, 2 * width :].astype(F32)
            + heads_spread(past, heads) * other[layer, :, width:].astype(F32)
        ).astype(BF)
        out_gathers[layer].finish()
        for first in range(0, width, 512):
            columns = slice(first, first + 512)
            middle[layer, :, columns] = stream[layer, :, columns] + plain(
                attended[layer], outs_all[layer, :, columns]
            )
        value = middle[layer]
        normed[...] = (value * inverse_rms(value) * gain_rows[2 + layer : 3 + layer, :]).astype(BF)
        if layer == 0:
            for item in second:
                item.pass_z(1)
        slices[layer].finish()
        save(both.at[layer], both_out.at[layer], 2 + layer)
        save(down_all.at[layer], down_out.at[layer], 4 + layer)
        team = Team(
            rows,
            normed,
            everyone.at[layer],
            sums,
            tuple(team_scratch) + (team_sent.at[layer], team_got.at[layer]),
        )

        def compute(m, start):
            block = everyone[layer, pl.ds(start, 2 * rows), :]
            rows_out = ffn_rows(block, both.at[layer], down_all.at[layer])
            split_pair(team, m, rows_out, sums, team.part)

        later = None
        if layer == 0:

            def later(m):
                pl.when(m == 1)(lambda: slices[1].pass_on())
                for step in (2, 3):

                    @pl.when(m == step)
                    def _():
                        for item in second:
                            item.pass_z(step)

        def between():
            if layer == 0:
                for item in second:
                    item.pass_x()

        team.run(compute, lambda: None, result, later)
        between()
        if layer == 0:
            stream[1] = middle[0] + result[...]
        else:
            act[...] = (middle[1] + result[...]).astype(BF)
        exchange.wait_send()
    save(outs_all, outs_out, 6)
    for item in [gain_gather, table_gather] + qkv_gathers + out_gathers + slices:
        item.drain()
    for copy in saves:
        copy.wait()


def forward(frames, onehot, gain_shard, table, w_qkv, w_out, gate, up, down):
    rows, width = frames.shape
    hidden = gate.shape[2] // 8
    vocab = table.shape[0] * 16
    shape = jax.ShapeDtypeStruct
    hbm = pl.BlockSpec(memory_space=pl.ANY)
    return pl.pallas_call(
        forward_kernel,
        out_shape=(
            shape((rows, width), BF),
            shape((2, rows, width), F32),
            shape((2, rows, width), F32),
            shape((2, rows, 3 * width), BF),
            shape((2, rows, 2 * width), BF),
            shape((2, rows, width), BF),
            shape((2, 8 * rows, width), BF),
            shape((8, width), F32),
            shape((width, 3 * width), BF),
            shape((width, 3 * width), BF),
            shape((2, width, width), BF),
            shape((2, width, 2 * hidden), BF),
            shape((2, hidden, width), BF),
        ),
        in_specs=in_vmem(2) + [hbm] * 9,
        out_specs=tuple(in_vmem(8) + [hbm] * 5),
        scratch_shapes=[
            pltpu.VMEM((8 * 16, 128), F32),
            pltpu.VMEM((vocab, width), BF),
            pltpu.VMEM((width, 3 * width), BF),
            pltpu.VMEM((width, 3 * width), BF),
            pltpu.VMEM((2, width, width), BF),
            pltpu.VMEM((2, width, 2 * hidden), BF),
            pltpu.VMEM((2, hidden, width), BF),
            pltpu.VMEM((width, 128), BF),
            pltpu.VMEM((rows, width), BF),
            pltpu.VMEM((rows, width), F32),
            pltpu.VMEM((4, rows, width), F32),
            pltpu.SemaphoreType.DMA((6, 20)),
            pltpu.SemaphoreType.DMA((6, 16)),
            pltpu.SemaphoreType.DMA((2, 3)),
            pltpu.SemaphoreType.DMA((2, 3)),
            pltpu.SemaphoreType.DMA((2,)),
            pltpu.SemaphoreType.DMA((2,)),
            pltpu.SemaphoreType.DMA((7,)),
        ]
        + Team.scratch(rows, width)[:8]
        + [
            pltpu.SemaphoreType.DMA((2, Team.SCRATCH_COPIES)),
            pltpu.SemaphoreType.DMA((2, Team.SCRATCH_COPIES)),
        ],
        compiler_params=pltpu.CompilerParams(
            collective_id=3, has_side_effects=True, vmem_limit_bytes=63 * 2**20
        ),
        name="forward_pass",
    )(
        frames,
        onehot,
        gain_shard,
        table,
        w_qkv[0],
        w_qkv[1],
        w_out[0],
        w_out[1],
        gate,
        up,
        down,
    )


def own_half(values, core, other):
    rows, width = values.shape
    parts = []
    for first in range(0, width, 256):
        low, high = values[:, first : first + 128], values[:, first + 128 : first + 256]
        lane = lax.broadcasted_iota(jnp.int32, low.shape, 1)
        even = jnp.where(lane < 64, low, pltpu.roll(high, 64, 1))
        odd = jnp.where(lane < 64, pltpu.roll(low, 64, 1), high)
        first_core = (core == 0) != other
        parts.append(jnp.where(first_core, even, odd))
    return jnp.concatenate(parts, axis=1)


def backward_kernel(
    cotangent, codes, codes_theirs, gain_rows, stream, middle, qkv, other, attended, normed, qkv0,
    qkv1, outs, both, down, *refs
):
    (input_grad, both_got, pair_got, down_got, attn_got, table_got, gain_got) = refs[:7]
    refs = refs[1:]
    (v_stream, v_middle, v_qkv, v_other, v_attended, v_normed, w_qkv, w_out, w_both, w_down) = refs[
        6:16
    ]
    (grad, d_middle, rounded, normed2, attended2, d_qkv2, d_middle2, for_core, d_other, y_in) = refs[
        16:26
    ]
    (codes2, grad2, part, from_x, everyone, gated, d_both, sums, both_part, down_part) = refs[26:36]
    (gain_sums, heads, loaded, core_sent, core_got, y_sent, y_got, x_sent, x_got) = refs[36:45]
    (z_sent, z_got, f_sent, f_got, f_kept, g_sent, g_got) = refs[45:52]
    team_scratch = refs[52:60]
    team_sent, team_got = refs[60:62]
    rows, width = cotangent.shape
    share = both_part.shape[0] // 16
    where = Place()
    own, theirs = pl.ds(0, rows), pl.ds(rows, rows)
    chunk, small = rows // 2, 32

    def load(source, target, number):
        return pltpu.make_async_copy(source, target, loaded.at[number])

    def loads_of(layer):
        return [
            load(normed.at[layer], v_normed, 0),
            load(both.at[layer], w_both, 1),
            load(down.at[layer], w_down, 2),
            load(middle.at[layer], v_middle, 3),
            load(outs.at[layer], w_out, 4),
            load(qkv.at[layer], v_qkv, 5),
            load(other.at[layer], v_other, 6),
            load(stream.at[layer], v_stream, 7),
            load(attended.at[layer], v_attended, 8),
            load((qkv0, qkv1)[layer], w_qkv, 9),
        ]

    def remote(source, target, sent, got, peer, place=None):
        return pltpu.make_async_remote_copy(
            src_ref=source,
            dst_ref=target,
            send_sem=sent,
            recv_sem=got,
            device_id=(peer, where.place if place is None else place),
            device_id_type=MESH,
        )

    def wait_bytes(like, semaphore):
        pltpu.make_async_copy(like, like, semaphore).wait()

    def to_core(source, target, number):
        return remote(source, target, core_sent.at[number], core_got.at[number], where.core_peer)

    def team_rows(ref, team):
        return ref.at[pl.ds(pl.multiple_of(team * 8 * share, 8 * share), 8 * share)]

    def swap(layer):
        team = where.index // 8
        return remote(
            team_rows(both_part, 1 - team),
            pair_got.at[layer],
            f_sent.at[3 * layer],
            f_got.at[3 * layer],
            lax.rem(where.index + 8, 16),
        )

    def share_ffn(layer, spare):
        index = where.index
        team, member = index // 8, lax.rem(index, 8)
        swap(layer).wait_recv()
        fetch = load(pair_got.at[layer], spare, 12 + layer)
        fetch.start()
        fetch.wait()
        start = pl.multiple_of(team * 8 * share, 8 * share)

        def add(i, carry):
            first = pl.multiple_of(i * 32, 32)
            here = pl.ds(pl.multiple_of(start + first, 32), 32)
            both_part[here, :] = (
                both_part[here, :].astype(F32) + spare[pl.ds(first, 32), :].astype(F32)
            ).astype(BF)
            return carry

        lax.fori_loop(0, 8 * share // 32, add, 0)

        def piece(owner):
            first = pl.multiple_of(start + owner * share, share)
            return both_part.at[pl.ds(first, share)]

        def send(step, carry):
            owner = lax.rem(member + step, 8)
            remote(
                piece(owner),
                both_got.at[layer, member],
                f_sent.at[3 * layer + 2],
                f_got.at[3 * layer + 2],
                team * 8 + owner,
            ).start()
            return carry

        lax.fori_loop(1, 8, send, 0)
        pltpu.make_async_copy(
            piece(member), both_got.at[layer, member], f_kept.at[2 * layer]
        ).start()

    def send_ffn(layer):
        index = where.index
        swap(layer).start()
        half = down_part.shape[0] // 2
        for side in (0, 1):
            owner = 2 * lax.rem(index, 8) + side
            piece = down_part.at[pl.ds(side * half, half)]
            target = down_got.at[layer, index // 8]

            @pl.when(owner != index)
            def _():
                remote(
                    piece, target, f_sent.at[3 * layer + 1], f_got.at[3 * layer + 1], owner
                ).start()

            @pl.when(owner == index)
            def _():
                pltpu.make_async_copy(piece, target, f_kept.at[2 * layer + 1]).start()

    def drain_ffn(layer):
        index = where.index
        swap(layer).wait_send()
        wait_bytes(both_part.at[pl.ds(0, 7 * share)], f_sent.at[3 * layer + 2])
        wait_bytes(both_part.at[pl.ds(0, share)], f_kept.at[2 * layer])
        ends = (index == 0) | (index == 15)
        half = down_part.shape[0] // 2
        semaphore = f_sent.at[3 * layer + 1]

        @pl.when(ends)
        def _():
            wait_bytes(down_part.at[pl.ds(0, half)], semaphore)
            wait_bytes(down_part.at[pl.ds(0, half)], f_kept.at[2 * layer + 1])

        @pl.when(jnp.logical_not(ends))
        def _():
            wait_bytes(down_part, semaphore)

    def landing(layer):
        return from_x if layer == 1 else everyone.at[pl.ds(0, 16 * share)]

    def send_x(layer, piece):
        for z in range(4):
            start = (z * 2 + 1 - where.x) * share
            remote(
                part.at[piece, pl.ds(pl.multiple_of(start, share), share)],
                landing(layer).at[pl.ds((z * 4 + piece) * share, share)],
                x_sent.at[4 * layer + piece],
                x_got.at[4 * layer + piece],
                where.x_peer,
            ).start()

    def attention_grads(piece):
        def step(i, carry):
            here = pl.ds(pl.multiple_of(i * 256, 256), 256)
            if piece < 3:
                right = d_qkv2[:, piece * width : (piece + 1) * width]
                value = left_trans(normed2[:, here], right)
            else:
                value = left_trans(attended2[:, here], d_middle2[...])
            part[piece, here, :] = value.astype(BF)
            return carry

        lax.fori_loop(0, normed2.shape[1] // 256, step, 0)

    def send_z(source, target, number, size):
        for z in range(4):
            piece = source.at[pl.ds(z * size, size)]
            peer = z * 4 + where.x * 2 + where.core

            @pl.when(where.z != z)
            def _():
                remote(piece, target, z_sent.at[number], z_got.at[number], peer).start()

            @pl.when(where.z == z)
            def _():
                pltpu.make_async_copy(piece, target, z_got.at[number]).start()

    def finish_x(layer):
        arrived = landing(layer)
        for piece in range(4):
            wait_bytes(arrived.at[pl.ds(0, 4 * share)], x_got.at[4 * layer + piece])
            for z in range(4):
                start = pl.multiple_of((z * 2 + where.x) * share, share)
                here = pl.ds((z * 4 + piece) * share, share)
                arrived[here, :] = (
                    arrived[here, :].astype(F32)
                    + part[piece, pl.ds(start, share), :].astype(F32)
                ).astype(BF)
        send_z(arrived, attn_got.at[layer, where.z], layer, 4 * share)

    first_loads = loads_of(1)
    starting = [load(cotangent, rounded, 10), load(codes, codes2.at[own], 11)]
    for copy in starting + first_loads:
        copy.start()
    where.greet_all()
    codes_copy = to_core(codes_theirs, codes2.at[theirs], 8)
    codes_copy.start()
    starting[0].wait()
    grad[...] = rounded[...].astype(F32)
    gain_sums[...] = jnp.zeros_like(gain_sums)
    fill_heads(heads)
    waiting = {1: first_loads, 0: loads_of(0)}

    for layer in (1, 0):
        copies = waiting[layer]
        team = Team(
            rows,
            rounded,
            everyone,
            sums,
            tuple(team_scratch) + (team_sent.at[layer], team_got.at[layer]),
        )

        def compute(m, start):
            here = pl.ds(start, 2 * rows)
            ffn_back_rows(everyone[here, :], v_normed, w_both, w_down, gated, d_both, here)
            split_pair(
                team, m, lambda c: right_trans(d_both[here, :], w_both[c, :]), sums, team.part
            )

        def between():
            if layer == 0:
                drain_ffn(1)

            def down_step(i, carry):
                here = pl.ds(pl.multiple_of(i * 256, 256), 256)
                down_part[here, :] = left_trans(gated[:, here], everyone[...]).astype(BF)
                return carry

            def both_step(i, carry):
                here = pl.ds(pl.multiple_of(i * 256, 256), 256)
                both_part[here, :] = left_trans(v_normed[:, here], d_both[...]).astype(BF)
                return carry

            lax.fori_loop(0, down_part.shape[0] // 256, down_step, 0)
            lax.fori_loop(0, width // 256, both_step, 0)
            if layer == 1:
                for copy in waiting[0][:3]:
                    copy.start()

        def early():
            for copy in copies[:3]:
                copy.wait()
            if layer == 0:
                share_ffn(1, d_both.at[pl.ds(0, 8 * share)])
                for piece in range(4):
                    attention_grads(piece)

        later = None
        if layer == 0:

            def later(m):
                for piece in range(4):
                    pl.when(m == piece)(lambda: send_x(1, piece))

        team.run(compute, between, d_middle, later, early)

        send_ffn(layer)
        copies[3].wait()

        def norm_step(i, carry):
            here = pl.ds(pl.multiple_of(i * chunk, 16), chunk)
            value = v_middle[here, :]
            back, gain_grad = norm_back(
                d_middle[here, :], value, inverse_rms(value), gain_rows[2 + layer : 3 + layer, :]
            )
            gain_sums[2 + layer : 3 + layer, :] += gain_grad[None]
            gradient = grad[here, :] + back
            d_middle[here, :] = gradient
            d_middle2[here, :] = gradient.astype(BF)
            return carry

        lax.fori_loop(0, rows // chunk, norm_step, 0)
        shared = [to_core(d_middle2.at[own], d_middle2.at[theirs], 4 * layer)]
        shared[0].start()
        for copy in copies[4:9]:
            copy.wait()

        for first in range(0, width, 256):
            columns = slice(first, first + 256)
            sums[2, :, columns] = right_trans(d_middle2[:rows, :], w_out[columns, :])

        def attention_step(i, carry):
            here = pl.ds(pl.multiple_of(i * small, small), small)
            d_attended = sums[2, here, :].astype(BF).astype(F32)
            q = v_qkv[here, :width].astype(F32)
            k = v_qkv[here, width : 2 * width].astype(F32)
            k0 = v_other[here, :width].astype(F32)
            mine, past = probabilities(q, k, k0, heads, where.place)
            d_mine = heads_summed(d_attended * v_qkv[here, 2 * width :].astype(F32), heads)
            d_past = heads_summed(d_attended * v_other[here, width:].astype(F32), heads)
            inner = mine * d_mine + past * d_past
            s_past = heads_spread(past * (d_past - inner) / math.sqrt(HD), heads)
            d_other[here, :width] = (s_past * q).astype(BF)
            d_other[here, width:] = (heads_spread(past, heads) * d_attended).astype(BF)
            s_mine = heads_spread(mine * (d_mine - inner) / math.sqrt(HD), heads)
            d_qkv2[here, :width] = (s_mine * k + s_past * k0).astype(BF)
            sums[0, here, :] = s_mine * q
            sums[1, here, :] = heads_spread(mine, heads) * d_attended
            return carry

        lax.fori_loop(0, rows // small, attention_step, 0)
        exchange = remote(
            d_other, y_in.at[layer], y_sent.at[layer], y_got.at[layer], where.index, 1 - where.place
        )
        exchange.start()

        def operand_step(i, carry):
            here = pl.ds(pl.multiple_of(i * chunk, 16), chunk)
            value = v_stream[here, :]
            value = value * inverse_rms(value) * gain_rows[layer : layer + 1, :]
            for number, item, target in (
                (0, value.astype(BF).astype(F32), normed2),
                (1, v_attended[here, :].astype(F32), attended2),
            ):
                for_core[number, here, :] = own_half(item, where.core, True).astype(BF)
                target[here, :] = own_half(item, where.core, False).astype(BF)
            return carry

        lax.fori_loop(0, rows // chunk, operand_step, 0)
        shared.append(to_core(for_core.at[0], normed2.at[theirs], 4 * layer + 1))
        shared.append(to_core(for_core.at[1], attended2.at[theirs], 4 * layer + 2))
        shared[1].start()
        shared[2].start()
        if layer == 0:
            finish_x(1)
        exchange.wait_recv()
        d_qkv2[:rows, width : 2 * width] = (
            sums[0] + y_in[layer, :, :width].astype(F32)
        ).astype(BF)
        d_qkv2[:rows, 2 * width :] = (sums[1] + y_in[layer, :, width:].astype(F32)).astype(BF)
        shared.append(to_core(d_qkv2.at[own], d_qkv2.at[theirs], 4 * layer + 3))
        shared[3].start()
        if layer == 0:
            for piece in range(4):
                wait_bytes(part.at[piece, pl.ds(0, 4 * share)], x_sent.at[4 + piece])
            for copy in shared:
                copy.wait_recv()
            for piece in range(4):
                attention_grads(piece)
                send_x(0, piece)
        copies[9].wait()
        for first in range(0, width, 256):
            columns = slice(first, first + 256)
            sums[2, :, columns] = right_trans(d_qkv2[:rows, :], w_qkv[columns, :])

        def stream_step(i, carry):
            here = pl.ds(pl.multiple_of(i * chunk, 16), chunk)
            value = v_stream[here, :]
            back, gain_grad = norm_back(
                sums[2, here, :], value, inverse_rms(value), gain_rows[layer : layer + 1, :]
            )
            gain_sums[layer : layer + 1, :] += gain_grad[None]
            gradient = d_middle[here, :] + back
            grad[here, :] = gradient
            rounded_to = rounded if layer == 1 else grad2
            rounded_to[here, :] = gradient.astype(BF)
            return carry

        lax.fori_loop(0, rows // chunk, stream_step, 0)
        for copy in shared:
            copy.wait_send()
        exchange.wait_send()
        if layer == 1:
            for copy in shared:
                copy.wait_recv()
            for copy in waiting[0][3:]:
                copy.start()

    grad_out = load(grad, input_grad, 14)
    grad_out.start()
    grad_copy = to_core(grad2.at[own], grad2.at[theirs], 9)
    grad_copy.start()
    index = where.index

    def gain_columns(device):
        return gain_sums.at[:, pl.ds(pl.multiple_of(device // 2 * 128, 128), 128)]

    def send_gain(step, carry):
        peer = lax.rem(index + step, 16)
        remote(gain_columns(peer), gain_got.at[index], g_sent.at[0], g_got.at[0], peer).start()
        return carry

    lax.fori_loop(1, 16, send_gain, 0)
    pltpu.make_async_copy(gain_columns(index), gain_got.at[index], g_got.at[0]).start()
    grad_copy.wait()
    codes_copy.wait()
    starting[1].wait()
    vocab = codes2.shape[1] // 8

    def table_step(i, carry):
        here = pl.ds(pl.multiple_of(i * 256, 256), 256)
        d_both[here, :] = left_trans(codes2[:, here], grad2[...]).astype(BF)
        return carry

    lax.fori_loop(0, 8 * vocab // 256, table_step, 0)
    table_in = everyone.at[pl.ds(16 * share, 4 * vocab)]
    for z in range(4):
        start = pl.multiple_of((z * 2 + 1 - where.x) * vocab, vocab)
        remote(
            d_both.at[pl.ds(start, vocab)],
            table_in.at[pl.ds(z * vocab, vocab)],
            x_sent.at[8],
            x_got.at[8],
            where.x_peer,
        ).start()
    share_ffn(0, d_both.at[pl.ds(8 * vocab, 8 * share)])
    finish_x(0)
    wait_bytes(table_in, x_got.at[8])
    for z in range(4):
        start = pl.multiple_of((z * 2 + where.x) * vocab, vocab)
        here = pl.ds(z * vocab, vocab)
        table_in[here, :] = (
            table_in[here, :].astype(F32) + d_both[pl.ds(start, vocab), :].astype(F32)
        ).astype(BF)
    send_z(table_in, table_got.at[where.z], 2, vocab)

    drain_ffn(0)
    for layer in (0, 1):
        wait_bytes(both_got.at[layer, pl.ds(0, 7)], f_got.at[3 * layer + 2])
        arrived, ends = f_got.at[3 * layer + 1], (index == 0) | (index == 15)
        pl.when(ends)(lambda: wait_bytes(down_got.at[layer, 0], arrived))
        pl.when(jnp.logical_not(ends))(lambda: wait_bytes(down_got.at[layer], arrived))
        wait_bytes(attn_got.at[layer], z_got.at[layer])
        wait_bytes(everyone.at[pl.ds(0, 12 * share)], z_sent.at[layer])
    for piece in range(4):
        wait_bytes(part.at[piece, pl.ds(0, 4 * share)], x_sent.at[piece])
    wait_bytes(table_got, z_got.at[2])
    wait_bytes(everyone.at[pl.ds(0, 3 * vocab)], z_sent.at[2])
    wait_bytes(d_both.at[pl.ds(0, 4 * vocab)], x_sent.at[8])
    grad_out.wait()
    wait_bytes(gain_got, g_got.at[0])
    wait_bytes(gain_got.at[pl.ds(0, 15)], g_sent.at[0])


def backward(
    cotangent, codes, codes_theirs, gain_rows, stream, middle, qkv, other, attended, normed, qkv0,
    qkv1, outs, both, down
):
    rows, width = cotangent.shape
    hidden = down.shape[1]
    share = width // 16
    vocab = codes.shape[1] // 8
    shape = jax.ShapeDtypeStruct
    hbm = pl.BlockSpec(memory_space=pl.ANY)
    vmem = pltpu.VMEM
    dma = pltpu.SemaphoreType.DMA
    return pl.pallas_call(
        backward_kernel,
        out_shape=(
            shape((rows, width), F32),
            shape((2, 8, share, 2 * hidden), BF),
            shape((2, 8 * share, 2 * hidden), BF),
            shape((2, 2, hidden // 2, width), BF),
            shape((2, 4, 4 * share, width), BF),
            shape((4, vocab, width), BF),
            shape((16, 8, 128), F32),
        ),
        in_specs=[hbm] * 3 + in_vmem(1) + [hbm] * 11,
        out_specs=tuple([hbm] * 7),
        scratch_shapes=[
            vmem((rows, width), F32),
            vmem((rows, width), F32),
            vmem((rows, 3 * width), BF),
            vmem((rows, 2 * width), BF),
            vmem((rows, width), BF),
            vmem((8 * rows, width), BF),
            vmem((width, 3 * width), BF),
            vmem((width, width), BF),
            vmem((width, 2 * hidden), BF),
            vmem((hidden, width), BF),
            vmem((rows, width), F32),
            vmem((rows, width), F32),
            vmem((rows, width), BF),
            vmem((2 * rows, width // 2), BF),
            vmem((2 * rows, width // 2), BF),
            vmem((2 * rows, 3 * width), BF),
            vmem((2 * rows, width), BF),
            vmem((2, rows, width // 2), BF),
            vmem((rows, 2 * width), BF),
            vmem((2, rows, 2 * width), BF),
            vmem((2 * rows, 8 * vocab), BF),
            vmem((2 * rows, width), BF),
            vmem((4, width // 2, width), BF),
            vmem((16 * share, width), BF),
            vmem((8 * rows, width), BF),
            vmem((8 * rows, hidden), BF),
            vmem((8 * rows, 2 * hidden), BF),
            vmem((4, rows, width), F32),
            vmem((width, 2 * hidden), BF),
            vmem((hidden, width), BF),
            vmem((8, width), F32),
            vmem((width, 128), BF),
            dma((15,)),
            dma((10,)),
            dma((10,)),
            dma((2,)),
            dma((2,)),
            dma((9,)),
            dma((9,)),
            dma((3,)),
            dma((3,)),
            dma((6,)),
            dma((6,)),
            dma((4,)),
            dma((1,)),
            dma((1,)),
        ]
        + Team.scratch(rows, width)[:8]
        + [dma((2, Team.SCRATCH_COPIES)), dma((2, Team.SCRATCH_COPIES))],
        compiler_params=pltpu.CompilerParams(
            collective_id=4, has_side_effects=True, vmem_limit_bytes=63 * 2**20
        ),
        name="backward_pass",
    )(
        cotangent,
        codes,
        codes_theirs,
        gain_rows,
        stream,
        middle,
        qkv,
        other,
        attended,
        normed,
        qkv0,
        qkv1,
        outs,
        both,
        down,
    )


def finish_kernel(both, down, attn, table, table_grad, qkv_grad, out_grad, gate_grad, up_grad, down_grad):
    hidden = both.shape[3] // 2
    share, width = both.shape[2], attn.shape[3]
    for layer in range(LAYERS):
        for member in range(8):
            columns = slice(member * hidden, (member + 1) * hidden)
            gate_grad[layer, 0, :, columns] = both[layer, member, :, :hidden].astype(F32)
            up_grad[layer, 0, :, columns] = both[layer, member, :, hidden:].astype(F32)
        down_grad[layer, 0] = down[layer, 0].astype(F32) + down[layer, 1].astype(F32)
        for piece in range(4):
            rows = slice(piece * share, (piece + 1) * share)
            value = sum(attn[layer, z, rows, :].astype(F32) for z in range(4))
            if piece < 3:
                qkv_grad[layer, 0, :, piece * width : (piece + 1) * width] = value
            else:
                out_grad[layer, 0] = value
    table_grad[0] = sum(table[z].astype(F32) for z in range(4))


def finish(both, down, attn, table):
    share, width = both.shape[2], attn.shape[3]
    hidden = both.shape[3] // 2
    shape = jax.ShapeDtypeStruct
    return pl.pallas_call(
        finish_kernel,
        out_shape=(
            shape((1,) + table.shape[1:], F32),
            shape((LAYERS, 1, share, 3 * width), F32),
            shape((LAYERS, 1, share, width), F32),
            shape((LAYERS, 1, share, 8 * hidden), F32),
            shape((LAYERS, 1, share, 8 * hidden), F32),
            shape((LAYERS, 1, hidden // 2, width), F32),
        ),
        in_specs=in_vmem(4),
        out_specs=tuple(in_vmem(6)),
        compiler_params=pltpu.CompilerParams(vmem_limit_bytes=48 * 2**20),
        name="finish",
    )(both, down, attn, table)


class Plan:
    def __init__(self, count):
        self.count = count
        self.team = 8
        self.teams = count // self.team
        self.across = [[g * self.team + t for g in range(self.teams)] for t in range(self.team)]

    def ffn_weights(self, gate, up, down):
        rows = gate.shape[0]
        both = jnp.stack([gate, up], axis=1).reshape(rows, 2, self.teams, self.team, -1)
        parts = both.transpose(3, 0, 1, 2, 4).reshape(self.team, rows, -1)
        parts = jnp.broadcast_to(parts[None], (self.teams,) + parts.shape)
        parts = parts.reshape((self.count,) + parts.shape[2:])
        mine = lax.all_to_all(parts, "frames", split_axis=0, concat_axis=0, tiled=True)
        return mine.reshape(self.count * rows, -1), self.gather_across(down)

    def gather_across(self, rows):
        if self.teams != 2:
            return lax.all_gather(rows, "frames", axis=0, tiled=True, axis_index_groups=self.across)
        theirs = lax.ppermute(rows, "frames", self.partners())
        first = lax.axis_index("frames") < self.team
        return jnp.concatenate([jnp.where(first, rows, theirs), jnp.where(first, theirs, rows)])

    def scatter_across(self, rows):
        if self.teams != 2:
            part = lax.psum_scatter(
                rows.astype(BF),
                "frames",
                scatter_dimension=0,
                tiled=True,
                axis_index_groups=self.across,
            )
            return part.astype(F32)
        half = rows.shape[0] // 2
        first = lax.axis_index("frames") < self.team
        mine = jnp.where(first, rows[:half], rows[half:])
        sent = jnp.where(first, rows[half:], rows[:half]).astype(BF)
        return mine + lax.ppermute(sent, "frames", self.partners()).astype(F32)

    def partners(self):
        return [(i, (i + self.team) % self.count) for i in range(self.count)]

    def ffn_grads(self, both_part, down_part):
        parts = both_part.astype(BF).reshape(self.count, -1, both_part.shape[1])
        parts = lax.all_to_all(parts, "frames", split_axis=0, concat_axis=0, tiled=True)
        rows = parts.shape[1]
        parts = parts.astype(F32).reshape(self.teams, self.team, rows, -1).sum(axis=0)
        down = self.scatter_across(down_part)
        parts = parts.reshape(self.team, rows, 2, self.teams, -1)
        both = parts.transpose(1, 2, 3, 0, 4).reshape(rows, 2, -1)
        return both[:, 0], both[:, 1], down


def attend(qkv, other):
    width = HEADS * HD
    position = lax.axis_index("pos")
    q, k, v = (qkv[:, i * width : (i + 1) * width].astype(F32) for i in range(3))
    k0, v0 = (other[:, i * width : (i + 1) * width].astype(F32) for i in range(2))
    own = head_sum(q * k) / math.sqrt(HD)
    past = jnp.where(position > 0, head_sum(q * k0) / math.sqrt(HD), -1e30)
    largest = jnp.maximum(own, past)
    own, past = jnp.exp(own - largest), jnp.exp(past - largest)
    total = own + past
    own, past = own / total, past / total
    attended = head_spread(own) * v + head_spread(past) * v0
    return attended.astype(BF), own, past


def attend_back(grad, qkv, other, own, past):
    width = HEADS * HD
    q, k, v = (qkv[:, i * width : (i + 1) * width].astype(F32) for i in range(3))
    k0, v0 = (other[:, i * width : (i + 1) * width].astype(F32) for i in range(2))
    grad = grad.astype(F32)
    d_own, d_past = head_sum(grad * v), head_sum(grad * v0)
    inner = own * d_own + past * d_past
    s_own = head_spread(own * (d_own - inner) / math.sqrt(HD))
    s_past = head_spread(past * (d_past - inner) / math.sqrt(HD))
    own, past = head_spread(own), head_spread(past)
    d_q = s_own * k + s_past * k0
    d_k = s_own * q
    d_v = own * grad
    d_other = jnp.concatenate([s_past * q, past * grad], axis=1)
    return d_q, d_k, d_v, d_other


def plain_forward(
    plan, onward, frames_in, onehot, code_table, w_qkv, w_out, w_gate, w_up, w_down, gain_attn, gain_ffn
):
    width = frames_in.shape[-1]
    gains = jnp.stack([gain_attn[0, 0], gain_attn[1, 0], gain_ffn[0, 0], gain_ffn[1, 0]], axis=1)
    gains = jnp.pad(gains, ((0, 0), (0, 124)))
    full_table = lax.all_gather(code_table[0], "frames", axis=0, tiled=True)
    first_qkv = lax.all_gather(
        jnp.concatenate([w_qkv[0, 0], gains], axis=1), "frames", axis=0, tiled=True
    )
    gain_rows = first_qkv[:, 3 * width : 3 * width + 4].astype(F32).T
    qkv_all = [first_qkv[:, : 3 * width], None]
    out_all = [lax.all_gather(w_out[0, 0], "frames", axis=0, tiled=True), None]
    ffn_all = [plan.ffn_weights(w_gate[0, 0], w_up[0, 0], w_down[0, 0]), None]
    qkv_all[1] = lax.all_gather(w_qkv[1, 0], "frames", axis=0, tiled=True)
    out_all[1] = lax.all_gather(w_out[1, 0], "frames", axis=0, tiled=True)
    ffn_all[1] = plan.ffn_weights(w_gate[1, 0], w_up[1, 0], w_down[1, 0])

    stream = frames_in[:, 0].astype(F32) + plain(onehot, full_table)
    kept = []
    for layer in range(LAYERS):
        inv_attn = inverse_rms(stream)
        normed_attn = (stream * inv_attn * gain_rows[layer]).astype(BF)
        qkv = plain(normed_attn, qkv_all[layer]).astype(BF)
        other = lax.ppermute(qkv[:, width:], "pos", onward)
        attended, own, past = attend(qkv, other)
        middle = stream + plain(attended, out_all[layer])
        inv_ffn = inverse_rms(middle)
        normed_ffn = (middle * inv_ffn * gain_rows[2 + layer]).astype(BF)
        both_all, down_all = ffn_all[layer]
        team_normed, summed = ffn_forward(normed_ffn, both_all, down_all)
        new_stream = middle + summed
        kept.append(
            (
                stream,
                inv_attn,
                normed_attn,
                qkv,
                other,
                own,
                past,
                attended,
                middle,
                inv_ffn,
                team_normed,
            )
        )
        stream = new_stream
    return kept, stream, gain_rows, qkv_all, out_all, ffn_all


def fused_body(
    onehot, frames_in, code_table, w_qkv, w_out, w_gate, w_up, w_down, gain_attn, gain_ffn, cotangent
):
    share = gain_attn.shape[-1]
    width = frames_in.shape[-1]
    gains = jnp.concatenate([gain_attn[:, 0], gain_ffn[:, 0]], axis=0).astype(F32)
    gains = jnp.pad(gains, ((0, 4), (0, share)))
    odd = lax.rem(lax.axis_index("frames"), 2) == 1
    gains = jnp.where(odd, jnp.roll(gains, share, axis=1), gains)
    act, *saved = forward(
        frames_in[:, 0],
        onehot,
        gains,
        code_table[0],
        w_qkv[:, 0],
        w_out[:, 0],
        w_gate[:, 0],
        w_up[:, 0],
        w_down[:, 0],
    )
    stream, middle, qkv, other, attended, normed, gain_rows, qkv0, qkv1, outs, both, down = saved
    blocks = onehot.reshape(onehot.shape[0], 8, 2, -1)
    first, second = (blocks[:, :, i].reshape(onehot.shape[0], -1) for i in (0, 1))
    codes, codes_theirs = jnp.where(odd, second, first), jnp.where(odd, first, second)
    input_grad, both_got, pair_got, down_got, attn_got, table_got, gain_got = backward(
        cotangent[:, 0],
        codes,
        codes_theirs,
        gain_rows,
        stream,
        middle,
        qkv,
        other,
        attended,
        normed,
        qkv0,
        qkv1,
        outs,
        both,
        down,
    )
    table, qkv_grad, out_grad, gate_grad, up_grad, down_grad = finish(
        both_got, down_got, attn_got, table_got
    )
    sums = gain_got.sum(axis=0)
    sums = jnp.where(odd, sums[:4, 64:], sums[:4, :64]).reshape(2, LAYERS, 1, share)
    return (
        act[:, None, :],
        input_grad[:, None, :],
        table,
        qkv_grad,
        out_grad,
        gate_grad,
        up_grad,
        down_grad,
        sums[0],
        sums[1],
    )


def body(
    frames_in,
    code_table,
    code_ids,
    delays,
    item_lengths,
    w_qkv,
    w_out,
    w_gate,
    w_up,
    w_down,
    gain_attn,
    gain_ffn,
    cotangent,
):
    count = lax.axis_size("frames")
    plan = Plan(count)
    positions = lax.axis_size("pos")
    onward = [(i, i + 1) for i in range(positions - 1)]
    backward = [(i + 1, i) for i in range(positions - 1)]
    local_frames = frames_in.shape[0]
    item_count = item_lengths.shape[0]
    width = frames_in.shape[-1]

    neighbours = [(i, i + 1) for i in range(count - 1)]
    earlier = lax.ppermute(code_ids[local_frames - 2 :], "frames", neighbours)
    extended = jnp.concatenate([earlier, code_ids], axis=0)[:, 0]
    global_frame = lax.axis_index("frames") * local_frames + jnp.arange(
        local_frames, dtype=jnp.int32
    )
    item_ends = jnp.cumsum(item_lengths)
    starts = item_ends - item_lengths
    item_index = jnp.sum((starts[None, :] <= global_frame[:, None]).astype(jnp.int32), axis=1) - 1
    chosen = item_index[:, None] == jnp.arange(item_count, dtype=jnp.int32)[None, :]
    item_begin = jnp.sum(jnp.where(chosen, starts[None, :], 0), axis=1)
    delay_rows = jnp.sum(jnp.where(chosen, delays[:, 0][None, :], 0), axis=1)
    one_back = extended[1 : local_frames + 1]
    two_back = extended[:local_frames]
    code_rows = jnp.where(delay_rows == 1, one_back, two_back)
    is_valid = global_frame - delay_rows >= item_begin
    vocab_size = code_table.shape[1] * count
    matches = code_rows[:, None] == jnp.arange(vocab_size, dtype=jnp.int32)[None, :]
    onehot = (matches & is_valid[:, None]).astype(BF)

    if count == 16:
        return fused_body(
            onehot, frames_in, code_table, w_qkv, w_out, w_gate, w_up, w_down, gain_attn, gain_ffn,
            cotangent,
        )
    kept, stream, gain_rows, qkv_all, out_all, ffn_all = plain_forward(
        plan, onward, frames_in, onehot, code_table, w_qkv, w_out, w_gate, w_up, w_down,
        gain_attn, gain_ffn,
    )
    output = stream.astype(BF)[:, None, :]

    gradient = cotangent[:, 0].astype(F32)
    collected = [None] * LAYERS
    gain_parts = [None] * (2 * LAYERS)
    for layer in reversed(range(LAYERS)):
        (
            stream,
            inv_attn,
            normed_attn,
            qkv,
            other,
            own,
            past,
            attended,
            middle,
            inv_ffn,
            team_normed,
        ) = kept[layer]
        both_all, down_all = ffn_all[layer]
        grad_normed, both_part, down_part = ffn_backward(
            gradient.astype(BF), both_all, down_all, team_normed
        )
        ffn_shares = plan.ffn_grads(both_part, down_part)
        grad_middle, gain_parts[2 + layer] = norm_back(
            grad_normed, middle, inv_ffn, gain_rows[2 + layer]
        )
        grad_middle = gradient + grad_middle
        grad_attn = grad_middle.astype(BF)
        grad_attended = right_trans(grad_attn, out_all[layer]).astype(BF)
        d_q, d_k, d_v, d_other = attend_back(grad_attended, qkv, other, own, past)
        arrived = lax.ppermute(d_other.astype(BF), "pos", backward).astype(F32)
        grad_qkv = jnp.concatenate([d_q, d_k + arrived[:, :width], d_v + arrived[:, width:]], axis=1)
        grad_qkv = grad_qkv.astype(BF)
        out_part = left_trans(attended, grad_attn).astype(BF)
        out_share = lax.psum_scatter(out_part, "frames", scatter_dimension=0, tiled=True)
        grad_normed_attn = right_trans(grad_qkv, qkv_all[layer])
        grad_stream, gain_parts[layer] = norm_back(
            grad_normed_attn, stream, inv_attn, gain_rows[layer]
        )
        gradient = grad_middle + grad_stream
        qkv_part = left_trans(normed_attn, grad_qkv).astype(BF)
        if layer == 0:
            tail = jnp.stack(gain_parts, axis=1).astype(BF)
            qkv_part = jnp.concatenate([qkv_part, jnp.pad(tail, ((0, 0), (0, 124)))], axis=1)
        qkv_share = lax.psum_scatter(qkv_part, "frames", scatter_dimension=0, tiled=True)
        collected[layer] = (qkv_share.astype(F32), out_share.astype(F32)) + ffn_shares
    table_part = left_trans(onehot, gradient.astype(BF)).astype(BF)
    table_share = lax.psum_scatter(table_part, "frames", scatter_dimension=0, tiled=True)
    gain_shares = collected[0][0][:, 3 * width : 3 * width + 4].T
    collected[0] = (collected[0][0][:, : 3 * width],) + collected[0][1:]
    stacked = [
        jnp.stack([collected[layer][slot] for layer in range(LAYERS)], axis=0)[:, None]
        for slot in range(5)
    ]
    return (
        output,
        gradient[:, None, :],
        table_share.astype(F32)[None],
        stacked[0],
        stacked[1],
        stacked[2],
        stacked[3],
        stacked[4],
        gain_shares[:2][:, None],
        gain_shares[2:][:, None],
    )


def solution(mesh):
    return jax.shard_map(
        body,
        mesh=mesh,
        in_specs=(
            P("frames", "pos", None),
            P("pos", "frames", None),
            P("frames", "pos"),
            P(None, "pos"),
            P(),
            P(None, "pos", "frames", None),
            P(None, "pos", "frames", None),
            P(None, "pos", "frames", None),
            P(None, "pos", "frames", None),
            P(None, "pos", "frames", None),
            P(None, "pos", "frames"),
            P(None, "pos", "frames"),
            P("frames", "pos", None),
        ),
        out_specs=(
            P("frames", "pos", None),
            P("frames", "pos", None),
            P("pos", "frames", None),
            P(None, "pos", "frames", None),
            P(None, "pos", "frames", None),
            P(None, "pos", "frames", None),
            P(None, "pos", "frames", None),
            P(None, "pos", "frames", None),
            P(None, "pos", "frames"),
            P(None, "pos", "frames"),
        ),
        check_vma=False,
    )
```

```python
import math

import jax
import jax.numpy as jnp
from jax import lax
from jax.experimental import pallas as pl
from jax.experimental.pallas import tpu as pltpu
from jax.sharding import PartitionSpec as P

HEADS = 16
HD = 64
LAYERS = 2
EPSILON = 1e-06
HIGHEST = lax.Precision.HIGHEST
BF = jnp.bfloat16
F32 = jnp.float32


def plain(left, right):
    return jnp.dot(left, right, preferred_element_type=F32)


def left_trans(left, right):
    return lax.dot_general(left, right, (((0,), (0,)), ((), ())), preferred_element_type=F32)


def right_trans(left, right):
    return lax.dot_general(left, right, (((1,), (1,)), ((), ())), preferred_element_type=F32)


def inverse_rms(stream):
    return lax.rsqrt(jnp.mean(stream * stream, axis=-1, keepdims=True) + EPSILON)


def norm_back(gradient, stream, inverse, gain_row):
    scaled = gradient * gain_row
    gain_grad = jnp.sum(gradient * stream * inverse, axis=0)
    inner_sum = jnp.mean(scaled * stream, axis=-1, keepdims=True)
    return (inverse * scaled - stream * inverse * inverse * inverse * inner_sum, gain_grad)


def head_matrix():
    rows = lax.broadcasted_iota(jnp.int32, (HEADS * HD, HEADS), 0) // HD
    cols = lax.broadcasted_iota(jnp.int32, (HEADS * HD, HEADS), 1)
    return (rows == cols).astype(F32)


def head_sum(values):
    return jnp.dot(values, head_matrix(), precision=HIGHEST)


def head_spread(values):
    return jnp.dot(values, head_matrix().T, precision=HIGHEST)


MESH = pl.DeviceIdType.MESH
VMEM_LIMIT = 60 * 2**20


def in_vmem(count):
    return [pl.BlockSpec(memory_space=pltpu.VMEM)] * count


class Team:
    SCRATCH_COPIES = 19

    def __init__(self, rows, mine, everyone, sums, scratch):
        (self.part, self.from_core, self.from_across, self.from_x, self.from_z) = scratch[:5]
        (self.to_x, self.to_z, self.to_across, self.sent, self.got) = scratch[5:10]
        self.rows, self.half = rows, rows // 2
        self.mine, self.everyone, self.sums = mine, everyone, sums
        index = lax.axis_index("frames")
        self.place = lax.axis_index("pos")
        member = lax.rem(index, 8)
        self.core = lax.rem(member, 2)
        self.x = lax.rem(member // 2, 2)
        self.z = member // 4
        self.core_peer = index + 1 - 2 * self.core
        self.x_peer = index + 2 - 4 * self.x
        self.z_peer = index + 4 - 8 * self.z

    @staticmethod
    def scratch(rows, width):
        half = rows // 2
        return [
            pltpu.VMEM((4, rows, width), BF),
            pltpu.VMEM((4, rows, width), BF),
            pltpu.VMEM((2, half, width), BF),
            pltpu.VMEM((rows, width), BF),
            pltpu.VMEM((rows, width), BF),
            pltpu.VMEM((rows, width), BF),
            pltpu.VMEM((rows, width), BF),
            pltpu.VMEM((rows, width), BF),
            pltpu.SemaphoreType.DMA((Team.SCRATCH_COPIES,)),
            pltpu.SemaphoreType.DMA((Team.SCRATCH_COPIES,)),
        ]

    def greet(self):
        barrier = pltpu.get_barrier_semaphore()
        for peer in (self.core_peer, self.x_peer, self.z_peer):
            pl.semaphore_signal(barrier, inc=1, device_id=(peer, self.place), device_id_type=MESH)
        pl.semaphore_wait(barrier, 3)

    def copy(self, number, source, target, peer):
        return pltpu.make_async_remote_copy(
            src_ref=source,
            dst_ref=target,
            send_sem=self.sent.at[number],
            recv_sem=self.got.at[number],
            device_id=(peer, self.place),
            device_id_type=MESH,
        )

    def pair_start(self, m):
        x = self.x + (m % 2) * (1 - 2 * self.x)
        z = self.z + (m // 2) * (1 - 2 * self.z)
        return pl.multiple_of((z * 2 + x) * (2 * self.rows), 2 * self.rows)

    def shard(self, m, part=None, core=None):
        core = self.core if core is None else core
        start = self.pair_start(m) + core * self.rows
        size = self.rows
        if part is not None:
            start, size = start + part * self.half, self.half
        return self.everyone.at[pl.ds(pl.multiple_of(start, 16), size)]

    def gather_copies(self):
        own = self.shard(0)
        x_rows, z_rows = self.shard(1), self.shard(2)
        x_low, z_high = self.shard(1, 1), self.shard(2, 0)
        high, low = self.shard(3, 0), self.shard(3, 1)
        return [
            self.copy(0, self.mine, own, self.core_peer),
            self.copy(1, self.mine, own, self.x_peer),
            self.copy(2, self.mine, own, self.z_peer),
            self.copy(3, x_rows, x_rows, self.core_peer),
            self.copy(4, x_low, x_low, self.z_peer),
            self.copy(5, z_rows, z_rows, self.core_peer),
            self.copy(6, z_high, z_high, self.x_peer),
            self.copy(7, high, high, self.core_peer),
            self.copy(8, low, low, self.core_peer),
        ]

    def arrived(self, number):
        other = 1 - self.core
        target = [
            self.shard(0, core=other),
            self.shard(1),
            self.shard(2),
            self.shard(1, core=other),
            self.shard(3, 1),
            self.shard(2, core=other),
            self.shard(3, 0),
            self.shard(3, 0, core=other),
            self.shard(3, 1, core=other),
        ][number]
        self.copy(number, target, target, self.core_peer).wait_recv()

    def sum_copies(self):
        half = self.half
        high, low = pl.ds(0, half), pl.ds(half, half)
        copies = [
            self.copy(9 + m, self.part.at[m], self.from_core.at[m], self.core_peer)
            for m in range(4)
        ]
        copies += [
            self.copy(13, self.to_across.at[high], self.from_across.at[0], self.x_peer),
            self.copy(14, self.to_across.at[low], self.from_across.at[1], self.z_peer),
            self.copy(15, self.to_x.at[high], self.from_x.at[high], self.x_peer),
            self.copy(16, self.to_x.at[low], self.from_x.at[low], self.x_peer),
            self.copy(17, self.to_z.at[low], self.from_z.at[low], self.z_peer),
            self.copy(18, self.to_z.at[high], self.from_z.at[high], self.z_peer),
        ]
        return copies

    def run(self, compute, between, result, later=None, early=None):
        half, rows = self.half, self.rows
        gather = self.gather_copies()
        adds = self.sum_copies()
        for copy in gather[:3]:
            copy.start()
        start = self.pair_start(0) + self.core * rows
        self.everyone[pl.ds(pl.multiple_of(start, 16), rows), :] = self.mine[...]
        if early is not None:
            early()

        def total(m, first):
            return self.sums[m, first : first + half, :] + self.from_core[
                m, first : first + half, :
            ].astype(F32)

        def step(m, carry):
            @pl.when(m == 0)
            def _():
                self.arrived(0)

            @pl.when(m == 1)
            def _():
                self.arrived(1)
                gather[4].start()
                gather[3].start()
                self.arrived(2)
                gather[6].start()
                gather[5].start()
                self.arrived(3)

            @pl.when(m == 2)
            def _():
                self.arrived(5)

            @pl.when(m == 3)
            def _():
                self.arrived(6)
                gather[7].start()
                self.arrived(4)
                gather[8].start()
                self.arrived(7)
                self.arrived(8)

            compute(m, self.pair_start(m))
            self.copy(9 + m, self.part.at[m], self.from_core.at[m], self.core_peer).start()
            if later is not None:
                later(m)

            @pl.when(m == 2)
            def _():
                adds[1].wait_recv()
                self.to_x[:half, :] = total(1, 0).astype(BF)
                adds[6].start()

            return carry

        lax.fori_loop(0, 4, step, 0)
        adds[3].wait_recv()
        self.to_across[:half, :] = total(3, 0).astype(BF)
        adds[4].start()
        self.to_across[half:, :] = total(3, half).astype(BF)
        adds[5].start()
        adds[2].wait_recv()
        self.to_z[half:, :] = total(2, half).astype(BF)
        adds[8].start()
        between()
        for copy in gather:
            copy.wait_send()
        adds[5].wait_recv()
        self.to_x[half:, :] = (total(1, half) + self.from_across[1].astype(F32)).astype(BF)
        adds[7].start()
        adds[4].wait_recv()
        self.to_z[:half, :] = (total(2, 0) + self.from_across[0].astype(F32)).astype(BF)
        adds[9].start()
        adds[0].wait_recv()
        for number in (6, 7, 8, 9):
            adds[number].wait_recv()
        for first in (0, half):
            rows_here = slice(first, first + half)
            result[rows_here, :] = (
                total(0, first)
                + self.from_x[rows_here, :].astype(F32)
                + self.from_z[rows_here, :].astype(F32)
            )
        for copy in adds:
            copy.wait_send()


def split_pair(team, m, product, sums, part):
    rows = team.rows
    for first in range(0, sums.shape[2], 256):
        columns = slice(first, first + 256)
        value = product(columns)
        low, high = value[:rows], value[rows:]
        sums[m, :, columns] = jnp.where(team.core == 0, low, high)
        part[m, :, columns] = jnp.where(team.core == 0, high, low).astype(BF)


def hidden_units(block, both, hidden, first):
    gate = plain(block, both[:, first : first + 256])
    return gate, plain(block, both[:, hidden + first : hidden + first + 256])


def ffn_rows(block, both, down):
    hidden = down.shape[0]
    parts = []
    for first in range(0, hidden, 256):
        gate, up = hidden_units(block, both, hidden, first)
        parts.append((gate * jax.nn.sigmoid(gate) * up).astype(BF))
    gated = jnp.concatenate(parts, axis=1)
    return lambda columns: plain(gated, down[:, columns])


def ffn_forward_kernel(normed, both, down, everyone, result, sums, *scratch):
    rows = normed.shape[0]
    team = Team(rows, normed, everyone, sums, scratch)
    team.greet()

    def compute(m, start):
        block = everyone[pl.ds(start, 2 * rows), :]
        split_pair(team, m, ffn_rows(block, both, down), sums, team.part)

    team.run(compute, lambda: None, result)


def ffn_back_rows(block, normed, both, down, gated, d_both, here):
    hidden = down.shape[0]
    before = normed[here, :]
    for first in range(0, hidden, 256):
        columns = slice(first, first + 256)
        gate, up = hidden_units(before, both, hidden, first)
        d_gated = right_trans(block, down[columns, :])
        sig = jax.nn.sigmoid(gate)
        act = gate * sig
        gated[here, columns] = (act * up).astype(BF)
        d_both[here, columns] = (d_gated * up * sig * (1.0 + gate * (1.0 - sig))).astype(BF)
        d_both[here, hidden + first : hidden + first + 256] = (d_gated * act).astype(BF)


def ffn_backward_kernel(
    grad, both, down, normed, result, both_part, down_part, everyone, gated, d_both, sums, *scratch
):
    rows = grad.shape[0]
    team = Team(rows, grad, everyone, sums, scratch)
    team.greet()

    def compute(m, start):
        here = pl.ds(start, 2 * rows)
        ffn_back_rows(everyone[here, :], normed, both, down, gated, d_both, here)
        split_pair(team, m, lambda c: right_trans(d_both[here, :], both[c, :]), sums, team.part)

    def between():
        def down_step(i, carry):
            cols = pl.ds(pl.multiple_of(i * 256, 256), 256)
            down_part[:, cols] = left_trans(gated[...], everyone[:, cols])
            return carry

        def both_step(i, carry):
            cols = pl.ds(pl.multiple_of(i * 256, 256), 256)
            both_part[:, cols] = left_trans(normed[...], d_both[:, cols]).astype(BF)
            return carry

        lax.fori_loop(0, down_part.shape[1] // 256, down_step, 0)
        lax.fori_loop(0, both_part.shape[1] // 256, both_step, 0)

    team.run(compute, between, result)


def ffn_forward(normed, both, down):
    rows, width = normed.shape
    return pl.pallas_call(
        ffn_forward_kernel,
        out_shape=(
            jax.ShapeDtypeStruct((8 * rows, width), BF),
            jax.ShapeDtypeStruct((rows, width), F32),
        ),
        in_specs=in_vmem(3),
        out_specs=in_vmem(2),
        scratch_shapes=[pltpu.VMEM((4, rows, width), F32)] + Team.scratch(rows, width),
        compiler_params=pltpu.CompilerParams(
            collective_id=1, has_side_effects=True, vmem_limit_bytes=VMEM_LIMIT
        ),
        name="ffn_forward",
    )(normed, both, down)


def ffn_backward(grad, both, down, normed):
    rows, width = grad.shape
    hidden = down.shape[0]
    return pl.pallas_call(
        ffn_backward_kernel,
        out_shape=(
            jax.ShapeDtypeStruct((rows, width), F32),
            jax.ShapeDtypeStruct((width, 2 * hidden), BF),
            jax.ShapeDtypeStruct((hidden, width), F32),
        ),
        in_specs=in_vmem(4),
        out_specs=in_vmem(3),
        scratch_shapes=[
            pltpu.VMEM((8 * rows, width), BF),
            pltpu.VMEM((8 * rows, hidden), BF),
            pltpu.VMEM((8 * rows, 2 * hidden), BF),
            pltpu.VMEM((4, rows, width), F32),
        ]
        + Team.scratch(rows, width),
        compiler_params=pltpu.CompilerParams(
            collective_id=2, has_side_effects=True, vmem_limit_bytes=VMEM_LIMIT
        ),
        name="ffn_backward",
    )(grad, both, down, normed)


class Place:
    def __init__(self):
        self.index = lax.axis_index("frames")
        self.place = lax.axis_index("pos")
        self.core = lax.rem(self.index, 2)
        self.x = lax.rem(self.index // 2, 2)
        self.z = self.index // 4
        self.core_peer = self.index + 1 - 2 * self.core
        self.x_peer = self.index + 2 - 4 * self.x

    def greet_all(self):
        barrier = pltpu.get_barrier_semaphore()

        def signal(step, carry):
            peer = lax.rem(self.index + step, 16)
            pl.semaphore_signal(barrier, inc=1, device_id=(peer, self.place), device_id_type=MESH)
            return carry

        lax.fori_loop(1, 16, signal, 0)
        pl.semaphore_signal(
            barrier, inc=1, device_id=(self.index, 1 - self.place), device_id_type=MESH
        )
        pl.semaphore_wait(barrier, 16)


class Gather:
    def __init__(self, where, number, source, full, sent, got):
        self.where, self.source, self.full = where, source, full
        self.sent, self.got = sent.at[number], got.at[number]
        self.rows = source.shape[0]

    def shard(self, z, x, core):
        start = (z * 4 + x * 2 + core) * self.rows
        return self.full.at[pl.ds(pl.multiple_of(start, self.rows), self.rows)]

    def copy(self, source, target, sent, got, peer):
        return pltpu.make_async_remote_copy(
            src_ref=source,
            dst_ref=target,
            send_sem=self.sent.at[sent],
            recv_sem=self.got.at[got],
            device_id=(peer, self.where.place),
            device_id_type=MESH,
        )

    def z_copy(self, z, up, own=False):
        w = self.where
        target = self.shard(z, w.x, w.core)
        source = self.source if own else target
        if up:
            return self.copy(source, target, z, z, jnp.minimum(w.index + 4, 15))
        return self.copy(source, target, 4 + z, z, jnp.maximum(w.index - 4, 0))

    def x_copy(self, z, own=False):
        w = self.where
        target = self.shard(z, w.x, w.core)
        return self.copy(self.source if own else target, target, 8 + z, 4 + z, w.x_peer)

    def core_copy(self, z, other_x, own=False):
        w = self.where
        x = 1 - w.x if other_x else w.x
        target = self.shard(z, x, w.core)
        number = z * 2 + other_x
        return self.copy(
            self.source if own else target, target, 12 + number, 8 + number, w.core_peer
        )

    def local(self):
        w = self.where
        return pltpu.make_async_copy(
            self.source, self.shard(w.z, w.x, w.core), self.got.at[w.z]
        )

    def start(self):
        w = self.where
        pl.when(w.z < 3)(lambda: self.z_copy(w.z, True, True).start())
        pl.when(w.z > 0)(lambda: self.z_copy(w.z, False, True).start())
        self.x_copy(w.z, True).start()
        self.core_copy(w.z, 0, True).start()
        self.local().start()

    def pass_z(self, distance):
        w = self.where

        @pl.when(w.z >= distance)
        def _():
            z = w.z - distance
            self.z_copy(z, True).wait_recv()
            pl.when(w.z < 3)(lambda: self.z_copy(z, True).start())
            self.x_copy(z).start()
            self.core_copy(z, 0).start()

        @pl.when(w.z + distance <= 3)
        def _():
            z = w.z + distance
            self.z_copy(z, False).wait_recv()
            pl.when(w.z > 0)(lambda: self.z_copy(z, False).start())
            self.x_copy(z).start()
            self.core_copy(z, 0).start()

    def pass_x(self):
        w = self.where

        def hand(z):
            target = self.shard(z, 1 - w.x, w.core)
            self.copy(target, target, 8 + z, 4 + z, w.x_peer).wait_recv()
            self.core_copy(z, 1).start()

        hand(w.z)
        for distance in (1, 2, 3):
            pl.when(w.z >= distance)(lambda: hand(w.z - distance))
            pl.when(w.z + distance <= 3)(lambda: hand(w.z + distance))

    def finish(self):
        w = self.where
        for z in range(4):
            for other_x in (0, 1):
                x = 1 - w.x if other_x else w.x
                target = self.shard(z, x, 1 - w.core)
                number = z * 2 + other_x
                self.copy(target, target, 12 + number, 8 + number, w.core_peer).wait_recv()
        self.local().wait()

    def drain(self):
        w = self.where
        for z in range(4):
            pl.when((z <= w.z) & (w.z < 3))(lambda: self.z_copy(z, True).wait_send())
            pl.when((z >= w.z) & (w.z > 0))(lambda: self.z_copy(z, False).wait_send())
            self.x_copy(z).wait_send()
            self.core_copy(z, 0).wait_send()
            self.core_copy(z, 1).wait_send()


class Slices:
    def __init__(self, where, layer, gate, up, down, both, down_all, sent, got):
        self.where, self.both, self.down_all = where, both.at[layer], down_all.at[layer]
        self.gate, self.up, self.down = gate.at[layer], up.at[layer], down.at[layer]
        self.sent, self.got = sent.at[layer], got.at[layer]
        self.rows = self.gate.shape[0]
        self.hidden = self.down_all.shape[0]

    def piece(self, source, side, member):
        here = pl.ds(pl.multiple_of(self.where.index * self.rows, self.rows), self.rows)
        columns = pl.ds(pl.multiple_of(member * self.hidden, self.hidden), self.hidden)
        return source.at[:, columns], self.both.at[
            here, side * self.hidden : (side + 1) * self.hidden
        ]

    def remote(self, source, target, number, peer):
        return pltpu.make_async_remote_copy(
            src_ref=source,
            dst_ref=target,
            send_sem=self.sent.at[number],
            recv_sem=self.got.at[number],
            device_id=(peer, self.where.place),
            device_id_type=MESH,
        )

    def down_target(self):
        half = self.hidden // 2
        start = lax.rem(self.where.index, 2) * half
        return self.down_all.at[pl.ds(pl.multiple_of(start, half), half)]

    def start(self):
        index = self.where.index
        base = index - lax.rem(index, 8)

        def send(step, carry):
            member = lax.rem(index + step, 8)
            for side, source in ((0, self.gate), (1, self.up)):
                part, target = self.piece(source, side, member)
                self.remote(part, target, 0, base + member).start()
            return carry

        lax.fori_loop(1, 8, send, 0)
        for side, source in ((0, self.gate), (1, self.up)):
            part, target = self.piece(source, side, lax.rem(index, 8))
            pltpu.make_async_copy(part, target, self.got.at[0]).start()
        for team in (0, 1):
            peer = team * 8 + index // 2

            @pl.when(peer != index)
            def _():
                self.remote(self.down, self.down_target(), 1, peer).start()

            @pl.when(peer == index)
            def _():
                pltpu.make_async_copy(self.down, self.down_target(), self.got.at[1]).start()

    def team_rows(self, team):
        size = 8 * self.rows
        return self.both.at[pl.ds(pl.multiple_of(team * size, size), size)]

    def swap(self):
        mine = self.team_rows(self.where.index // 8)
        return self.remote(mine, mine, 2, lax.rem(self.where.index + 8, 16))

    def pass_on(self):
        mine = self.team_rows(self.where.index // 8)
        pltpu.make_async_copy(mine, mine, self.got.at[0]).wait()
        self.swap().start()

    def finish(self):
        theirs = self.team_rows(1 - self.where.index // 8)
        pltpu.make_async_copy(theirs, theirs, self.got.at[2]).wait()
        pltpu.make_async_copy(self.down_all, self.down_all, self.got.at[1]).wait()

    def drain(self):
        index = self.where.index
        most = self.both.at[pl.ds(0, 7 * self.rows)]
        pltpu.make_async_copy(most, most, self.sent.at[0]).wait()
        self.swap().wait_send()
        ends = (index == 0) | (index == 15)
        half = self.down_all.at[pl.ds(0, self.hidden // 2)]

        @pl.when(ends)
        def _():
            pltpu.make_async_copy(half, half, self.sent.at[1]).wait()

        @pl.when(jnp.logical_not(ends))
        def _():
            pltpu.make_async_copy(self.down_all, self.down_all, self.sent.at[1]).wait()


def two_parts(values):
    high = values.astype(BF)
    return high, (values - high.astype(F32)).astype(BF)


def heads_summed(values, heads):
    high, low = two_parts(values)
    return plain(high, heads[...]) + plain(low, heads[...])


def heads_spread(values, heads):
    high, low = two_parts(values)
    return right_trans(high, heads[...]) + right_trans(low, heads[...])


def fill_heads(heads):
    rows = lax.broadcasted_iota(jnp.int32, heads.shape, 0) // HD
    columns = lax.broadcasted_iota(jnp.int32, heads.shape, 1)
    heads[...] = jnp.where(rows == columns, 1.0, 0.0).astype(BF)


def probabilities(q, k, k0, heads, place):
    own = heads_summed(q * k, heads) / math.sqrt(HD)
    past = jnp.where(place > 0, heads_summed(q * k0, heads) / math.sqrt(HD), -1e30)
    largest = jnp.maximum(own, past)
    own, past = jnp.exp(own - largest), jnp.exp(past - largest)
    total = own + past
    return own / total, past / total


def forward_kernel(
    frames, onehot, gain_shard, table, qkv0, qkv1, out0, out1, gate, up, down, *refs
):
    (act, stream, middle, qkv, other, attended, everyone, gain_rows) = refs[:8]
    (qkv0_out, qkv1_out, outs_out, both_out, down_out) = refs[8:13]
    (gains, table_all, qkv0_all, qkv1_all, outs_all, both, down_all) = refs[13:20]
    (heads, normed, result, sums, gather_sent, gather_got, slice_sent, slice_got) = refs[20:28]
    (y_sent, y_got, saved) = refs[28:31]
    team_scratch = refs[31:39]
    team_sent, team_got = refs[39:41]
    rows, width = frames.shape
    where = Place()

    def gather(number, source, full):
        return Gather(where, number, source, full, gather_sent, gather_got)

    gain_gather = gather(0, gain_shard, gains)
    table_gather = gather(1, table, table_all)
    qkv_gathers = [gather(2, qkv0, qkv0_all), gather(3, qkv1, qkv1_all)]
    out_gathers = [gather(4, out0, outs_all.at[0]), gather(5, out1, outs_all.at[1])]
    slices = [
        Slices(where, layer, gate, up, down, both, down_all, slice_sent, slice_got)
        for layer in range(LAYERS)
    ]
    where.greet_all()
    for item in (gain_gather, table_gather, qkv_gathers[0], out_gathers[0]):
        item.start()
    slices[0].start()
    fill_heads(heads)
    first = (gain_gather, table_gather, qkv_gathers[0], out_gathers[0])
    for item in first:
        for distance in (1, 2, 3):
            item.pass_z(distance)
    slices[0].pass_on()
    for item in first:
        item.pass_x()
    gain_gather.finish()
    for block in range(8):
        first, second = block * 16, block * 16 + 8
        gain_rows[:, block * 128 : (block + 1) * 128] = (
            gains[first : first + 8, :] + gains[second : second + 8, :]
        )
    table_gather.finish()
    for first in range(0, width, 256):
        columns = slice(first, first + 256)
        stream[0, :, columns] = frames[:, columns].astype(F32) + plain(
            onehot[...], table_all[:, columns]
        )
    saves = []
    second = (qkv_gathers[1], out_gathers[1])

    def save(source, target, number):
        copy = pltpu.make_async_copy(source, target, saved.at[number])
        copy.start()
        saves.append(copy)

    for layer in range(LAYERS):
        value = stream[layer]
        normed[...] = (value * inverse_rms(value) * gain_rows[layer : layer + 1, :]).astype(BF)
        qkv_gathers[layer].finish()
        weights = (qkv0_all, qkv1_all)[layer]
        if layer == 0:
            for item in second:
                item.start()
        save(weights, (qkv0_out, qkv1_out)[layer], layer)
        exchange = pltpu.make_async_remote_copy(
            src_ref=qkv.at[layer, :, pl.ds(width, 2 * width)],
            dst_ref=other.at[layer],
            send_sem=y_sent.at[layer],
            recv_sem=y_got.at[layer],
            device_id=(where.index, 1 - where.place),
            device_id_type=MESH,
        )
        for first in list(range(width, 3 * width, 512)) + list(range(0, width, 512)):
            if first == 0:
                exchange.start()
            columns = slice(first, first + 512)
            qkv[layer, :, columns] = plain(normed[...], weights[:, columns]).astype(BF)
        if layer == 0:
            slices[1].start()
        exchange.wait_recv()
        q = qkv[layer, :, :width].astype(F32)
        k = qkv[layer, :, width : 2 * width].astype(F32)
        k0 = other[layer, :, :width].astype(F32)
        own, past = probabilities(q, k, k0, heads, where.place)
        attended[layer] = (
            heads_spread(own, heads) * qkv[layer, :, 2 * width :].astype(F32)
            + heads_spread(past, heads) * other[layer, :, width:].astype(F32)
        ).astype(BF)
        out_gathers[layer].finish()
        for first in range(0, width, 512):
            columns = slice(first, first + 512)
            middle[layer, :, columns] = stream[layer, :, columns] + plain(
                attended[layer], outs_all[layer, :, columns]
            )
        value = middle[layer]
        normed[...] = (value * inverse_rms(value) * gain_rows[2 + layer : 3 + layer, :]).astype(BF)
        if layer == 0:
            for item in second:
                item.pass_z(1)
        slices[layer].finish()
        save(both.at[layer], both_out.at[layer], 2 + layer)
        save(down_all.at[layer], down_out.at[layer], 4 + layer)
        team = Team(
            rows,
            normed,
            everyone.at[layer],
            sums,
            tuple(team_scratch) + (team_sent.at[layer], team_got.at[layer]),
        )

        def compute(m, start):
            block = everyone[layer, pl.ds(start, 2 * rows), :]
            rows_out = ffn_rows(block, both.at[layer], down_all.at[layer])
            split_pair(team, m, rows_out, sums, team.part)

        later = None
        if layer == 0:

            def later(m):
                pl.when(m == 1)(lambda: slices[1].pass_on())
                for step in (2, 3):

                    @pl.when(m == step)
                    def _():
                        for item in second:
                            item.pass_z(step)

        def between():
            if layer == 0:
                for item in second:
                    item.pass_x()

        team.run(compute, lambda: None, result, later)
        between()
        if layer == 0:
            stream[1] = middle[0] + result[...]
        else:
            act[...] = (middle[1] + result[...]).astype(BF)
        exchange.wait_send()
    save(outs_all, outs_out, 6)
    for item in [gain_gather, table_gather] + qkv_gathers + out_gathers + slices:
        item.drain()
    for copy in saves:
        copy.wait()


def forward(frames, onehot, gain_shard, table, w_qkv, w_out, gate, up, down):
    rows, width = frames.shape
    hidden = gate.shape[2] // 8
    vocab = table.shape[0] * 16
    shape = jax.ShapeDtypeStruct
    hbm = pl.BlockSpec(memory_space=pl.ANY)
    return pl.pallas_call(
        forward_kernel,
        out_shape=(
            shape((rows, width), BF),
            shape((2, rows, width), F32),
            shape((2, rows, width), F32),
            shape((2, rows, 3 * width), BF),
            shape((2, rows, 2 * width), BF),
            shape((2, rows, width), BF),
            shape((2, 8 * rows, width), BF),
            shape((8, width), F32),
            shape((width, 3 * width), BF),
            shape((width, 3 * width), BF),
            shape((2, width, width), BF),
            shape((2, width, 2 * hidden), BF),
            shape((2, hidden, width), BF),
        ),
        in_specs=in_vmem(2) + [hbm] * 9,
        out_specs=tuple(in_vmem(8) + [hbm] * 5),
        scratch_shapes=[
            pltpu.VMEM((8 * 16, 128), F32),
            pltpu.VMEM((vocab, width), BF),
            pltpu.VMEM((width, 3 * width), BF),
            pltpu.VMEM((width, 3 * width), BF),
            pltpu.VMEM((2, width, width), BF),
            pltpu.VMEM((2, width, 2 * hidden), BF),
            pltpu.VMEM((2, hidden, width), BF),
            pltpu.VMEM((width, 128), BF),
            pltpu.VMEM((rows, width), BF),
            pltpu.VMEM((rows, width), F32),
            pltpu.VMEM((4, rows, width), F32),
            pltpu.SemaphoreType.DMA((6, 20)),
            pltpu.SemaphoreType.DMA((6, 16)),
            pltpu.SemaphoreType.DMA((2, 3)),
            pltpu.SemaphoreType.DMA((2, 3)),
            pltpu.SemaphoreType.DMA((2,)),
            pltpu.SemaphoreType.DMA((2,)),
            pltpu.SemaphoreType.DMA((7,)),
        ]
        + Team.scratch(rows, width)[:8]
        + [
            pltpu.SemaphoreType.DMA((2, Team.SCRATCH_COPIES)),
            pltpu.SemaphoreType.DMA((2, Team.SCRATCH_COPIES)),
        ],
        compiler_params=pltpu.CompilerParams(
            collective_id=3, has_side_effects=True, vmem_limit_bytes=63 * 2**20
        ),
        name="forward_pass",
    )(
        frames,
        onehot,
        gain_shard,
        table,
        w_qkv[0],
        w_qkv[1],
        w_out[0],
        w_out[1],
        gate,
        up,
        down,
    )


def own_half(values, core, other):
    rows, width = values.shape
    parts = []
    for first in range(0, width, 256):
        low, high = values[:, first : first + 128], values[:, first + 128 : first + 256]
        lane = lax.broadcasted_iota(jnp.int32, low.shape, 1)
        even = jnp.where(lane < 64, low, pltpu.roll(high, 64, 1))
        odd = jnp.where(lane < 64, pltpu.roll(low, 64, 1), high)
        first_core = (core == 0) != other
        parts.append(jnp.where(first_core, even, odd))
    return jnp.concatenate(parts, axis=1)


def backward_kernel(
    cotangent, codes, codes_theirs, gain_rows, stream, middle, qkv, other, attended, normed, qkv0,
    qkv1, outs, both, down, *refs
):
    (input_grad, both_got, pair_got, down_got, attn_got, table_got, gain_got) = refs[:7]
    refs = refs[1:]
    (v_stream, v_middle, v_qkv, v_other, v_attended, v_normed, w_qkv, w_out, w_both, w_down) = refs[
        6:16
    ]
    (grad, d_middle, rounded, normed2, attended2, d_qkv2, d_middle2, for_core, d_other, y_in) = refs[
        16:26
    ]
    (codes2, grad2, part, from_x, everyone, gated, d_both, sums, both_part, down_part) = refs[26:36]
    (gain_sums, heads, loaded, core_sent, core_got, y_sent, y_got, x_sent, x_got) = refs[36:45]
    (z_sent, z_got, f_sent, f_got, f_kept, g_sent, g_got) = refs[45:52]
    team_scratch = refs[52:60]
    team_sent, team_got = refs[60:62]
    rows, width = cotangent.shape
    share = both_part.shape[0] // 16
    where = Place()
    own, theirs = pl.ds(0, rows), pl.ds(rows, rows)
    chunk, small = rows // 2, 32

    def load(source, target, number):
        return pltpu.make_async_copy(source, target, loaded.at[number])

    def loads_of(layer):
        return [
            load(normed.at[layer], v_normed, 0),
            load(both.at[layer], w_both, 1),
            load(down.at[layer], w_down, 2),
            load(middle.at[layer], v_middle, 3),
            load(outs.at[layer], w_out, 4),
            load(qkv.at[layer], v_qkv, 5),
            load(other.at[layer], v_other, 6),
            load(stream.at[layer], v_stream, 7),
            load(attended.at[layer], v_attended, 8),
            load((qkv0, qkv1)[layer], w_qkv, 9),
        ]

    def remote(source, target, sent, got, peer, place=None):
        return pltpu.make_async_remote_copy(
            src_ref=source,
            dst_ref=target,
            send_sem=sent,
            recv_sem=got,
            device_id=(peer, where.place if place is None else place),
            device_id_type=MESH,
        )

    def wait_bytes(like, semaphore):
        pltpu.make_async_copy(like, like, semaphore).wait()

    def to_core(source, target, number):
        return remote(source, target, core_sent.at[number], core_got.at[number], where.core_peer)

    def team_rows(ref, team):
        return ref.at[pl.ds(pl.multiple_of(team * 8 * share, 8 * share), 8 * share)]

    def swap(layer):
        team = where.index // 8
        return remote(
            team_rows(both_part, 1 - team),
            pair_got.at[layer],
            f_sent.at[3 * layer],
            f_got.at[3 * layer],
            lax.rem(where.index + 8, 16),
        )

    def share_ffn(layer, spare):
        index = where.index
        team, member = index // 8, lax.rem(index, 8)
        swap(layer).wait_recv()
        fetch = load(pair_got.at[layer], spare, 12 + layer)
        fetch.start()
        fetch.wait()
        start = pl.multiple_of(team * 8 * share, 8 * share)

        def add(i, carry):
            first = pl.multiple_of(i * 32, 32)
            here = pl.ds(pl.multiple_of(start + first, 32), 32)
            both_part[here, :] = (
                both_part[here, :].astype(F32) + spare[pl.ds(first, 32), :].astype(F32)
            ).astype(BF)
            return carry

        lax.fori_loop(0, 8 * share // 32, add, 0)

        def piece(owner):
            first = pl.multiple_of(start + owner * share, share)
            return both_part.at[pl.ds(first, share)]

        def send(step, carry):
            owner = lax.rem(member + step, 8)
            remote(
                piece(owner),
                both_got.at[layer, member],
                f_sent.at[3 * layer + 2],
                f_got.at[3 * layer + 2],
                team * 8 + owner,
            ).start()
            return carry

        lax.fori_loop(1, 8, send, 0)
        pltpu.make_async_copy(
            piece(member), both_got.at[layer, member], f_kept.at[2 * layer]
        ).start()

    def send_ffn(layer):
        index = where.index
        swap(layer).start()
        half = down_part.shape[0] // 2
        for side in (0, 1):
            owner = 2 * lax.rem(index, 8) + side
            piece = down_part.at[pl.ds(side * half, half)]
            target = down_got.at[layer, index // 8]

            @pl.when(owner != index)
            def _():
                remote(
                    piece, target, f_sent.at[3 * layer + 1], f_got.at[3 * layer + 1], owner
                ).start()

            @pl.when(owner == index)
            def _():
                pltpu.make_async_copy(piece, target, f_kept.at[2 * layer + 1]).start()

    def drain_ffn(layer):
        index = where.index
        swap(layer).wait_send()
        wait_bytes(both_part.at[pl.ds(0, 7 * share)], f_sent.at[3 * layer + 2])
        wait_bytes(both_part.at[pl.ds(0, share)], f_kept.at[2 * layer])
        ends = (index == 0) | (index == 15)
        half = down_part.shape[0] // 2
        semaphore = f_sent.at[3 * layer + 1]

        @pl.when(ends)
        def _():
            wait_bytes(down_part.at[pl.ds(0, half)], semaphore)
            wait_bytes(down_part.at[pl.ds(0, half)], f_kept.at[2 * layer + 1])

        @pl.when(jnp.logical_not(ends))
        def _():
            wait_bytes(down_part, semaphore)

    def landing(layer):
        return from_x if layer == 1 else everyone.at[pl.ds(0, 16 * share)]

    def send_x(layer, piece):
        for z in range(4):
            start = (z * 2 + 1 - where.x) * share
            remote(
                part.at[piece, pl.ds(pl.multiple_of(start, share), share)],
                landing(layer).at[pl.ds((z * 4 + piece) * share, share)],
                x_sent.at[4 * layer + piece],
                x_got.at[4 * layer + piece],
                where.x_peer,
            ).start()

    def attention_grads(piece):
        def step(i, carry):
            here = pl.ds(pl.multiple_of(i * 256, 256), 256)
            if piece < 3:
                right = d_qkv2[:, piece * width : (piece + 1) * width]
                value = left_trans(normed2[:, here], right)
            else:
                value = left_trans(attended2[:, here], d_middle2[...])
            part[piece, here, :] = value.astype(BF)
            return carry

        lax.fori_loop(0, normed2.shape[1] // 256, step, 0)

    def send_z(source, target, number, size, stride, first=0):
        for z in range(4):
            piece = source.at[pl.ds(z * stride + first, size)]
            peer = z * 4 + where.x * 2 + where.core

            @pl.when(where.z != z)
            def _():
                remote(piece, target, z_sent.at[number], z_got.at[number], peer).start()

            @pl.when(where.z == z)
            def _():
                pltpu.make_async_copy(piece, target, z_got.at[number]).start()

    def finish_x(layer, pieces):
        arrived = landing(layer)
        for piece in pieces:
            wait_bytes(arrived.at[pl.ds(0, 4 * share)], x_got.at[4 * layer + piece])
            for z in range(4):
                start = pl.multiple_of((z * 2 + where.x) * share, share)
                here = pl.ds((z * 4 + piece) * share, share)
                arrived[here, :] = (
                    arrived[here, :].astype(F32)
                    + part[piece, pl.ds(start, share), :].astype(F32)
                ).astype(BF)
            target = attn_got.at[layer, where.z, pl.ds(piece * share, share)]
            send_z(arrived, target, layer, share, 4 * share, piece * share)

    first_loads = loads_of(1)
    starting = [load(cotangent, rounded, 10), load(codes, codes2.at[own], 11)]
    for copy in starting + first_loads:
        copy.start()
    where.greet_all()
    codes_copy = to_core(codes_theirs, codes2.at[theirs], 10)
    codes_copy.start()
    starting[0].wait()
    grad[...] = rounded[...].astype(F32)
    gain_sums[...] = jnp.zeros_like(gain_sums)
    fill_heads(heads)
    waiting = {1: first_loads, 0: loads_of(0)}

    for layer in (1, 0):
        copies = waiting[layer]
        team = Team(
            rows,
            rounded,
            everyone,
            sums,
            tuple(team_scratch) + (team_sent.at[layer], team_got.at[layer]),
        )

        def compute(m, start):
            here = pl.ds(start, 2 * rows)
            ffn_back_rows(everyone[here, :], v_normed, w_both, w_down, gated, d_both, here)
            split_pair(
                team, m, lambda c: right_trans(d_both[here, :], w_both[c, :]), sums, team.part
            )

        def between():
            if layer == 0:
                drain_ffn(1)

            def down_step(i, carry):
                here = pl.ds(pl.multiple_of(i * 256, 256), 256)
                down_part[here, :] = left_trans(gated[:, here], everyone[...]).astype(BF)
                return carry

            def both_step(i, carry):
                here = pl.ds(pl.multiple_of(i * 256, 256), 256)
                both_part[here, :] = left_trans(v_normed[:, here], d_both[...]).astype(BF)
                return carry

            lax.fori_loop(0, down_part.shape[0] // 256, down_step, 0)
            lax.fori_loop(0, width // 256, both_step, 0)
            if layer == 1:
                for copy in waiting[0][:3]:
                    copy.start()

        def early():
            for copy in copies[:3]:
                copy.wait()
            if layer == 0:
                share_ffn(1, d_both.at[pl.ds(0, 8 * share)])
                for piece in (1, 2):
                    attention_grads(piece)

        team.run(compute, between, d_middle, early=early)
        if layer == 0:
            send_x(1, 1)
            send_x(1, 2)
        send_ffn(layer)
        copies[3].wait()

        def norm_step(i, carry):
            here = pl.ds(pl.multiple_of(i * chunk, 16), chunk)
            value = v_middle[here, :]
            back, gain_grad = norm_back(
                d_middle[here, :], value, inverse_rms(value), gain_rows[2 + layer : 3 + layer, :]
            )
            gain_sums[2 + layer : 3 + layer, :] += gain_grad[None]
            gradient = grad[here, :] + back
            d_middle[here, :] = gradient
            d_middle2[here, :] = gradient.astype(BF)
            return carry

        lax.fori_loop(0, rows // chunk, norm_step, 0)
        shared = [to_core(d_middle2.at[own], d_middle2.at[theirs], 5 * layer)]
        shared[0].start()
        for copy in copies[4:9]:
            copy.wait()

        for first in range(0, width, 256):
            columns = slice(first, first + 256)
            sums[2, :, columns] = right_trans(d_middle2[:rows, :], w_out[columns, :])

        def attention_step(i, carry):
            here = pl.ds(pl.multiple_of(i * small, small), small)
            d_attended = sums[2, here, :].astype(BF).astype(F32)
            q = v_qkv[here, :width].astype(F32)
            k = v_qkv[here, width : 2 * width].astype(F32)
            k0 = v_other[here, :width].astype(F32)
            mine, past = probabilities(q, k, k0, heads, where.place)
            d_mine = heads_summed(d_attended * v_qkv[here, 2 * width :].astype(F32), heads)
            d_past = heads_summed(d_attended * v_other[here, width:].astype(F32), heads)
            inner = mine * d_mine + past * d_past
            s_past = heads_spread(past * (d_past - inner) / math.sqrt(HD), heads)
            d_other[here, :width] = (s_past * q).astype(BF)
            d_other[here, width:] = (heads_spread(past, heads) * d_attended).astype(BF)
            s_mine = heads_spread(mine * (d_mine - inner) / math.sqrt(HD), heads)
            d_qkv2[here, :width] = (s_mine * k + s_past * k0).astype(BF)
            sums[0, here, :] = s_mine * q
            sums[1, here, :] = heads_spread(mine, heads) * d_attended
            return carry

        lax.fori_loop(0, rows // small, attention_step, 0)
        exchange = remote(
            d_other, y_in.at[layer], y_sent.at[layer], y_got.at[layer], where.index, 1 - where.place
        )
        exchange.start()

        def operand_step(i, carry):
            here = pl.ds(pl.multiple_of(i * chunk, 16), chunk)
            value = v_stream[here, :]
            value = value * inverse_rms(value) * gain_rows[layer : layer + 1, :]
            for number, item, target in (
                (0, value.astype(BF).astype(F32), normed2),
                (1, v_attended[here, :].astype(F32), attended2),
            ):
                for_core[number, here, :] = own_half(item, where.core, True).astype(BF)
                target[here, :] = own_half(item, where.core, False).astype(BF)
            return carry

        lax.fori_loop(0, rows // chunk, operand_step, 0)
        shared.append(to_core(for_core.at[0], normed2.at[theirs], 5 * layer + 1))
        shared.append(to_core(for_core.at[1], attended2.at[theirs], 5 * layer + 2))
        queries, others = pl.ds(0, width), pl.ds(width, 2 * width)
        shared.append(
            to_core(d_qkv2.at[own, queries], d_qkv2.at[theirs, queries], 5 * layer + 3)
        )
        for copy in shared[1:]:
            copy.start()
        for copy in shared:
            copy.wait_recv()
        for piece in (3, 0):
            if layer == 0:
                finish_x(1, (piece,))
                wait_bytes(part.at[piece, pl.ds(0, 4 * share)], x_sent.at[4 + piece])
            attention_grads(piece)
            send_x(layer, piece)
        exchange.wait_recv()
        d_qkv2[:rows, width : 2 * width] = (
            sums[0] + y_in[layer, :, :width].astype(F32)
        ).astype(BF)
        d_qkv2[:rows, 2 * width :] = (sums[1] + y_in[layer, :, width:].astype(F32)).astype(BF)
        last = to_core(d_qkv2.at[own, others], d_qkv2.at[theirs, others], 5 * layer + 4)
        last.start()
        shared.append(last)
        if layer == 0:
            finish_x(1, (1, 2))
            for piece in (1, 2):
                wait_bytes(part.at[piece, pl.ds(0, 4 * share)], x_sent.at[4 + piece])
            last.wait_recv()
            for piece in (1, 2):
                attention_grads(piece)
                send_x(0, piece)
        copies[9].wait()
        for first in range(0, width, 256):
            columns = slice(first, first + 256)
            sums[2, :, columns] = right_trans(d_qkv2[:rows, :], w_qkv[columns, :])

        def stream_step(i, carry):
            here = pl.ds(pl.multiple_of(i * chunk, 16), chunk)
            value = v_stream[here, :]
            back, gain_grad = norm_back(
                sums[2, here, :], value, inverse_rms(value), gain_rows[layer : layer + 1, :]
            )
            gain_sums[layer : layer + 1, :] += gain_grad[None]
            gradient = d_middle[here, :] + back
            grad[here, :] = gradient
            rounded_to = rounded if layer == 1 else grad2
            rounded_to[here, :] = gradient.astype(BF)
            return carry

        lax.fori_loop(0, rows // chunk, stream_step, 0)
        for copy in shared:
            copy.wait_send()
        exchange.wait_send()
        if layer == 1:
            last.wait_recv()
            for copy in waiting[0][3:]:
                copy.start()

    grad_out = load(grad, input_grad, 14)
    grad_out.start()
    grad_copy = to_core(grad2.at[own], grad2.at[theirs], 11)
    grad_copy.start()
    index = where.index

    def gain_columns(device):
        return gain_sums.at[:, pl.ds(pl.multiple_of(device // 2 * 128, 128), 128)]

    def send_gain(step, carry):
        peer = lax.rem(index + step, 16)
        remote(gain_columns(peer), gain_got.at[index], g_sent.at[0], g_got.at[0], peer).start()
        return carry

    lax.fori_loop(1, 16, send_gain, 0)
    pltpu.make_async_copy(gain_columns(index), gain_got.at[index], g_got.at[0]).start()
    grad_copy.wait()
    codes_copy.wait()
    starting[1].wait()
    vocab = codes2.shape[1] // 8

    def table_step(i, carry):
        here = pl.ds(pl.multiple_of(i * 256, 256), 256)
        d_both[here, :] = left_trans(codes2[:, here], grad2[...]).astype(BF)
        return carry

    lax.fori_loop(0, 8 * vocab // 256, table_step, 0)
    table_in = everyone.at[pl.ds(16 * share, 4 * vocab)]
    for z in range(4):
        start = pl.multiple_of((z * 2 + 1 - where.x) * vocab, vocab)
        remote(
            d_both.at[pl.ds(start, vocab)],
            table_in.at[pl.ds(z * vocab, vocab)],
            x_sent.at[8],
            x_got.at[8],
            where.x_peer,
        ).start()
    share_ffn(0, d_both.at[pl.ds(8 * vocab, 8 * share)])
    finish_x(0, (3, 0, 1, 2))
    wait_bytes(table_in, x_got.at[8])
    for z in range(4):
        start = pl.multiple_of((z * 2 + where.x) * vocab, vocab)
        here = pl.ds(z * vocab, vocab)
        table_in[here, :] = (
            table_in[here, :].astype(F32) + d_both[pl.ds(start, vocab), :].astype(F32)
        ).astype(BF)
    send_z(table_in, table_got.at[where.z], 2, vocab, vocab)

    drain_ffn(0)
    for layer in (0, 1):
        wait_bytes(both_got.at[layer, pl.ds(0, 7)], f_got.at[3 * layer + 2])
        arrived, ends = f_got.at[3 * layer + 1], (index == 0) | (index == 15)
        pl.when(ends)(lambda: wait_bytes(down_got.at[layer, 0], arrived))
        pl.when(jnp.logical_not(ends))(lambda: wait_bytes(down_got.at[layer], arrived))
        wait_bytes(attn_got.at[layer], z_got.at[layer])
        wait_bytes(everyone.at[pl.ds(0, 12 * share)], z_sent.at[layer])
    for piece in range(4):
        wait_bytes(part.at[piece, pl.ds(0, 4 * share)], x_sent.at[piece])
    wait_bytes(table_got, z_got.at[2])
    wait_bytes(everyone.at[pl.ds(0, 3 * vocab)], z_sent.at[2])
    wait_bytes(d_both.at[pl.ds(0, 4 * vocab)], x_sent.at[8])
    grad_out.wait()
    wait_bytes(gain_got, g_got.at[0])
    wait_bytes(gain_got.at[pl.ds(0, 15)], g_sent.at[0])


def backward(
    cotangent, codes, codes_theirs, gain_rows, stream, middle, qkv, other, attended, normed, qkv0,
    qkv1, outs, both, down
):
    rows, width = cotangent.shape
    hidden = down.shape[1]
    share = width // 16
    vocab = codes.shape[1] // 8
    shape = jax.ShapeDtypeStruct
    hbm = pl.BlockSpec(memory_space=pl.ANY)
    vmem = pltpu.VMEM
    dma = pltpu.SemaphoreType.DMA
    return pl.pallas_call(
        backward_kernel,
        out_shape=(
            shape((rows, width), F32),
            shape((2, 8, share, 2 * hidden), BF),
            shape((2, 8 * share, 2 * hidden), BF),
            shape((2, 2, hidden // 2, width), BF),
            shape((2, 4, 4 * share, width), BF),
            shape((4, vocab, width), BF),
            shape((16, 8, 128), F32),
        ),
        in_specs=[hbm] * 3 + in_vmem(1) + [hbm] * 11,
        out_specs=tuple([hbm] * 7),
        scratch_shapes=[
            vmem((rows, width), F32),
            vmem((rows, width), F32),
            vmem((rows, 3 * width), BF),
            vmem((rows, 2 * width), BF),
            vmem((rows, width), BF),
            vmem((8 * rows, width), BF),
            vmem((width, 3 * width), BF),
            vmem((width, width), BF),
            vmem((width, 2 * hidden), BF),
            vmem((hidden, width), BF),
            vmem((rows, width), F32),
            vmem((rows, width), F32),
            vmem((rows, width), BF),
            vmem((2 * rows, width // 2), BF),
            vmem((2 * rows, width // 2), BF),
            vmem((2 * rows, 3 * width), BF),
            vmem((2 * rows, width), BF),
            vmem((2, rows, width // 2), BF),
            vmem((rows, 2 * width), BF),
            vmem((2, rows, 2 * width), BF),
            vmem((2 * rows, 8 * vocab), BF),
            vmem((2 * rows, width), BF),
            vmem((4, width // 2, width), BF),
            vmem((16 * share, width), BF),
            vmem((8 * rows, width), BF),
            vmem((8 * rows, hidden), BF),
            vmem((8 * rows, 2 * hidden), BF),
            vmem((4, rows, width), F32),
            vmem((width, 2 * hidden), BF),
            vmem((hidden, width), BF),
            vmem((8, width), F32),
            vmem((width, 128), BF),
            dma((15,)),
            dma((12,)),
            dma((12,)),
            dma((2,)),
            dma((2,)),
            dma((9,)),
            dma((9,)),
            dma((3,)),
            dma((3,)),
            dma((6,)),
            dma((6,)),
            dma((4,)),
            dma((1,)),
            dma((1,)),
        ]
        + Team.scratch(rows, width)[:8]
        + [dma((2, Team.SCRATCH_COPIES)), dma((2, Team.SCRATCH_COPIES))],
        compiler_params=pltpu.CompilerParams(
            collective_id=4, has_side_effects=True, vmem_limit_bytes=63 * 2**20
        ),
        name="backward_pass",
    )(
        cotangent,
        codes,
        codes_theirs,
        gain_rows,
        stream,
        middle,
        qkv,
        other,
        attended,
        normed,
        qkv0,
        qkv1,
        outs,
        both,
        down,
    )


def finish_kernel(both, down, attn, table, table_grad, qkv_grad, out_grad, gate_grad, up_grad, down_grad):
    hidden = both.shape[3] // 2
    share, width = both.shape[2], attn.shape[3]
    for layer in range(LAYERS):
        for member in range(8):
            columns = slice(member * hidden, (member + 1) * hidden)
            gate_grad[layer, 0, :, columns] = both[layer, member, :, :hidden].astype(F32)
            up_grad[layer, 0, :, columns] = both[layer, member, :, hidden:].astype(F32)
        down_grad[layer, 0] = down[layer, 0].astype(F32) + down[layer, 1].astype(F32)
        for piece in range(4):
            rows = slice(piece * share, (piece + 1) * share)
            value = sum(attn[layer, z, rows, :].astype(F32) for z in range(4))
            if piece < 3:
                qkv_grad[layer, 0, :, piece * width : (piece + 1) * width] = value
            else:
                out_grad[layer, 0] = value
    table_grad[0] = sum(table[z].astype(F32) for z in range(4))


def finish(both, down, attn, table):
    share, width = both.shape[2], attn.shape[3]
    hidden = both.shape[3] // 2
    shape = jax.ShapeDtypeStruct
    return pl.pallas_call(
        finish_kernel,
        out_shape=(
            shape((1,) + table.shape[1:], F32),
            shape((LAYERS, 1, share, 3 * width), F32),
            shape((LAYERS, 1, share, width), F32),
            shape((LAYERS, 1, share, 8 * hidden), F32),
            shape((LAYERS, 1, share, 8 * hidden), F32),
            shape((LAYERS, 1, hidden // 2, width), F32),
        ),
        in_specs=in_vmem(4),
        out_specs=tuple(in_vmem(6)),
        compiler_params=pltpu.CompilerParams(vmem_limit_bytes=48 * 2**20),
        name="finish",
    )(both, down, attn, table)


class Plan:
    def __init__(self, count):
        self.count = count
        self.team = 8
        self.teams = count // self.team
        self.across = [[g * self.team + t for g in range(self.teams)] for t in range(self.team)]

    def ffn_weights(self, gate, up, down):
        rows = gate.shape[0]
        both = jnp.stack([gate, up], axis=1).reshape(rows, 2, self.teams, self.team, -1)
        parts = both.transpose(3, 0, 1, 2, 4).reshape(self.team, rows, -1)
        parts = jnp.broadcast_to(parts[None], (self.teams,) + parts.shape)
        parts = parts.reshape((self.count,) + parts.shape[2:])
        mine = lax.all_to_all(parts, "frames", split_axis=0, concat_axis=0, tiled=True)
        return mine.reshape(self.count * rows, -1), self.gather_across(down)

    def gather_across(self, rows):
        if self.teams != 2:
            return lax.all_gather(rows, "frames", axis=0, tiled=True, axis_index_groups=self.across)
        theirs = lax.ppermute(rows, "frames", self.partners())
        first = lax.axis_index("frames") < self.team
        return jnp.concatenate([jnp.where(first, rows, theirs), jnp.where(first, theirs, rows)])

    def scatter_across(self, rows):
        if self.teams != 2:
            part = lax.psum_scatter(
                rows.astype(BF),
                "frames",
                scatter_dimension=0,
                tiled=True,
                axis_index_groups=self.across,
            )
            return part.astype(F32)
        half = rows.shape[0] // 2
        first = lax.axis_index("frames") < self.team
        mine = jnp.where(first, rows[:half], rows[half:])
        sent = jnp.where(first, rows[half:], rows[:half]).astype(BF)
        return mine + lax.ppermute(sent, "frames", self.partners()).astype(F32)

    def partners(self):
        return [(i, (i + self.team) % self.count) for i in range(self.count)]

    def ffn_grads(self, both_part, down_part):
        parts = both_part.astype(BF).reshape(self.count, -1, both_part.shape[1])
        parts = lax.all_to_all(parts, "frames", split_axis=0, concat_axis=0, tiled=True)
        rows = parts.shape[1]
        parts = parts.astype(F32).reshape(self.teams, self.team, rows, -1).sum(axis=0)
        down = self.scatter_across(down_part)
        parts = parts.reshape(self.team, rows, 2, self.teams, -1)
        both = parts.transpose(1, 2, 3, 0, 4).reshape(rows, 2, -1)
        return both[:, 0], both[:, 1], down


def attend(qkv, other):
    width = HEADS * HD
    position = lax.axis_index("pos")
    q, k, v = (qkv[:, i * width : (i + 1) * width].astype(F32) for i in range(3))
    k0, v0 = (other[:, i * width : (i + 1) * width].astype(F32) for i in range(2))
    own = head_sum(q * k) / math.sqrt(HD)
    past = jnp.where(position > 0, head_sum(q * k0) / math.sqrt(HD), -1e30)
    largest = jnp.maximum(own, past)
    own, past = jnp.exp(own - largest), jnp.exp(past - largest)
    total = own + past
    own, past = own / total, past / total
    attended = head_spread(own) * v + head_spread(past) * v0
    return attended.astype(BF), own, past


def attend_back(grad, qkv, other, own, past):
    width = HEADS * HD
    q, k, v = (qkv[:, i * width : (i + 1) * width].astype(F32) for i in range(3))
    k0, v0 = (other[:, i * width : (i + 1) * width].astype(F32) for i in range(2))
    grad = grad.astype(F32)
    d_own, d_past = head_sum(grad * v), head_sum(grad * v0)
    inner = own * d_own + past * d_past
    s_own = head_spread(own * (d_own - inner) / math.sqrt(HD))
    s_past = head_spread(past * (d_past - inner) / math.sqrt(HD))
    own, past = head_spread(own), head_spread(past)
    d_q = s_own * k + s_past * k0
    d_k = s_own * q
    d_v = own * grad
    d_other = jnp.concatenate([s_past * q, past * grad], axis=1)
    return d_q, d_k, d_v, d_other


def plain_forward(
    plan, onward, frames_in, onehot, code_table, w_qkv, w_out, w_gate, w_up, w_down, gain_attn, gain_ffn
):
    width = frames_in.shape[-1]
    gains = jnp.stack([gain_attn[0, 0], gain_attn[1, 0], gain_ffn[0, 0], gain_ffn[1, 0]], axis=1)
    gains = jnp.pad(gains, ((0, 0), (0, 124)))
    full_table = lax.all_gather(code_table[0], "frames", axis=0, tiled=True)
    first_qkv = lax.all_gather(
        jnp.concatenate([w_qkv[0, 0], gains], axis=1), "frames", axis=0, tiled=True
    )
    gain_rows = first_qkv[:, 3 * width : 3 * width + 4].astype(F32).T
    qkv_all = [first_qkv[:, : 3 * width], None]
    out_all = [lax.all_gather(w_out[0, 0], "frames", axis=0, tiled=True), None]
    ffn_all = [plan.ffn_weights(w_gate[0, 0], w_up[0, 0], w_down[0, 0]), None]
    qkv_all[1] = lax.all_gather(w_qkv[1, 0], "frames", axis=0, tiled=True)
    out_all[1] = lax.all_gather(w_out[1, 0], "frames", axis=0, tiled=True)
    ffn_all[1] = plan.ffn_weights(w_gate[1, 0], w_up[1, 0], w_down[1, 0])

    stream = frames_in[:, 0].astype(F32) + plain(onehot, full_table)
    kept = []
    for layer in range(LAYERS):
        inv_attn = inverse_rms(stream)
        normed_attn = (stream * inv_attn * gain_rows[layer]).astype(BF)
        qkv = plain(normed_attn, qkv_all[layer]).astype(BF)
        other = lax.ppermute(qkv[:, width:], "pos", onward)
        attended, own, past = attend(qkv, other)
        middle = stream + plain(attended, out_all[layer])
        inv_ffn = inverse_rms(middle)
        normed_ffn = (middle * inv_ffn * gain_rows[2 + layer]).astype(BF)
        both_all, down_all = ffn_all[layer]
        team_normed, summed = ffn_forward(normed_ffn, both_all, down_all)
        new_stream = middle + summed
        kept.append(
            (
                stream,
                inv_attn,
                normed_attn,
                qkv,
                other,
                own,
                past,
                attended,
                middle,
                inv_ffn,
                team_normed,
            )
        )
        stream = new_stream
    return kept, stream, gain_rows, qkv_all, out_all, ffn_all


def fused_body(
    onehot, frames_in, code_table, w_qkv, w_out, w_gate, w_up, w_down, gain_attn, gain_ffn, cotangent
):
    share = gain_attn.shape[-1]
    width = frames_in.shape[-1]
    gains = jnp.concatenate([gain_attn[:, 0], gain_ffn[:, 0]], axis=0).astype(F32)
    gains = jnp.pad(gains, ((0, 4), (0, share)))
    odd = lax.rem(lax.axis_index("frames"), 2) == 1
    gains = jnp.where(odd, jnp.roll(gains, share, axis=1), gains)
    act, *saved = forward(
        frames_in[:, 0],
        onehot,
        gains,
        code_table[0],
        w_qkv[:, 0],
        w_out[:, 0],
        w_gate[:, 0],
        w_up[:, 0],
        w_down[:, 0],
    )
    stream, middle, qkv, other, attended, normed, gain_rows, qkv0, qkv1, outs, both, down = saved
    blocks = onehot.reshape(onehot.shape[0], 8, 2, -1)
    first, second = (blocks[:, :, i].reshape(onehot.shape[0], -1) for i in (0, 1))
    codes, codes_theirs = jnp.where(odd, second, first), jnp.where(odd, first, second)
    input_grad, both_got, pair_got, down_got, attn_got, table_got, gain_got = backward(
        cotangent[:, 0],
        codes,
        codes_theirs,
        gain_rows,
        stream,
        middle,
        qkv,
        other,
        attended,
        normed,
        qkv0,
        qkv1,
        outs,
        both,
        down,
    )
    table, qkv_grad, out_grad, gate_grad, up_grad, down_grad = finish(
        both_got, down_got, attn_got, table_got
    )
    sums = gain_got.sum(axis=0)
    sums = jnp.where(odd, sums[:4, 64:], sums[:4, :64]).reshape(2, LAYERS, 1, share)
    return (
        act[:, None, :],
        input_grad[:, None, :],
        table,
        qkv_grad,
        out_grad,
        gate_grad,
        up_grad,
        down_grad,
        sums[0],
        sums[1],
    )


def body(
    frames_in,
    code_table,
    code_ids,
    delays,
    item_lengths,
    w_qkv,
    w_out,
    w_gate,
    w_up,
    w_down,
    gain_attn,
    gain_ffn,
    cotangent,
):
    count = lax.axis_size("frames")
    plan = Plan(count)
    positions = lax.axis_size("pos")
    onward = [(i, i + 1) for i in range(positions - 1)]
    backward = [(i + 1, i) for i in range(positions - 1)]
    local_frames = frames_in.shape[0]
    item_count = item_lengths.shape[0]
    width = frames_in.shape[-1]

    neighbours = [(i, i + 1) for i in range(count - 1)]
    earlier = lax.ppermute(code_ids[local_frames - 2 :], "frames", neighbours)
    extended = jnp.concatenate([earlier, code_ids], axis=0)[:, 0]
    global_frame = lax.axis_index("frames") * local_frames + jnp.arange(
        local_frames, dtype=jnp.int32
    )
    item_ends = jnp.cumsum(item_lengths)
    starts = item_ends - item_lengths
    item_index = jnp.sum((starts[None, :] <= global_frame[:, None]).astype(jnp.int32), axis=1) - 1
    chosen = item_index[:, None] == jnp.arange(item_count, dtype=jnp.int32)[None, :]
    item_begin = jnp.sum(jnp.where(chosen, starts[None, :], 0), axis=1)
    delay_rows = jnp.sum(jnp.where(chosen, delays[:, 0][None, :], 0), axis=1)
    one_back = extended[1 : local_frames + 1]
    two_back = extended[:local_frames]
    code_rows = jnp.where(delay_rows == 1, one_back, two_back)
    is_valid = global_frame - delay_rows >= item_begin
    vocab_size = code_table.shape[1] * count
    matches = code_rows[:, None] == jnp.arange(vocab_size, dtype=jnp.int32)[None, :]
    onehot = (matches & is_valid[:, None]).astype(BF)

    if count == 16:
        return fused_body(
            onehot, frames_in, code_table, w_qkv, w_out, w_gate, w_up, w_down, gain_attn, gain_ffn,
            cotangent,
        )
    kept, stream, gain_rows, qkv_all, out_all, ffn_all = plain_forward(
        plan, onward, frames_in, onehot, code_table, w_qkv, w_out, w_gate, w_up, w_down,
        gain_attn, gain_ffn,
    )
    output = stream.astype(BF)[:, None, :]

    gradient = cotangent[:, 0].astype(F32)
    collected = [None] * LAYERS
    gain_parts = [None] * (2 * LAYERS)
    for layer in reversed(range(LAYERS)):
        (
            stream,
            inv_attn,
            normed_attn,
            qkv,
            other,
            own,
            past,
            attended,
            middle,
            inv_ffn,
            team_normed,
        ) = kept[layer]
        both_all, down_all = ffn_all[layer]
        grad_normed, both_part, down_part = ffn_backward(
            gradient.astype(BF), both_all, down_all, team_normed
        )
        ffn_shares = plan.ffn_grads(both_part, down_part)
        grad_middle, gain_parts[2 + layer] = norm_back(
            grad_normed, middle, inv_ffn, gain_rows[2 + layer]
        )
        grad_middle = gradient + grad_middle
        grad_attn = grad_middle.astype(BF)
        grad_attended = right_trans(grad_attn, out_all[layer]).astype(BF)
        d_q, d_k, d_v, d_other = attend_back(grad_attended, qkv, other, own, past)
        arrived = lax.ppermute(d_other.astype(BF), "pos", backward).astype(F32)
        grad_qkv = jnp.concatenate([d_q, d_k + arrived[:, :width], d_v + arrived[:, width:]], axis=1)
        grad_qkv = grad_qkv.astype(BF)
        out_part = left_trans(attended, grad_attn).astype(BF)
        out_share = lax.psum_scatter(out_part, "frames", scatter_dimension=0, tiled=True)
        grad_normed_attn = right_trans(grad_qkv, qkv_all[layer])
        grad_stream, gain_parts[layer] = norm_back(
            grad_normed_attn, stream, inv_attn, gain_rows[layer]
        )
        gradient = grad_middle + grad_stream
        qkv_part = left_trans(normed_attn, grad_qkv).astype(BF)
        if layer == 0:
            tail = jnp.stack(gain_parts, axis=1).astype(BF)
            qkv_part = jnp.concatenate([qkv_part, jnp.pad(tail, ((0, 0), (0, 124)))], axis=1)
        qkv_share = lax.psum_scatter(qkv_part, "frames", scatter_dimension=0, tiled=True)
        collected[layer] = (qkv_share.astype(F32), out_share.astype(F32)) + ffn_shares
    table_part = left_trans(onehot, gradient.astype(BF)).astype(BF)
    table_share = lax.psum_scatter(table_part, "frames", scatter_dimension=0, tiled=True)
    gain_shares = collected[0][0][:, 3 * width : 3 * width + 4].T
    collected[0] = (collected[0][0][:, : 3 * width],) + collected[0][1:]
    stacked = [
        jnp.stack([collected[layer][slot] for layer in range(LAYERS)], axis=0)[:, None]
        for slot in range(5)
    ]
    return (
        output,
        gradient[:, None, :],
        table_share.astype(F32)[None],
        stacked[0],
        stacked[1],
        stacked[2],
        stacked[3],
        stacked[4],
        gain_shares[:2][:, None],
        gain_shares[2:][:, None],
    )


def solution(mesh):
    return jax.shard_map(
        body,
        mesh=mesh,
        in_specs=(
            P("frames", "pos", None),
            P("pos", "frames", None),
            P("frames", "pos"),
            P(None, "pos"),
            P(),
            P(None, "pos", "frames", None),
            P(None, "pos", "frames", None),
            P(None, "pos", "frames", None),
            P(None, "pos", "frames", None),
            P(None, "pos", "frames", None),
            P(None, "pos", "frames"),
            P(None, "pos", "frames"),
            P("frames", "pos", None),
        ),
        out_specs=(
            P("frames", "pos", None),
            P("frames", "pos", None),
            P("pos", "frames", None),
            P(None, "pos", "frames", None),
            P(None, "pos", "frames", None),
            P(None, "pos", "frames", None),
            P(None, "pos", "frames", None),
            P(None, "pos", "frames", None),
            P(None, "pos", "frames"),
            P(None, "pos", "frames"),
        ),
        check_vma=False,
    )
```

```python
import math

import jax
import jax.numpy as jnp
from jax import lax
from jax.experimental import pallas as pl
from jax.experimental.pallas import tpu as pltpu
from jax.sharding import PartitionSpec as P

HEADS = 16
HD = 64
LAYERS = 2
EPSILON = 1e-06
HIGHEST = lax.Precision.HIGHEST
BF = jnp.bfloat16
F32 = jnp.float32


def plain(left, right):
    return jnp.dot(left, right, preferred_element_type=F32)


def left_trans(left, right):
    return lax.dot_general(left, right, (((0,), (0,)), ((), ())), preferred_element_type=F32)


def right_trans(left, right):
    return lax.dot_general(left, right, (((1,), (1,)), ((), ())), preferred_element_type=F32)


def inverse_rms(stream):
    return lax.rsqrt(jnp.mean(stream * stream, axis=-1, keepdims=True) + EPSILON)


def norm_back(gradient, stream, inverse, gain_row):
    scaled = gradient * gain_row
    gain_grad = jnp.sum(gradient * stream * inverse, axis=0)
    inner_sum = jnp.mean(scaled * stream, axis=-1, keepdims=True)
    return (inverse * scaled - stream * inverse * inverse * inverse * inner_sum, gain_grad)


def head_matrix():
    rows = lax.broadcasted_iota(jnp.int32, (HEADS * HD, HEADS), 0) // HD
    cols = lax.broadcasted_iota(jnp.int32, (HEADS * HD, HEADS), 1)
    return (rows == cols).astype(F32)


def head_sum(values):
    return jnp.dot(values, head_matrix(), precision=HIGHEST)


def head_spread(values):
    return jnp.dot(values, head_matrix().T, precision=HIGHEST)


MESH = pl.DeviceIdType.MESH
VMEM_LIMIT = 60 * 2**20


def in_vmem(count):
    return [pl.BlockSpec(memory_space=pltpu.VMEM)] * count


class Team:
    SCRATCH_COPIES = 19

    def __init__(self, rows, mine, everyone, sums, scratch):
        (self.part, self.from_core, self.from_across, self.from_x, self.from_z) = scratch[:5]
        (self.to_x, self.to_z, self.to_across, self.sent, self.got) = scratch[5:10]
        self.rows, self.half = rows, rows // 2
        self.mine, self.everyone, self.sums = mine, everyone, sums
        index = lax.axis_index("frames")
        self.place = lax.axis_index("pos")
        member = lax.rem(index, 8)
        self.core = lax.rem(member, 2)
        self.x = lax.rem(member // 2, 2)
        self.z = member // 4
        self.core_peer = index + 1 - 2 * self.core
        self.x_peer = index + 2 - 4 * self.x
        self.z_peer = index + 4 - 8 * self.z

    @staticmethod
    def scratch(rows, width):
        half = rows // 2
        return [
            pltpu.VMEM((4, rows, width), BF),
            pltpu.VMEM((4, rows, width), BF),
            pltpu.VMEM((2, half, width), BF),
            pltpu.VMEM((rows, width), BF),
            pltpu.VMEM((rows, width), BF),
            pltpu.VMEM((rows, width), BF),
            pltpu.VMEM((rows, width), BF),
            pltpu.VMEM((rows, width), BF),
            pltpu.SemaphoreType.DMA((Team.SCRATCH_COPIES,)),
            pltpu.SemaphoreType.DMA((Team.SCRATCH_COPIES,)),
        ]

    def greet(self):
        barrier = pltpu.get_barrier_semaphore()
        for peer in (self.core_peer, self.x_peer, self.z_peer):
            pl.semaphore_signal(barrier, inc=1, device_id=(peer, self.place), device_id_type=MESH)
        pl.semaphore_wait(barrier, 3)

    def copy(self, number, source, target, peer):
        return pltpu.make_async_remote_copy(
            src_ref=source,
            dst_ref=target,
            send_sem=self.sent.at[number],
            recv_sem=self.got.at[number],
            device_id=(peer, self.place),
            device_id_type=MESH,
        )

    def pair_start(self, m):
        x = self.x + (m % 2) * (1 - 2 * self.x)
        z = self.z + (m // 2) * (1 - 2 * self.z)
        return pl.multiple_of((z * 2 + x) * (2 * self.rows), 2 * self.rows)

    def shard(self, m, part=None, core=None):
        core = self.core if core is None else core
        start = self.pair_start(m) + core * self.rows
        size = self.rows
        if part is not None:
            start, size = start + part * self.half, self.half
        return self.everyone.at[pl.ds(pl.multiple_of(start, 16), size)]

    def gather_copies(self):
        own = self.shard(0)
        x_rows, z_rows = self.shard(1), self.shard(2)
        x_low, z_high = self.shard(1, 1), self.shard(2, 0)
        high, low = self.shard(3, 0), self.shard(3, 1)
        return [
            self.copy(0, self.mine, own, self.core_peer),
            self.copy(1, self.mine, own, self.x_peer),
            self.copy(2, self.mine, own, self.z_peer),
            self.copy(3, x_rows, x_rows, self.core_peer),
            self.copy(4, x_low, x_low, self.z_peer),
            self.copy(5, z_rows, z_rows, self.core_peer),
            self.copy(6, z_high, z_high, self.x_peer),
            self.copy(7, high, high, self.core_peer),
            self.copy(8, low, low, self.core_peer),
        ]

    def arrived(self, number):
        other = 1 - self.core
        target = [
            self.shard(0, core=other),
            self.shard(1),
            self.shard(2),
            self.shard(1, core=other),
            self.shard(3, 1),
            self.shard(2, core=other),
            self.shard(3, 0),
            self.shard(3, 0, core=other),
            self.shard(3, 1, core=other),
        ][number]
        self.copy(number, target, target, self.core_peer).wait_recv()

    def sum_copies(self):
        half = self.half
        high, low = pl.ds(0, half), pl.ds(half, half)
        copies = [
            self.copy(9 + m, self.part.at[m], self.from_core.at[m], self.core_peer)
            for m in range(4)
        ]
        copies += [
            self.copy(13, self.to_across.at[high], self.from_across.at[0], self.x_peer),
            self.copy(14, self.to_across.at[low], self.from_across.at[1], self.z_peer),
            self.copy(15, self.to_x.at[high], self.from_x.at[high], self.x_peer),
            self.copy(16, self.to_x.at[low], self.from_x.at[low], self.x_peer),
            self.copy(17, self.to_z.at[low], self.from_z.at[low], self.z_peer),
            self.copy(18, self.to_z.at[high], self.from_z.at[high], self.z_peer),
        ]
        return copies

    def run(self, compute, between, result, later=None, early=None):
        half, rows = self.half, self.rows
        gather = self.gather_copies()
        adds = self.sum_copies()
        for copy in gather[:3]:
            copy.start()
        start = self.pair_start(0) + self.core * rows
        self.everyone[pl.ds(pl.multiple_of(start, 16), rows), :] = self.mine[...]
        if early is not None:
            early()

        def total(m, first):
            return self.sums[m, first : first + half, :] + self.from_core[
                m, first : first + half, :
            ].astype(F32)

        def step(m, carry):
            @pl.when(m == 0)
            def _():
                self.arrived(0)

            @pl.when(m == 1)
            def _():
                self.arrived(1)
                gather[4].start()
                gather[3].start()
                self.arrived(2)
                gather[6].start()
                gather[5].start()
                self.arrived(3)

            @pl.when(m == 2)
            def _():
                self.arrived(5)

            @pl.when(m == 3)
            def _():
                self.arrived(6)
                gather[7].start()
                self.arrived(4)
                gather[8].start()
                self.arrived(7)
                self.arrived(8)

            compute(m, self.pair_start(m))
            self.copy(9 + m, self.part.at[m], self.from_core.at[m], self.core_peer).start()
            if later is not None:
                later(m)

            @pl.when(m == 2)
            def _():
                adds[1].wait_recv()
                self.to_x[:half, :] = total(1, 0).astype(BF)
                adds[6].start()

            return carry

        lax.fori_loop(0, 4, step, 0)
        adds[3].wait_recv()
        self.to_across[:half, :] = total(3, 0).astype(BF)
        adds[4].start()
        self.to_across[half:, :] = total(3, half).astype(BF)
        adds[5].start()
        adds[2].wait_recv()
        self.to_z[half:, :] = total(2, half).astype(BF)
        adds[8].start()
        between()
        for copy in gather:
            copy.wait_send()
        adds[5].wait_recv()
        self.to_x[half:, :] = (total(1, half) + self.from_across[1].astype(F32)).astype(BF)
        adds[7].start()
        adds[4].wait_recv()
        self.to_z[:half, :] = (total(2, 0) + self.from_across[0].astype(F32)).astype(BF)
        adds[9].start()
        adds[0].wait_recv()
        for number in (6, 7, 8, 9):
            adds[number].wait_recv()
        for first in (0, half):
            rows_here = slice(first, first + half)
            result[rows_here, :] = (
                total(0, first)
                + self.from_x[rows_here, :].astype(F32)
                + self.from_z[rows_here, :].astype(F32)
            )
        for copy in adds:
            copy.wait_send()


def split_pair(team, m, product, sums, part):
    rows = team.rows
    for first in range(0, sums.shape[2], 256):
        columns = slice(first, first + 256)
        value = product(columns)
        low, high = value[:rows], value[rows:]
        sums[m, :, columns] = jnp.where(team.core == 0, low, high)
        part[m, :, columns] = jnp.where(team.core == 0, high, low).astype(BF)


def hidden_units(block, both, hidden, first):
    gate = plain(block, both[:, first : first + 256])
    return gate, plain(block, both[:, hidden + first : hidden + first + 256])


def ffn_rows(block, both, down):
    hidden = down.shape[0]
    parts = []
    for first in range(0, hidden, 256):
        gate, up = hidden_units(block, both, hidden, first)
        parts.append((gate * jax.nn.sigmoid(gate) * up).astype(BF))
    gated = jnp.concatenate(parts, axis=1)
    return lambda columns: plain(gated, down[:, columns])


def ffn_forward_kernel(normed, both, down, everyone, result, sums, *scratch):
    rows = normed.shape[0]
    team = Team(rows, normed, everyone, sums, scratch)
    team.greet()

    def compute(m, start):
        block = everyone[pl.ds(start, 2 * rows), :]
        split_pair(team, m, ffn_rows(block, both, down), sums, team.part)

    team.run(compute, lambda: None, result)


def ffn_back_rows(block, normed, both, down, gated, d_both, here):
    hidden = down.shape[0]
    before = normed[here, :]
    for first in range(0, hidden, 256):
        columns = slice(first, first + 256)
        gate, up = hidden_units(before, both, hidden, first)
        d_gated = right_trans(block, down[columns, :])
        sig = jax.nn.sigmoid(gate)
        act = gate * sig
        gated[here, columns] = (act * up).astype(BF)
        d_both[here, columns] = (d_gated * up * sig * (1.0 + gate * (1.0 - sig))).astype(BF)
        d_both[here, hidden + first : hidden + first + 256] = (d_gated * act).astype(BF)


def ffn_backward_kernel(
    grad, both, down, normed, result, both_part, down_part, everyone, gated, d_both, sums, *scratch
):
    rows = grad.shape[0]
    team = Team(rows, grad, everyone, sums, scratch)
    team.greet()

    def compute(m, start):
        here = pl.ds(start, 2 * rows)
        ffn_back_rows(everyone[here, :], normed, both, down, gated, d_both, here)
        split_pair(team, m, lambda c: right_trans(d_both[here, :], both[c, :]), sums, team.part)

    def between():
        def down_step(i, carry):
            cols = pl.ds(pl.multiple_of(i * 256, 256), 256)
            down_part[:, cols] = left_trans(gated[...], everyone[:, cols])
            return carry

        def both_step(i, carry):
            cols = pl.ds(pl.multiple_of(i * 256, 256), 256)
            both_part[:, cols] = left_trans(normed[...], d_both[:, cols]).astype(BF)
            return carry

        lax.fori_loop(0, down_part.shape[1] // 256, down_step, 0)
        lax.fori_loop(0, both_part.shape[1] // 256, both_step, 0)

    team.run(compute, between, result)


def ffn_forward(normed, both, down):
    rows, width = normed.shape
    return pl.pallas_call(
        ffn_forward_kernel,
        out_shape=(
            jax.ShapeDtypeStruct((8 * rows, width), BF),
            jax.ShapeDtypeStruct((rows, width), F32),
        ),
        in_specs=in_vmem(3),
        out_specs=in_vmem(2),
        scratch_shapes=[pltpu.VMEM((4, rows, width), F32)] + Team.scratch(rows, width),
        compiler_params=pltpu.CompilerParams(
            collective_id=1, has_side_effects=True, vmem_limit_bytes=VMEM_LIMIT
        ),
        name="ffn_forward",
    )(normed, both, down)


def ffn_backward(grad, both, down, normed):
    rows, width = grad.shape
    hidden = down.shape[0]
    return pl.pallas_call(
        ffn_backward_kernel,
        out_shape=(
            jax.ShapeDtypeStruct((rows, width), F32),
            jax.ShapeDtypeStruct((width, 2 * hidden), BF),
            jax.ShapeDtypeStruct((hidden, width), F32),
        ),
        in_specs=in_vmem(4),
        out_specs=in_vmem(3),
        scratch_shapes=[
            pltpu.VMEM((8 * rows, width), BF),
            pltpu.VMEM((8 * rows, hidden), BF),
            pltpu.VMEM((8 * rows, 2 * hidden), BF),
            pltpu.VMEM((4, rows, width), F32),
        ]
        + Team.scratch(rows, width),
        compiler_params=pltpu.CompilerParams(
            collective_id=2, has_side_effects=True, vmem_limit_bytes=VMEM_LIMIT
        ),
        name="ffn_backward",
    )(grad, both, down, normed)


class Place:
    def __init__(self):
        self.index = lax.axis_index("frames")
        self.place = lax.axis_index("pos")
        self.core = lax.rem(self.index, 2)
        self.x = lax.rem(self.index // 2, 2)
        self.z = self.index // 4
        self.core_peer = self.index + 1 - 2 * self.core
        self.x_peer = self.index + 2 - 4 * self.x

    def greet_all(self):
        barrier = pltpu.get_barrier_semaphore()

        def signal(step, carry):
            peer = lax.rem(self.index + step, 16)
            pl.semaphore_signal(barrier, inc=1, device_id=(peer, self.place), device_id_type=MESH)
            return carry

        lax.fori_loop(1, 16, signal, 0)
        pl.semaphore_signal(
            barrier, inc=1, device_id=(self.index, 1 - self.place), device_id_type=MESH
        )
        pl.semaphore_wait(barrier, 16)


class Gather:
    def __init__(self, where, number, source, full, sent, got):
        self.where, self.source, self.full = where, source, full
        self.sent, self.got = sent.at[number], got.at[number]
        self.rows = source.shape[0]

    def shard(self, z, x, core):
        start = (z * 4 + x * 2 + core) * self.rows
        return self.full.at[pl.ds(pl.multiple_of(start, self.rows), self.rows)]

    def copy(self, source, target, sent, got, peer):
        return pltpu.make_async_remote_copy(
            src_ref=source,
            dst_ref=target,
            send_sem=self.sent.at[sent],
            recv_sem=self.got.at[got],
            device_id=(peer, self.where.place),
            device_id_type=MESH,
        )

    def z_copy(self, z, up, own=False):
        w = self.where
        target = self.shard(z, w.x, w.core)
        source = self.source if own else target
        if up:
            return self.copy(source, target, z, z, jnp.minimum(w.index + 4, 15))
        return self.copy(source, target, 4 + z, z, jnp.maximum(w.index - 4, 0))

    def x_copy(self, z, own=False):
        w = self.where
        target = self.shard(z, w.x, w.core)
        return self.copy(self.source if own else target, target, 8 + z, 4 + z, w.x_peer)

    def core_copy(self, z, other_x, own=False):
        w = self.where
        x = 1 - w.x if other_x else w.x
        target = self.shard(z, x, w.core)
        number = z * 2 + other_x
        return self.copy(
            self.source if own else target, target, 12 + number, 8 + number, w.core_peer
        )

    def local(self):
        w = self.where
        return pltpu.make_async_copy(
            self.source, self.shard(w.z, w.x, w.core), self.got.at[w.z]
        )

    def start(self):
        w = self.where
        pl.when(w.z < 3)(lambda: self.z_copy(w.z, True, True).start())
        pl.when(w.z > 0)(lambda: self.z_copy(w.z, False, True).start())
        self.x_copy(w.z, True).start()
        self.core_copy(w.z, 0, True).start()
        self.local().start()

    def pass_z(self, distance):
        w = self.where

        @pl.when(w.z >= distance)
        def _():
            z = w.z - distance
            self.z_copy(z, True).wait_recv()
            pl.when(w.z < 3)(lambda: self.z_copy(z, True).start())
            self.x_copy(z).start()
            self.core_copy(z, 0).start()

        @pl.when(w.z + distance <= 3)
        def _():
            z = w.z + distance
            self.z_copy(z, False).wait_recv()
            pl.when(w.z > 0)(lambda: self.z_copy(z, False).start())
            self.x_copy(z).start()
            self.core_copy(z, 0).start()

    def pass_x(self):
        w = self.where

        def hand(z):
            target = self.shard(z, 1 - w.x, w.core)
            self.copy(target, target, 8 + z, 4 + z, w.x_peer).wait_recv()
            self.core_copy(z, 1).start()

        hand(w.z)
        for distance in (1, 2, 3):
            pl.when(w.z >= distance)(lambda: hand(w.z - distance))
            pl.when(w.z + distance <= 3)(lambda: hand(w.z + distance))

    def finish(self):
        w = self.where
        for z in range(4):
            for other_x in (0, 1):
                x = 1 - w.x if other_x else w.x
                target = self.shard(z, x, 1 - w.core)
                number = z * 2 + other_x
                self.copy(target, target, 12 + number, 8 + number, w.core_peer).wait_recv()
        self.local().wait()

    def drain(self):
        w = self.where
        for z in range(4):
            pl.when((z <= w.z) & (w.z < 3))(lambda: self.z_copy(z, True).wait_send())
            pl.when((z >= w.z) & (w.z > 0))(lambda: self.z_copy(z, False).wait_send())
            self.x_copy(z).wait_send()
            self.core_copy(z, 0).wait_send()
            self.core_copy(z, 1).wait_send()


class Slices:
    def __init__(self, where, layer, gate, up, down, both, down_all, sent, got):
        self.where, self.both, self.down_all = where, both.at[layer], down_all.at[layer]
        self.gate, self.up, self.down = gate.at[layer], up.at[layer], down.at[layer]
        self.sent, self.got = sent.at[layer], got.at[layer]
        self.rows = self.gate.shape[0]
        self.hidden = self.down_all.shape[0]

    def piece(self, source, side, member):
        here = pl.ds(pl.multiple_of(self.where.index * self.rows, self.rows), self.rows)
        columns = pl.ds(pl.multiple_of(member * self.hidden, self.hidden), self.hidden)
        return source.at[:, columns], self.both.at[
            here, side * self.hidden : (side + 1) * self.hidden
        ]

    def remote(self, source, target, number, peer):
        return pltpu.make_async_remote_copy(
            src_ref=source,
            dst_ref=target,
            send_sem=self.sent.at[number],
            recv_sem=self.got.at[number],
            device_id=(peer, self.where.place),
            device_id_type=MESH,
        )

    def down_target(self):
        half = self.hidden // 2
        start = lax.rem(self.where.index, 2) * half
        return self.down_all.at[pl.ds(pl.multiple_of(start, half), half)]

    def start(self):
        index = self.where.index
        base = index - lax.rem(index, 8)

        def send(step, carry):
            member = lax.rem(index + step, 8)
            for side, source in ((0, self.gate), (1, self.up)):
                part, target = self.piece(source, side, member)
                self.remote(part, target, 0, base + member).start()
            return carry

        lax.fori_loop(1, 8, send, 0)
        for side, source in ((0, self.gate), (1, self.up)):
            part, target = self.piece(source, side, lax.rem(index, 8))
            pltpu.make_async_copy(part, target, self.got.at[0]).start()
        for team in (0, 1):
            peer = team * 8 + index // 2

            @pl.when(peer != index)
            def _():
                self.remote(self.down, self.down_target(), 1, peer).start()

            @pl.when(peer == index)
            def _():
                pltpu.make_async_copy(self.down, self.down_target(), self.got.at[1]).start()

    def team_rows(self, team):
        size = 8 * self.rows
        return self.both.at[pl.ds(pl.multiple_of(team * size, size), size)]

    def swap(self):
        mine = self.team_rows(self.where.index // 8)
        return self.remote(mine, mine, 2, lax.rem(self.where.index + 8, 16))

    def pass_on(self):
        mine = self.team_rows(self.where.index // 8)
        pltpu.make_async_copy(mine, mine, self.got.at[0]).wait()
        self.swap().start()

    def finish(self):
        theirs = self.team_rows(1 - self.where.index // 8)
        pltpu.make_async_copy(theirs, theirs, self.got.at[2]).wait()
        pltpu.make_async_copy(self.down_all, self.down_all, self.got.at[1]).wait()

    def drain(self):
        index = self.where.index
        most = self.both.at[pl.ds(0, 7 * self.rows)]
        pltpu.make_async_copy(most, most, self.sent.at[0]).wait()
        self.swap().wait_send()
        ends = (index == 0) | (index == 15)
        half = self.down_all.at[pl.ds(0, self.hidden // 2)]

        @pl.when(ends)
        def _():
            pltpu.make_async_copy(half, half, self.sent.at[1]).wait()

        @pl.when(jnp.logical_not(ends))
        def _():
            pltpu.make_async_copy(self.down_all, self.down_all, self.sent.at[1]).wait()


def two_parts(values):
    high = values.astype(BF)
    return high, (values - high.astype(F32)).astype(BF)


def heads_summed(values, heads):
    high, low = two_parts(values)
    return plain(high, heads[...]) + plain(low, heads[...])


def heads_spread(values, heads):
    high, low = two_parts(values)
    return right_trans(high, heads[...]) + right_trans(low, heads[...])


def fill_heads(heads):
    rows = lax.broadcasted_iota(jnp.int32, heads.shape, 0) // HD
    columns = lax.broadcasted_iota(jnp.int32, heads.shape, 1)
    heads[...] = jnp.where(rows == columns, 1.0, 0.0).astype(BF)


def probabilities(q, k, k0, heads, place):
    own = heads_summed(q * k, heads) / math.sqrt(HD)
    past = jnp.where(place > 0, heads_summed(q * k0, heads) / math.sqrt(HD), -1e30)
    return softmax_pair(own, past)


def softmax_pair(own, past):
    largest = jnp.maximum(own, past)
    own, past = jnp.exp(own - largest), jnp.exp(past - largest)
    total = own + past
    return own / total, past / total


def forward_kernel(
    frames, onehot, gain_shard, table, qkv0, qkv1, out0, out1, gate, up, down, *refs
):
    (act, stream, middle, qkv, other, attended, everyone, gain_rows) = refs[:8]
    (qkv0_out, qkv1_out, outs_out, both_out, down_out) = refs[8:13]
    (gains, table_all, qkv0_all, qkv1_all, outs_all, both, down_all) = refs[13:20]
    (heads, normed, result, sums, gather_sent, gather_got, slice_sent, slice_got) = refs[20:28]
    (y_sent, y_got, saved, scores, scores_in) = refs[28:33]
    team_scratch = refs[33:41]
    team_sent, team_got = refs[41:43]
    rows, width = frames.shape
    where = Place()

    def gather(number, source, full):
        return Gather(where, number, source, full, gather_sent, gather_got)

    gain_gather = gather(0, gain_shard, gains)
    table_gather = gather(1, table, table_all)
    qkv_gathers = [gather(2, qkv0, qkv0_all), gather(3, qkv1, qkv1_all)]
    out_gathers = [gather(4, out0, outs_all.at[0]), gather(5, out1, outs_all.at[1])]
    slices = [
        Slices(where, layer, gate, up, down, both, down_all, slice_sent, slice_got)
        for layer in range(LAYERS)
    ]
    where.greet_all()
    for item in (gain_gather, table_gather, qkv_gathers[0], out_gathers[0]):
        item.start()
    slices[0].start()
    fill_heads(heads)
    first = (gain_gather, table_gather, qkv_gathers[0], out_gathers[0])
    for item in first:
        for distance in (1, 2, 3):
            item.pass_z(distance)
    slices[0].pass_on()
    for item in first:
        item.pass_x()
    gain_gather.finish()
    for block in range(8):
        first, second = block * 16, block * 16 + 8
        gain_rows[:, block * 128 : (block + 1) * 128] = (
            gains[first : first + 8, :] + gains[second : second + 8, :]
        )
    table_gather.finish()
    for first in range(0, width, 256):
        columns = slice(first, first + 256)
        stream[0, :, columns] = frames[:, columns].astype(F32) + plain(
            onehot[...], table_all[:, columns]
        )
    saves = []
    second = (qkv_gathers[1], out_gathers[1])

    def save(source, target, number):
        copy = pltpu.make_async_copy(source, target, saved.at[number])
        copy.start()
        saves.append(copy)

    for layer in range(LAYERS):
        value = stream[layer]
        normed[...] = (value * inverse_rms(value) * gain_rows[layer : layer + 1, :]).astype(BF)
        qkv_gathers[layer].finish()
        weights = (qkv0_all, qkv1_all)[layer]
        if layer == 0:
            for item in second:
                item.start()
        save(weights, (qkv0_out, qkv1_out)[layer], layer)
        def to_other(source, target, number):
            return pltpu.make_async_remote_copy(
                src_ref=source,
                dst_ref=target,
                send_sem=y_sent.at[3 * layer + number],
                recv_sem=y_got.at[3 * layer + number],
                device_id=(where.index, 1 - where.place),
                device_id_type=MESH,
            )

        first = pl.multiple_of(2 * width * (1 - where.place), 128)
        exchange = [
            to_other(
                qkv.at[layer, :, pl.ds(first, width)], other.at[layer, :, pl.ds(width, width)], 0
            ),
            to_other(scores, scores_in.at[layer], 1),
            to_other(
                qkv.at[layer, :, pl.ds(width, width)], other.at[layer, :, pl.ds(0, width)], 2
            ),
        ]
        for first in list(range(0, width, 512)) + list(range(2 * width, 3 * width, 512)):
            columns = slice(first, first + 512)
            qkv[layer, :, columns] = plain(normed[...], weights[:, columns]).astype(BF)
        exchange[0].start()
        for first in range(width, 2 * width, 512):
            columns = slice(first, first + 512)
            qkv[layer, :, columns] = plain(normed[...], weights[:, columns]).astype(BF)
        if layer == 0:
            slices[1].start()
        k = qkv[layer, :, width : 2 * width].astype(F32)
        own = heads_summed(qkv[layer, :, :width].astype(F32) * k, heads) / math.sqrt(HD)
        exchange[0].wait_recv()
        scores[...] = heads_summed(other[layer, :, width:].astype(F32) * k, heads)
        exchange[1].start()
        exchange[2].start()
        exchange[1].wait_recv()
        past = jnp.where(where.place > 0, scores_in[layer] / math.sqrt(HD), -1e30)
        own, past = softmax_pair(own, past)
        attended[layer] = (
            heads_spread(own, heads) * qkv[layer, :, 2 * width :].astype(F32)
            + heads_spread(past, heads) * other[layer, :, width:].astype(F32)
        ).astype(BF)
        out_gathers[layer].finish()
        for first in range(0, width, 512):
            columns = slice(first, first + 512)
            middle[layer, :, columns] = stream[layer, :, columns] + plain(
                attended[layer], outs_all[layer, :, columns]
            )
        value = middle[layer]
        normed[...] = (value * inverse_rms(value) * gain_rows[2 + layer : 3 + layer, :]).astype(BF)
        if layer == 0:
            for item in second:
                item.pass_z(1)
        slices[layer].finish()
        save(both.at[layer], both_out.at[layer], 2 + layer)
        save(down_all.at[layer], down_out.at[layer], 4 + layer)
        team = Team(
            rows,
            normed,
            everyone.at[layer],
            sums,
            tuple(team_scratch) + (team_sent.at[layer], team_got.at[layer]),
        )

        def compute(m, start):
            block = everyone[layer, pl.ds(start, 2 * rows), :]
            rows_out = ffn_rows(block, both.at[layer], down_all.at[layer])
            split_pair(team, m, rows_out, sums, team.part)

        later = None
        if layer == 0:

            def later(m):
                pl.when(m == 1)(lambda: slices[1].pass_on())
                for step in (2, 3):

                    @pl.when(m == step)
                    def _():
                        for item in second:
                            item.pass_z(step)

        def between():
            if layer == 0:
                for item in second:
                    item.pass_x()

        team.run(compute, lambda: None, result, later)
        between()
        if layer == 0:
            stream[1] = middle[0] + result[...]
        else:
            act[...] = (middle[1] + result[...]).astype(BF)
        exchange[2].wait_recv()
        for copy in exchange:
            copy.wait_send()
    save(outs_all, outs_out, 6)
    for item in [gain_gather, table_gather] + qkv_gathers + out_gathers + slices:
        item.drain()
    for copy in saves:
        copy.wait()


def forward(frames, onehot, gain_shard, table, w_qkv, w_out, gate, up, down):
    rows, width = frames.shape
    hidden = gate.shape[2] // 8
    vocab = table.shape[0] * 16
    shape = jax.ShapeDtypeStruct
    hbm = pl.BlockSpec(memory_space=pl.ANY)
    return pl.pallas_call(
        forward_kernel,
        out_shape=(
            shape((rows, width), BF),
            shape((2, rows, width), F32),
            shape((2, rows, width), F32),
            shape((2, rows, 3 * width), BF),
            shape((2, rows, 2 * width), BF),
            shape((2, rows, width), BF),
            shape((2, 8 * rows, width), BF),
            shape((8, width), F32),
            shape((width, 3 * width), BF),
            shape((width, 3 * width), BF),
            shape((2, width, width), BF),
            shape((2, width, 2 * hidden), BF),
            shape((2, hidden, width), BF),
        ),
        in_specs=in_vmem(2) + [hbm] * 9,
        out_specs=tuple(in_vmem(8) + [hbm] * 5),
        scratch_shapes=[
            pltpu.VMEM((8 * 16, 128), F32),
            pltpu.VMEM((vocab, width), BF),
            pltpu.VMEM((width, 3 * width), BF),
            pltpu.VMEM((width, 3 * width), BF),
            pltpu.VMEM((2, width, width), BF),
            pltpu.VMEM((2, width, 2 * hidden), BF),
            pltpu.VMEM((2, hidden, width), BF),
            pltpu.VMEM((width, 128), BF),
            pltpu.VMEM((rows, width), BF),
            pltpu.VMEM((rows, width), F32),
            pltpu.VMEM((4, rows, width), F32),
            pltpu.SemaphoreType.DMA((6, 20)),
            pltpu.SemaphoreType.DMA((6, 16)),
            pltpu.SemaphoreType.DMA((2, 3)),
            pltpu.SemaphoreType.DMA((2, 3)),
            pltpu.SemaphoreType.DMA((6,)),
            pltpu.SemaphoreType.DMA((6,)),
            pltpu.SemaphoreType.DMA((7,)),
            pltpu.VMEM((rows, 128), F32),
            pltpu.VMEM((2, rows, 128), F32),
        ]
        + Team.scratch(rows, width)[:8]
        + [
            pltpu.SemaphoreType.DMA((2, Team.SCRATCH_COPIES)),
            pltpu.SemaphoreType.DMA((2, Team.SCRATCH_COPIES)),
        ],
        compiler_params=pltpu.CompilerParams(
            collective_id=3, has_side_effects=True, vmem_limit_bytes=63 * 2**20
        ),
        name="forward_pass",
    )(
        frames,
        onehot,
        gain_shard,
        table,
        w_qkv[0],
        w_qkv[1],
        w_out[0],
        w_out[1],
        gate,
        up,
        down,
    )


def own_half(values, core, other):
    rows, width = values.shape
    parts = []
    for first in range(0, width, 256):
        low, high = values[:, first : first + 128], values[:, first + 128 : first + 256]
        lane = lax.broadcasted_iota(jnp.int32, low.shape, 1)
        even = jnp.where(lane < 64, low, pltpu.roll(high, 64, 1))
        odd = jnp.where(lane < 64, pltpu.roll(low, 64, 1), high)
        first_core = (core == 0) != other
        parts.append(jnp.where(first_core, even, odd))
    return jnp.concatenate(parts, axis=1)


def backward_kernel(
    cotangent, codes, codes_theirs, gain_rows, stream, middle, qkv, other, attended, normed, qkv0,
    qkv1, outs, both, down, *refs
):
    (input_grad, both_got, pair_got, down_got, attn_got, table_got, gain_got) = refs[:7]
    refs = refs[1:]
    (v_stream, v_middle, v_qkv, v_other, v_attended, v_normed, w_qkv, w_out, w_both, w_down) = refs[
        6:16
    ]
    (grad, d_middle, rounded, normed2, attended2, d_qkv2, d_middle2, for_core, d_other, y_in) = refs[
        16:26
    ]
    (codes2, grad2, part, from_x, everyone, gated, d_both, sums, both_part, down_part) = refs[26:36]
    (gain_sums, heads, loaded, core_sent, core_got, y_sent, y_got, x_sent, x_got) = refs[36:45]
    (z_sent, z_got, f_sent, f_got, f_kept, g_sent, g_got, d_scores, s_in) = refs[45:54]
    team_scratch = refs[54:62]
    team_sent, team_got = refs[62:64]
    rows, width = cotangent.shape
    share = both_part.shape[0] // 16
    where = Place()
    own, theirs = pl.ds(0, rows), pl.ds(rows, rows)
    chunk, small = rows // 2, 32

    def load(source, target, number):
        return pltpu.make_async_copy(source, target, loaded.at[number])

    def loads_of(layer):
        return [
            load(normed.at[layer], v_normed, 0),
            load(both.at[layer], w_both, 1),
            load(down.at[layer], w_down, 2),
            load(middle.at[layer], v_middle, 3),
            load(outs.at[layer], w_out, 4),
            load(qkv.at[layer], v_qkv, 5),
            load(other.at[layer], v_other, 6),
            load(stream.at[layer], v_stream, 7),
            load(attended.at[layer], v_attended, 8),
            load((qkv0, qkv1)[layer], w_qkv, 9),
        ]

    def remote(source, target, sent, got, peer, place=None):
        return pltpu.make_async_remote_copy(
            src_ref=source,
            dst_ref=target,
            send_sem=sent,
            recv_sem=got,
            device_id=(peer, where.place if place is None else place),
            device_id_type=MESH,
        )

    def wait_bytes(like, semaphore):
        pltpu.make_async_copy(like, like, semaphore).wait()

    def to_core(source, target, number):
        return remote(source, target, core_sent.at[number], core_got.at[number], where.core_peer)

    def team_rows(ref, team):
        return ref.at[pl.ds(pl.multiple_of(team * 8 * share, 8 * share), 8 * share)]

    def swap(layer):
        team = where.index // 8
        return remote(
            team_rows(both_part, 1 - team),
            pair_got.at[layer],
            f_sent.at[3 * layer],
            f_got.at[3 * layer],
            lax.rem(where.index + 8, 16),
        )

    def share_ffn(layer, spare):
        index = where.index
        team, member = index // 8, lax.rem(index, 8)
        swap(layer).wait_recv()
        fetch = load(pair_got.at[layer], spare, 12 + layer)
        fetch.start()
        fetch.wait()
        start = pl.multiple_of(team * 8 * share, 8 * share)

        def add(i, carry):
            first = pl.multiple_of(i * 32, 32)
            here = pl.ds(pl.multiple_of(start + first, 32), 32)
            both_part[here, :] = (
                both_part[here, :].astype(F32) + spare[pl.ds(first, 32), :].astype(F32)
            ).astype(BF)
            return carry

        lax.fori_loop(0, 8 * share // 32, add, 0)

        def piece(owner):
            first = pl.multiple_of(start + owner * share, share)
            return both_part.at[pl.ds(first, share)]

        def send(step, carry):
            owner = lax.rem(member + step, 8)
            remote(
                piece(owner),
                both_got.at[layer, member],
                f_sent.at[3 * layer + 2],
                f_got.at[3 * layer + 2],
                team * 8 + owner,
            ).start()
            return carry

        lax.fori_loop(1, 8, send, 0)
        pltpu.make_async_copy(
            piece(member), both_got.at[layer, member], f_kept.at[2 * layer]
        ).start()

    def send_ffn(layer):
        index = where.index
        swap(layer).start()
        half = down_part.shape[0] // 2
        for side in (0, 1):
            owner = 2 * lax.rem(index, 8) + side
            piece = down_part.at[pl.ds(side * half, half)]
            target = down_got.at[layer, index // 8]

            @pl.when(owner != index)
            def _():
                remote(
                    piece, target, f_sent.at[3 * layer + 1], f_got.at[3 * layer + 1], owner
                ).start()

            @pl.when(owner == index)
            def _():
                pltpu.make_async_copy(piece, target, f_kept.at[2 * layer + 1]).start()

    def drain_ffn(layer):
        index = where.index
        swap(layer).wait_send()
        wait_bytes(both_part.at[pl.ds(0, 7 * share)], f_sent.at[3 * layer + 2])
        wait_bytes(both_part.at[pl.ds(0, share)], f_kept.at[2 * layer])
        ends = (index == 0) | (index == 15)
        half = down_part.shape[0] // 2
        semaphore = f_sent.at[3 * layer + 1]

        @pl.when(ends)
        def _():
            wait_bytes(down_part.at[pl.ds(0, half)], semaphore)
            wait_bytes(down_part.at[pl.ds(0, half)], f_kept.at[2 * layer + 1])

        @pl.when(jnp.logical_not(ends))
        def _():
            wait_bytes(down_part, semaphore)

    def landing(layer):
        return from_x if layer == 1 else everyone.at[pl.ds(0, 16 * share)]

    def send_x(layer, piece):
        for z in range(4):
            start = (z * 2 + 1 - where.x) * share
            remote(
                part.at[piece, pl.ds(pl.multiple_of(start, share), share)],
                landing(layer).at[pl.ds((z * 4 + piece) * share, share)],
                x_sent.at[4 * layer + piece],
                x_got.at[4 * layer + piece],
                where.x_peer,
            ).start()

    def attention_grads(piece):
        def step(i, carry):
            here = pl.ds(pl.multiple_of(i * 256, 256), 256)
            if piece < 3:
                right = d_qkv2[:, piece * width : (piece + 1) * width]
                value = left_trans(normed2[:, here], right)
            else:
                value = left_trans(attended2[:, here], d_middle2[...])
            part[piece, here, :] = value.astype(BF)
            return carry

        lax.fori_loop(0, normed2.shape[1] // 256, step, 0)

    def send_z(source, target, number, size, stride, first=0):
        for z in range(4):
            piece = source.at[pl.ds(z * stride + first, size)]
            peer = z * 4 + where.x * 2 + where.core

            @pl.when(where.z != z)
            def _():
                remote(piece, target, z_sent.at[number], z_got.at[number], peer).start()

            @pl.when(where.z == z)
            def _():
                pltpu.make_async_copy(piece, target, z_got.at[number]).start()

    def finish_x(layer, pieces):
        arrived = landing(layer)
        for piece in pieces:
            wait_bytes(arrived.at[pl.ds(0, 4 * share)], x_got.at[4 * layer + piece])
            for z in range(4):
                start = pl.multiple_of((z * 2 + where.x) * share, share)
                here = pl.ds((z * 4 + piece) * share, share)
                arrived[here, :] = (
                    arrived[here, :].astype(F32)
                    + part[piece, pl.ds(start, share), :].astype(F32)
                ).astype(BF)
            target = attn_got.at[layer, where.z, pl.ds(piece * share, share)]
            send_z(arrived, target, layer, share, 4 * share, piece * share)

    first_loads = loads_of(1)
    starting = [load(cotangent, rounded, 10), load(codes, codes2.at[own], 11)]
    for copy in starting + first_loads:
        copy.start()
    where.greet_all()
    codes_copy = to_core(codes_theirs, codes2.at[theirs], 10)
    codes_copy.start()
    starting[0].wait()
    grad[...] = rounded[...].astype(F32)
    gain_sums[...] = jnp.zeros_like(gain_sums)
    fill_heads(heads)
    waiting = {1: first_loads, 0: loads_of(0)}

    for layer in (1, 0):
        copies = waiting[layer]
        team = Team(
            rows,
            rounded,
            everyone,
            sums,
            tuple(team_scratch) + (team_sent.at[layer], team_got.at[layer]),
        )

        def compute(m, start):
            here = pl.ds(start, 2 * rows)
            ffn_back_rows(everyone[here, :], v_normed, w_both, w_down, gated, d_both, here)
            split_pair(
                team, m, lambda c: right_trans(d_both[here, :], w_both[c, :]), sums, team.part
            )

        def between():
            if layer == 0:
                drain_ffn(1)

            def down_step(i, carry):
                here = pl.ds(pl.multiple_of(i * 256, 256), 256)
                down_part[here, :] = left_trans(gated[:, here], everyone[...]).astype(BF)
                return carry

            def both_step(i, carry):
                here = pl.ds(pl.multiple_of(i * 256, 256), 256)
                both_part[here, :] = left_trans(v_normed[:, here], d_both[...]).astype(BF)
                return carry

            lax.fori_loop(0, down_part.shape[0] // 256, down_step, 0)
            lax.fori_loop(0, width // 256, both_step, 0)
            if layer == 1:
                for copy in waiting[0][:3]:
                    copy.start()

        def early():
            for copy in copies[:3]:
                copy.wait()
            if layer == 0:
                share_ffn(1, d_both.at[pl.ds(0, 8 * share)])
                for piece in (1, 2):
                    attention_grads(piece)

        team.run(compute, between, d_middle, early=early)
        if layer == 0:
            send_x(1, 1)
            send_x(1, 2)
        send_ffn(layer)
        copies[3].wait()

        def norm_step(i, carry):
            here = pl.ds(pl.multiple_of(i * chunk, 16), chunk)
            value = v_middle[here, :]
            back, gain_grad = norm_back(
                d_middle[here, :], value, inverse_rms(value), gain_rows[2 + layer : 3 + layer, :]
            )
            gain_sums[2 + layer : 3 + layer, :] += gain_grad[None]
            gradient = grad[here, :] + back
            d_middle[here, :] = gradient
            d_middle2[here, :] = gradient.astype(BF)
            return carry

        lax.fori_loop(0, rows // chunk, norm_step, 0)
        shared = [to_core(d_middle2.at[own], d_middle2.at[theirs], 5 * layer)]
        shared[0].start()
        for copy in copies[4:9]:
            copy.wait()

        for first in range(0, width, 256):
            columns = slice(first, first + 256)
            sums[2, :, columns] = right_trans(d_middle2[:rows, :], w_out[columns, :])

        def attention_step(i, carry):
            here = pl.ds(pl.multiple_of(i * small, small), small)
            d_attended = sums[2, here, :].astype(BF).astype(F32)
            q = v_qkv[here, :width].astype(F32)
            k = v_qkv[here, width : 2 * width].astype(F32)
            k0 = v_other[here, :width].astype(F32)
            mine, past = probabilities(q, k, k0, heads, where.place)
            d_mine = heads_summed(d_attended * v_qkv[here, 2 * width :].astype(F32), heads)
            d_past = heads_summed(d_attended * v_other[here, width:].astype(F32), heads)
            inner = mine * d_mine + past * d_past
            s_past = past * (d_past - inner) / math.sqrt(HD)
            d_scores[here, :] = s_past
            s_past = heads_spread(s_past, heads)
            d_other[here, :] = (heads_spread(past, heads) * d_attended).astype(BF)
            s_mine = heads_spread(mine * (d_mine - inner) / math.sqrt(HD), heads)
            d_qkv2[here, :width] = (s_mine * k + s_past * k0).astype(BF)
            sums[0, here, :] = s_mine * q
            sums[1, here, :] = heads_spread(mine, heads) * d_attended
            return carry

        lax.fori_loop(0, rows // small, attention_step, 0)
        exchange = [
            remote(
                source,
                target.at[layer],
                y_sent.at[2 * layer + number],
                y_got.at[2 * layer + number],
                where.index,
                1 - where.place,
            )
            for number, (source, target) in enumerate(((d_scores, s_in), (d_other, y_in)))
        ]
        for copy in exchange:
            copy.start()

        def operand_step(i, carry):
            here = pl.ds(pl.multiple_of(i * chunk, 16), chunk)
            value = v_stream[here, :]
            value = value * inverse_rms(value) * gain_rows[layer : layer + 1, :]
            for number, item, target in (
                (0, value.astype(BF).astype(F32), normed2),
                (1, v_attended[here, :].astype(F32), attended2),
            ):
                for_core[number, here, :] = own_half(item, where.core, True).astype(BF)
                target[here, :] = own_half(item, where.core, False).astype(BF)
            return carry

        lax.fori_loop(0, rows // chunk, operand_step, 0)
        shared.append(to_core(for_core.at[0], normed2.at[theirs], 5 * layer + 1))
        shared.append(to_core(for_core.at[1], attended2.at[theirs], 5 * layer + 2))
        queries, others = pl.ds(0, width), pl.ds(width, 2 * width)
        shared.append(
            to_core(d_qkv2.at[own, queries], d_qkv2.at[theirs, queries], 5 * layer + 3)
        )
        for copy in shared[1:]:
            copy.start()
        for copy in shared:
            copy.wait_recv()
        for piece in (3, 0):
            if layer == 0:
                finish_x(1, (piece,))
                wait_bytes(part.at[piece, pl.ds(0, 4 * share)], x_sent.at[4 + piece])
            attention_grads(piece)
            send_x(layer, piece)
        for copy in exchange:
            copy.wait_recv()

        def arrival_step(i, carry):
            here = pl.ds(pl.multiple_of(i * chunk, 16), chunk)
            spread = heads_spread(s_in[layer, here, :], heads)
            d_qkv2[here, width : 2 * width] = (
                sums[0, here, :] + spread * v_other[here, width:].astype(F32)
            ).astype(BF)
            d_qkv2[here, 2 * width :] = (
                sums[1, here, :] + y_in[layer, here, :].astype(F32)
            ).astype(BF)
            return carry

        lax.fori_loop(0, rows // chunk, arrival_step, 0)
        last = to_core(d_qkv2.at[own, others], d_qkv2.at[theirs, others], 5 * layer + 4)
        last.start()
        shared.append(last)
        if layer == 0:
            finish_x(1, (1, 2))
            for piece in (1, 2):
                wait_bytes(part.at[piece, pl.ds(0, 4 * share)], x_sent.at[4 + piece])
            last.wait_recv()
            for piece in (1, 2):
                attention_grads(piece)
                send_x(0, piece)
        copies[9].wait()
        for first in range(0, width, 256):
            columns = slice(first, first + 256)
            sums[2, :, columns] = right_trans(d_qkv2[:rows, :], w_qkv[columns, :])

        def stream_step(i, carry):
            here = pl.ds(pl.multiple_of(i * chunk, 16), chunk)
            value = v_stream[here, :]
            back, gain_grad = norm_back(
                sums[2, here, :], value, inverse_rms(value), gain_rows[layer : layer + 1, :]
            )
            gain_sums[layer : layer + 1, :] += gain_grad[None]
            gradient = d_middle[here, :] + back
            grad[here, :] = gradient
            rounded_to = rounded if layer == 1 else grad2
            rounded_to[here, :] = gradient.astype(BF)
            return carry

        lax.fori_loop(0, rows // chunk, stream_step, 0)
        for copy in shared:
            copy.wait_send()
        for copy in exchange:
            copy.wait_send()
        if layer == 1:
            last.wait_recv()
            for copy in waiting[0][3:]:
                copy.start()

    grad_out = load(grad, input_grad, 14)
    grad_out.start()
    grad_copy = to_core(grad2.at[own], grad2.at[theirs], 11)
    grad_copy.start()
    index = where.index

    def gain_columns(device):
        return gain_sums.at[:, pl.ds(pl.multiple_of(device // 2 * 128, 128), 128)]

    def send_gain(step, carry):
        peer = lax.rem(index + step, 16)
        remote(gain_columns(peer), gain_got.at[index], g_sent.at[0], g_got.at[0], peer).start()
        return carry

    lax.fori_loop(1, 16, send_gain, 0)
    pltpu.make_async_copy(gain_columns(index), gain_got.at[index], g_got.at[0]).start()
    grad_copy.wait()
    codes_copy.wait()
    starting[1].wait()
    vocab = codes2.shape[1] // 8

    def table_step(i, carry):
        here = pl.ds(pl.multiple_of(i * 256, 256), 256)
        d_both[here, :] = left_trans(codes2[:, here], grad2[...]).astype(BF)
        return carry

    lax.fori_loop(0, 8 * vocab // 256, table_step, 0)
    table_in = everyone.at[pl.ds(16 * share, 4 * vocab)]
    for z in range(4):
        start = pl.multiple_of((z * 2 + 1 - where.x) * vocab, vocab)
        remote(
            d_both.at[pl.ds(start, vocab)],
            table_in.at[pl.ds(z * vocab, vocab)],
            x_sent.at[8],
            x_got.at[8],
            where.x_peer,
        ).start()
    share_ffn(0, d_both.at[pl.ds(8 * vocab, 8 * share)])
    finish_x(0, (3, 0, 1, 2))
    wait_bytes(table_in, x_got.at[8])
    for z in range(4):
        start = pl.multiple_of((z * 2 + where.x) * vocab, vocab)
        here = pl.ds(z * vocab, vocab)
        table_in[here, :] = (
            table_in[here, :].astype(F32) + d_both[pl.ds(start, vocab), :].astype(F32)
        ).astype(BF)
    send_z(table_in, table_got.at[where.z], 2, vocab, vocab)

    drain_ffn(0)
    for layer in (0, 1):
        wait_bytes(both_got.at[layer, pl.ds(0, 7)], f_got.at[3 * layer + 2])
        arrived, ends = f_got.at[3 * layer + 1], (index == 0) | (index == 15)
        pl.when(ends)(lambda: wait_bytes(down_got.at[layer, 0], arrived))
        pl.when(jnp.logical_not(ends))(lambda: wait_bytes(down_got.at[layer], arrived))
        wait_bytes(attn_got.at[layer], z_got.at[layer])
        wait_bytes(everyone.at[pl.ds(0, 12 * share)], z_sent.at[layer])
    for piece in range(4):
        wait_bytes(part.at[piece, pl.ds(0, 4 * share)], x_sent.at[piece])
    wait_bytes(table_got, z_got.at[2])
    wait_bytes(everyone.at[pl.ds(0, 3 * vocab)], z_sent.at[2])
    wait_bytes(d_both.at[pl.ds(0, 4 * vocab)], x_sent.at[8])
    grad_out.wait()
    wait_bytes(gain_got, g_got.at[0])
    wait_bytes(gain_got.at[pl.ds(0, 15)], g_sent.at[0])


def backward(
    cotangent, codes, codes_theirs, gain_rows, stream, middle, qkv, other, attended, normed, qkv0,
    qkv1, outs, both, down
):
    rows, width = cotangent.shape
    hidden = down.shape[1]
    share = width // 16
    vocab = codes.shape[1] // 8
    shape = jax.ShapeDtypeStruct
    hbm = pl.BlockSpec(memory_space=pl.ANY)
    vmem = pltpu.VMEM
    dma = pltpu.SemaphoreType.DMA
    return pl.pallas_call(
        backward_kernel,
        out_shape=(
            shape((rows, width), F32),
            shape((2, 8, share, 2 * hidden), BF),
            shape((2, 8 * share, 2 * hidden), BF),
            shape((2, 2, hidden // 2, width), BF),
            shape((2, 4, 4 * share, width), BF),
            shape((4, vocab, width), BF),
            shape((16, 8, 128), F32),
        ),
        in_specs=[hbm] * 3 + in_vmem(1) + [hbm] * 11,
        out_specs=tuple([hbm] * 7),
        scratch_shapes=[
            vmem((rows, width), F32),
            vmem((rows, width), F32),
            vmem((rows, 3 * width), BF),
            vmem((rows, 2 * width), BF),
            vmem((rows, width), BF),
            vmem((8 * rows, width), BF),
            vmem((width, 3 * width), BF),
            vmem((width, width), BF),
            vmem((width, 2 * hidden), BF),
            vmem((hidden, width), BF),
            vmem((rows, width), F32),
            vmem((rows, width), F32),
            vmem((rows, width), BF),
            vmem((2 * rows, width // 2), BF),
            vmem((2 * rows, width // 2), BF),
            vmem((2 * rows, 3 * width), BF),
            vmem((2 * rows, width), BF),
            vmem((2, rows, width // 2), BF),
            vmem((rows, width), BF),
            vmem((2, rows, width), BF),
            vmem((2 * rows, 8 * vocab), BF),
            vmem((2 * rows, width), BF),
            vmem((4, width // 2, width), BF),
            vmem((16 * share, width), BF),
            vmem((8 * rows, width), BF),
            vmem((8 * rows, hidden), BF),
            vmem((8 * rows, 2 * hidden), BF),
            vmem((4, rows, width), F32),
            vmem((width, 2 * hidden), BF),
            vmem((hidden, width), BF),
            vmem((8, width), F32),
            vmem((width, 128), BF),
            dma((15,)),
            dma((12,)),
            dma((12,)),
            dma((4,)),
            dma((4,)),
            dma((9,)),
            dma((9,)),
            dma((3,)),
            dma((3,)),
            dma((6,)),
            dma((6,)),
            dma((4,)),
            dma((1,)),
            dma((1,)),
            vmem((rows, 128), F32),
            vmem((2, rows, 128), F32),
        ]
        + Team.scratch(rows, width)[:8]
        + [dma((2, Team.SCRATCH_COPIES)), dma((2, Team.SCRATCH_COPIES))],
        compiler_params=pltpu.CompilerParams(
            collective_id=4, has_side_effects=True, vmem_limit_bytes=63 * 2**20
        ),
        name="backward_pass",
    )(
        cotangent,
        codes,
        codes_theirs,
        gain_rows,
        stream,
        middle,
        qkv,
        other,
        attended,
        normed,
        qkv0,
        qkv1,
        outs,
        both,
        down,
    )


def finish_kernel(both, down, attn, table, table_grad, qkv_grad, out_grad, gate_grad, up_grad, down_grad):
    hidden = both.shape[3] // 2
    share, width = both.shape[2], attn.shape[3]
    for layer in range(LAYERS):
        for member in range(8):
            columns = slice(member * hidden, (member + 1) * hidden)
            gate_grad[layer, 0, :, columns] = both[layer, member, :, :hidden].astype(F32)
            up_grad[layer, 0, :, columns] = both[layer, member, :, hidden:].astype(F32)
        down_grad[layer, 0] = down[layer, 0].astype(F32) + down[layer, 1].astype(F32)
        for piece in range(4):
            rows = slice(piece * share, (piece + 1) * share)
            value = sum(attn[layer, z, rows, :].astype(F32) for z in range(4))
            if piece < 3:
                qkv_grad[layer, 0, :, piece * width : (piece + 1) * width] = value
            else:
                out_grad[layer, 0] = value
    table_grad[0] = sum(table[z].astype(F32) for z in range(4))


def finish(both, down, attn, table):
    share, width = both.shape[2], attn.shape[3]
    hidden = both.shape[3] // 2
    shape = jax.ShapeDtypeStruct
    return pl.pallas_call(
        finish_kernel,
        out_shape=(
            shape((1,) + table.shape[1:], F32),
            shape((LAYERS, 1, share, 3 * width), F32),
            shape((LAYERS, 1, share, width), F32),
            shape((LAYERS, 1, share, 8 * hidden), F32),
            shape((LAYERS, 1, share, 8 * hidden), F32),
            shape((LAYERS, 1, hidden // 2, width), F32),
        ),
        in_specs=in_vmem(4),
        out_specs=tuple(in_vmem(6)),
        compiler_params=pltpu.CompilerParams(vmem_limit_bytes=48 * 2**20),
        name="finish",
    )(both, down, attn, table)


class Plan:
    def __init__(self, count):
        self.count = count
        self.team = 8
        self.teams = count // self.team
        self.across = [[g * self.team + t for g in range(self.teams)] for t in range(self.team)]

    def ffn_weights(self, gate, up, down):
        rows = gate.shape[0]
        both = jnp.stack([gate, up], axis=1).reshape(rows, 2, self.teams, self.team, -1)
        parts = both.transpose(3, 0, 1, 2, 4).reshape(self.team, rows, -1)
        parts = jnp.broadcast_to(parts[None], (self.teams,) + parts.shape)
        parts = parts.reshape((self.count,) + parts.shape[2:])
        mine = lax.all_to_all(parts, "frames", split_axis=0, concat_axis=0, tiled=True)
        return mine.reshape(self.count * rows, -1), self.gather_across(down)

    def gather_across(self, rows):
        if self.teams != 2:
            return lax.all_gather(rows, "frames", axis=0, tiled=True, axis_index_groups=self.across)
        theirs = lax.ppermute(rows, "frames", self.partners())
        first = lax.axis_index("frames") < self.team
        return jnp.concatenate([jnp.where(first, rows, theirs), jnp.where(first, theirs, rows)])

    def scatter_across(self, rows):
        if self.teams != 2:
            part = lax.psum_scatter(
                rows.astype(BF),
                "frames",
                scatter_dimension=0,
                tiled=True,
                axis_index_groups=self.across,
            )
            return part.astype(F32)
        half = rows.shape[0] // 2
        first = lax.axis_index("frames") < self.team
        mine = jnp.where(first, rows[:half], rows[half:])
        sent = jnp.where(first, rows[half:], rows[:half]).astype(BF)
        return mine + lax.ppermute(sent, "frames", self.partners()).astype(F32)

    def partners(self):
        return [(i, (i + self.team) % self.count) for i in range(self.count)]

    def ffn_grads(self, both_part, down_part):
        parts = both_part.astype(BF).reshape(self.count, -1, both_part.shape[1])
        parts = lax.all_to_all(parts, "frames", split_axis=0, concat_axis=0, tiled=True)
        rows = parts.shape[1]
        parts = parts.astype(F32).reshape(self.teams, self.team, rows, -1).sum(axis=0)
        down = self.scatter_across(down_part)
        parts = parts.reshape(self.team, rows, 2, self.teams, -1)
        both = parts.transpose(1, 2, 3, 0, 4).reshape(rows, 2, -1)
        return both[:, 0], both[:, 1], down


def attend(qkv, other):
    width = HEADS * HD
    position = lax.axis_index("pos")
    q, k, v = (qkv[:, i * width : (i + 1) * width].astype(F32) for i in range(3))
    k0, v0 = (other[:, i * width : (i + 1) * width].astype(F32) for i in range(2))
    own = head_sum(q * k) / math.sqrt(HD)
    past = jnp.where(position > 0, head_sum(q * k0) / math.sqrt(HD), -1e30)
    largest = jnp.maximum(own, past)
    own, past = jnp.exp(own - largest), jnp.exp(past - largest)
    total = own + past
    own, past = own / total, past / total
    attended = head_spread(own) * v + head_spread(past) * v0
    return attended.astype(BF), own, past


def attend_back(grad, qkv, other, own, past):
    width = HEADS * HD
    q, k, v = (qkv[:, i * width : (i + 1) * width].astype(F32) for i in range(3))
    k0, v0 = (other[:, i * width : (i + 1) * width].astype(F32) for i in range(2))
    grad = grad.astype(F32)
    d_own, d_past = head_sum(grad * v), head_sum(grad * v0)
    inner = own * d_own + past * d_past
    s_own = head_spread(own * (d_own - inner) / math.sqrt(HD))
    s_past = head_spread(past * (d_past - inner) / math.sqrt(HD))
    own, past = head_spread(own), head_spread(past)
    d_q = s_own * k + s_past * k0
    d_k = s_own * q
    d_v = own * grad
    d_other = jnp.concatenate([s_past * q, past * grad], axis=1)
    return d_q, d_k, d_v, d_other


def plain_forward(
    plan, onward, frames_in, onehot, code_table, w_qkv, w_out, w_gate, w_up, w_down, gain_attn, gain_ffn
):
    width = frames_in.shape[-1]
    gains = jnp.stack([gain_attn[0, 0], gain_attn[1, 0], gain_ffn[0, 0], gain_ffn[1, 0]], axis=1)
    gains = jnp.pad(gains, ((0, 0), (0, 124)))
    full_table = lax.all_gather(code_table[0], "frames", axis=0, tiled=True)
    first_qkv = lax.all_gather(
        jnp.concatenate([w_qkv[0, 0], gains], axis=1), "frames", axis=0, tiled=True
    )
    gain_rows = first_qkv[:, 3 * width : 3 * width + 4].astype(F32).T
    qkv_all = [first_qkv[:, : 3 * width], None]
    out_all = [lax.all_gather(w_out[0, 0], "frames", axis=0, tiled=True), None]
    ffn_all = [plan.ffn_weights(w_gate[0, 0], w_up[0, 0], w_down[0, 0]), None]
    qkv_all[1] = lax.all_gather(w_qkv[1, 0], "frames", axis=0, tiled=True)
    out_all[1] = lax.all_gather(w_out[1, 0], "frames", axis=0, tiled=True)
    ffn_all[1] = plan.ffn_weights(w_gate[1, 0], w_up[1, 0], w_down[1, 0])

    stream = frames_in[:, 0].astype(F32) + plain(onehot, full_table)
    kept = []
    for layer in range(LAYERS):
        inv_attn = inverse_rms(stream)
        normed_attn = (stream * inv_attn * gain_rows[layer]).astype(BF)
        qkv = plain(normed_attn, qkv_all[layer]).astype(BF)
        other = lax.ppermute(qkv[:, width:], "pos", onward)
        attended, own, past = attend(qkv, other)
        middle = stream + plain(attended, out_all[layer])
        inv_ffn = inverse_rms(middle)
        normed_ffn = (middle * inv_ffn * gain_rows[2 + layer]).astype(BF)
        both_all, down_all = ffn_all[layer]
        team_normed, summed = ffn_forward(normed_ffn, both_all, down_all)
        new_stream = middle + summed
        kept.append(
            (
                stream,
                inv_attn,
                normed_attn,
                qkv,
                other,
                own,
                past,
                attended,
                middle,
                inv_ffn,
                team_normed,
            )
        )
        stream = new_stream
    return kept, stream, gain_rows, qkv_all, out_all, ffn_all


def fused_body(
    onehot, frames_in, code_table, w_qkv, w_out, w_gate, w_up, w_down, gain_attn, gain_ffn, cotangent
):
    share = gain_attn.shape[-1]
    width = frames_in.shape[-1]
    gains = jnp.concatenate([gain_attn[:, 0], gain_ffn[:, 0]], axis=0).astype(F32)
    gains = jnp.pad(gains, ((0, 4), (0, share)))
    odd = lax.rem(lax.axis_index("frames"), 2) == 1
    gains = jnp.where(odd, jnp.roll(gains, share, axis=1), gains)
    act, *saved = forward(
        frames_in[:, 0],
        onehot,
        gains,
        code_table[0],
        w_qkv[:, 0],
        w_out[:, 0],
        w_gate[:, 0],
        w_up[:, 0],
        w_down[:, 0],
    )
    stream, middle, qkv, other, attended, normed, gain_rows, qkv0, qkv1, outs, both, down = saved
    blocks = onehot.reshape(onehot.shape[0], 8, 2, -1)
    first, second = (blocks[:, :, i].reshape(onehot.shape[0], -1) for i in (0, 1))
    codes, codes_theirs = jnp.where(odd, second, first), jnp.where(odd, first, second)
    input_grad, both_got, pair_got, down_got, attn_got, table_got, gain_got = backward(
        cotangent[:, 0],
        codes,
        codes_theirs,
        gain_rows,
        stream,
        middle,
        qkv,
        other,
        attended,
        normed,
        qkv0,
        qkv1,
        outs,
        both,
        down,
    )
    table, qkv_grad, out_grad, gate_grad, up_grad, down_grad = finish(
        both_got, down_got, attn_got, table_got
    )
    sums = gain_got.sum(axis=0)
    sums = jnp.where(odd, sums[:4, 64:], sums[:4, :64]).reshape(2, LAYERS, 1, share)
    return (
        act[:, None, :],
        input_grad[:, None, :],
        table,
        qkv_grad,
        out_grad,
        gate_grad,
        up_grad,
        down_grad,
        sums[0],
        sums[1],
    )


def body(
    frames_in,
    code_table,
    code_ids,
    delays,
    item_lengths,
    w_qkv,
    w_out,
    w_gate,
    w_up,
    w_down,
    gain_attn,
    gain_ffn,
    cotangent,
):
    count = lax.axis_size("frames")
    plan = Plan(count)
    positions = lax.axis_size("pos")
    onward = [(i, i + 1) for i in range(positions - 1)]
    backward = [(i + 1, i) for i in range(positions - 1)]
    local_frames = frames_in.shape[0]
    item_count = item_lengths.shape[0]
    width = frames_in.shape[-1]

    neighbours = [(i, i + 1) for i in range(count - 1)]
    earlier = lax.ppermute(code_ids[local_frames - 2 :], "frames", neighbours)
    extended = jnp.concatenate([earlier, code_ids], axis=0)[:, 0]
    global_frame = lax.axis_index("frames") * local_frames + jnp.arange(
        local_frames, dtype=jnp.int32
    )
    item_ends = jnp.cumsum(item_lengths)
    starts = item_ends - item_lengths
    item_index = jnp.sum((starts[None, :] <= global_frame[:, None]).astype(jnp.int32), axis=1) - 1
    chosen = item_index[:, None] == jnp.arange(item_count, dtype=jnp.int32)[None, :]
    item_begin = jnp.sum(jnp.where(chosen, starts[None, :], 0), axis=1)
    delay_rows = jnp.sum(jnp.where(chosen, delays[:, 0][None, :], 0), axis=1)
    one_back = extended[1 : local_frames + 1]
    two_back = extended[:local_frames]
    code_rows = jnp.where(delay_rows == 1, one_back, two_back)
    is_valid = global_frame - delay_rows >= item_begin
    vocab_size = code_table.shape[1] * count
    matches = code_rows[:, None] == jnp.arange(vocab_size, dtype=jnp.int32)[None, :]
    onehot = (matches & is_valid[:, None]).astype(BF)

    if count == 16:
        return fused_body(
            onehot, frames_in, code_table, w_qkv, w_out, w_gate, w_up, w_down, gain_attn, gain_ffn,
            cotangent,
        )
    kept, stream, gain_rows, qkv_all, out_all, ffn_all = plain_forward(
        plan, onward, frames_in, onehot, code_table, w_qkv, w_out, w_gate, w_up, w_down,
        gain_attn, gain_ffn,
    )
    output = stream.astype(BF)[:, None, :]

    gradient = cotangent[:, 0].astype(F32)
    collected = [None] * LAYERS
    gain_parts = [None] * (2 * LAYERS)
    for layer in reversed(range(LAYERS)):
        (
            stream,
            inv_attn,
            normed_attn,
            qkv,
            other,
            own,
            past,
            attended,
            middle,
            inv_ffn,
            team_normed,
        ) = kept[layer]
        both_all, down_all = ffn_all[layer]
        grad_normed, both_part, down_part = ffn_backward(
            gradient.astype(BF), both_all, down_all, team_normed
        )
        ffn_shares = plan.ffn_grads(both_part, down_part)
        grad_middle, gain_parts[2 + layer] = norm_back(
            grad_normed, middle, inv_ffn, gain_rows[2 + layer]
        )
        grad_middle = gradient + grad_middle
        grad_attn = grad_middle.astype(BF)
        grad_attended = right_trans(grad_attn, out_all[layer]).astype(BF)
        d_q, d_k, d_v, d_other = attend_back(grad_attended, qkv, other, own, past)
        arrived = lax.ppermute(d_other.astype(BF), "pos", backward).astype(F32)
        grad_qkv = jnp.concatenate([d_q, d_k + arrived[:, :width], d_v + arrived[:, width:]], axis=1)
        grad_qkv = grad_qkv.astype(BF)
        out_part = left_trans(attended, grad_attn).astype(BF)
        out_share = lax.psum_scatter(out_part, "frames", scatter_dimension=0, tiled=True)
        grad_normed_attn = right_trans(grad_qkv, qkv_all[layer])
        grad_stream, gain_parts[layer] = norm_back(
            grad_normed_attn, stream, inv_attn, gain_rows[layer]
        )
        gradient = grad_middle + grad_stream
        qkv_part = left_trans(normed_attn, grad_qkv).astype(BF)
        if layer == 0:
            tail = jnp.stack(gain_parts, axis=1).astype(BF)
            qkv_part = jnp.concatenate([qkv_part, jnp.pad(tail, ((0, 0), (0, 124)))], axis=1)
        qkv_share = lax.psum_scatter(qkv_part, "frames", scatter_dimension=0, tiled=True)
        collected[layer] = (qkv_share.astype(F32), out_share.astype(F32)) + ffn_shares
    table_part = left_trans(onehot, gradient.astype(BF)).astype(BF)
    table_share = lax.psum_scatter(table_part, "frames", scatter_dimension=0, tiled=True)
    gain_shares = collected[0][0][:, 3 * width : 3 * width + 4].T
    collected[0] = (collected[0][0][:, : 3 * width],) + collected[0][1:]
    stacked = [
        jnp.stack([collected[layer][slot] for layer in range(LAYERS)], axis=0)[:, None]
        for slot in range(5)
    ]
    return (
        output,
        gradient[:, None, :],
        table_share.astype(F32)[None],
        stacked[0],
        stacked[1],
        stacked[2],
        stacked[3],
        stacked[4],
        gain_shares[:2][:, None],
        gain_shares[2:][:, None],
    )


def solution(mesh):
    return jax.shard_map(
        body,
        mesh=mesh,
        in_specs=(
            P("frames", "pos", None),
            P("pos", "frames", None),
            P("frames", "pos"),
            P(None, "pos"),
            P(),
            P(None, "pos", "frames", None),
            P(None, "pos", "frames", None),
            P(None, "pos", "frames", None),
            P(None, "pos", "frames", None),
            P(None, "pos", "frames", None),
            P(None, "pos", "frames"),
            P(None, "pos", "frames"),
            P("frames", "pos", None),
        ),
        out_specs=(
            P("frames", "pos", None),
            P("frames", "pos", None),
            P("pos", "frames", None),
            P(None, "pos", "frames", None),
            P(None, "pos", "frames", None),
            P(None, "pos", "frames", None),
            P(None, "pos", "frames", None),
            P(None, "pos", "frames", None),
            P(None, "pos", "frames"),
            P(None, "pos", "frames"),
        ),
        check_vma=False,
    )
```

```python
import math

import jax
import jax.numpy as jnp
from jax import lax
from jax.experimental import pallas as pl
from jax.experimental.pallas import tpu as pltpu
from jax.sharding import PartitionSpec as P

HEADS = 16
HD = 64
LAYERS = 2
EPSILON = 1e-06
HIGHEST = lax.Precision.HIGHEST
BF = jnp.bfloat16
F32 = jnp.float32


def plain(left, right):
    return jnp.dot(left, right, preferred_element_type=F32)


def left_trans(left, right):
    return lax.dot_general(left, right, (((0,), (0,)), ((), ())), preferred_element_type=F32)


def right_trans(left, right):
    return lax.dot_general(left, right, (((1,), (1,)), ((), ())), preferred_element_type=F32)


def inverse_rms(stream):
    return lax.rsqrt(jnp.mean(stream * stream, axis=-1, keepdims=True) + EPSILON)


def norm_back(gradient, stream, inverse, gain_row):
    scaled = gradient * gain_row
    gain_grad = jnp.sum(gradient * stream * inverse, axis=0)
    inner_sum = jnp.mean(scaled * stream, axis=-1, keepdims=True)
    return (inverse * scaled - stream * inverse * inverse * inverse * inner_sum, gain_grad)


def head_matrix():
    rows = lax.broadcasted_iota(jnp.int32, (HEADS * HD, HEADS), 0) // HD
    cols = lax.broadcasted_iota(jnp.int32, (HEADS * HD, HEADS), 1)
    return (rows == cols).astype(F32)


def head_sum(values):
    return jnp.dot(values, head_matrix(), precision=HIGHEST)


def head_spread(values):
    return jnp.dot(values, head_matrix().T, precision=HIGHEST)


MESH = pl.DeviceIdType.MESH
VMEM_LIMIT = 60 * 2**20


def in_vmem(count):
    return [pl.BlockSpec(memory_space=pltpu.VMEM)] * count


class Team:
    SCRATCH_COPIES = 19

    def __init__(self, rows, mine, everyone, sums, scratch):
        (self.part, self.from_core, self.from_across, self.from_x, self.from_z) = scratch[:5]
        (self.to_x, self.to_z, self.to_across, self.sent, self.got) = scratch[5:10]
        self.rows, self.half = rows, rows // 2
        self.mine, self.everyone, self.sums = mine, everyone, sums
        index = lax.axis_index("frames")
        self.place = lax.axis_index("pos")
        member = lax.rem(index, 8)
        self.core = lax.rem(member, 2)
        self.x = lax.rem(member // 2, 2)
        self.z = member // 4
        self.core_peer = index + 1 - 2 * self.core
        self.x_peer = index + 2 - 4 * self.x
        self.z_peer = index + 4 - 8 * self.z

    @staticmethod
    def scratch(rows, width):
        half = rows // 2
        return [
            pltpu.VMEM((4, rows, width), BF),
            pltpu.VMEM((4, rows, width), BF),
            pltpu.VMEM((2, half, width), BF),
            pltpu.VMEM((rows, width), BF),
            pltpu.VMEM((rows, width), BF),
            pltpu.VMEM((rows, width), BF),
            pltpu.VMEM((rows, width), BF),
            pltpu.VMEM((rows, width), BF),
            pltpu.SemaphoreType.DMA((Team.SCRATCH_COPIES,)),
            pltpu.SemaphoreType.DMA((Team.SCRATCH_COPIES,)),
        ]

    def greet(self):
        barrier = pltpu.get_barrier_semaphore()
        for peer in (self.core_peer, self.x_peer, self.z_peer):
            pl.semaphore_signal(barrier, inc=1, device_id=(peer, self.place), device_id_type=MESH)
        pl.semaphore_wait(barrier, 3)

    def copy(self, number, source, target, peer):
        return pltpu.make_async_remote_copy(
            src_ref=source,
            dst_ref=target,
            send_sem=self.sent.at[number],
            recv_sem=self.got.at[number],
            device_id=(peer, self.place),
            device_id_type=MESH,
        )

    def pair_start(self, m):
        x = self.x + (m % 2) * (1 - 2 * self.x)
        z = self.z + (m // 2) * (1 - 2 * self.z)
        return pl.multiple_of((z * 2 + x) * (2 * self.rows), 2 * self.rows)

    def shard(self, m, part=None, core=None):
        core = self.core if core is None else core
        start = self.pair_start(m) + core * self.rows
        size = self.rows
        if part is not None:
            start, size = start + part * self.half, self.half
        return self.everyone.at[pl.ds(pl.multiple_of(start, 16), size)]

    def gather_copies(self):
        own = self.shard(0)
        x_rows, z_rows = self.shard(1), self.shard(2)
        x_low, z_high = self.shard(1, 1), self.shard(2, 0)
        high, low = self.shard(3, 0), self.shard(3, 1)
        return [
            self.copy(0, self.mine, own, self.core_peer),
            self.copy(1, self.mine, own, self.x_peer),
            self.copy(2, self.mine, own, self.z_peer),
            self.copy(3, x_rows, x_rows, self.core_peer),
            self.copy(4, x_low, x_low, self.z_peer),
            self.copy(5, z_rows, z_rows, self.core_peer),
            self.copy(6, z_high, z_high, self.x_peer),
            self.copy(7, high, high, self.core_peer),
            self.copy(8, low, low, self.core_peer),
        ]

    def arrived(self, number):
        other = 1 - self.core
        target = [
            self.shard(0, core=other),
            self.shard(1),
            self.shard(2),
            self.shard(1, core=other),
            self.shard(3, 1),
            self.shard(2, core=other),
            self.shard(3, 0),
            self.shard(3, 0, core=other),
            self.shard(3, 1, core=other),
        ][number]
        self.copy(number, target, target, self.core_peer).wait_recv()

    def sum_copies(self):
        half = self.half
        high, low = pl.ds(0, half), pl.ds(half, half)
        copies = [
            self.copy(9 + m, self.part.at[m], self.from_core.at[m], self.core_peer)
            for m in range(4)
        ]
        copies += [
            self.copy(13, self.to_across.at[high], self.from_across.at[0], self.x_peer),
            self.copy(14, self.to_across.at[low], self.from_across.at[1], self.z_peer),
            self.copy(15, self.to_x.at[high], self.from_x.at[high], self.x_peer),
            self.copy(16, self.to_x.at[low], self.from_x.at[low], self.x_peer),
            self.copy(17, self.to_z.at[low], self.from_z.at[low], self.z_peer),
            self.copy(18, self.to_z.at[high], self.from_z.at[high], self.z_peer),
        ]
        return copies

    def run(self, compute, between, result, later=None, early=None):
        half, rows = self.half, self.rows
        gather = self.gather_copies()
        adds = self.sum_copies()
        for copy in gather[:3]:
            copy.start()
        start = self.pair_start(0) + self.core * rows
        self.everyone[pl.ds(pl.multiple_of(start, 16), rows), :] = self.mine[...]
        if early is not None:
            early()

        def total(m, first):
            return self.sums[m, first : first + half, :] + self.from_core[
                m, first : first + half, :
            ].astype(F32)

        def step(m, carry):
            @pl.when(m == 0)
            def _():
                self.arrived(0)

            @pl.when(m == 1)
            def _():
                self.arrived(1)
                gather[4].start()
                gather[3].start()
                self.arrived(2)
                gather[6].start()
                gather[5].start()
                self.arrived(3)

            @pl.when(m == 2)
            def _():
                self.arrived(5)

            @pl.when(m == 3)
            def _():
                self.arrived(6)
                gather[7].start()
                self.arrived(4)
                gather[8].start()
                self.arrived(7)
                self.arrived(8)

            compute(m, self.pair_start(m))
            self.copy(9 + m, self.part.at[m], self.from_core.at[m], self.core_peer).start()
            if later is not None:
                later(m)

            @pl.when(m == 2)
            def _():
                adds[1].wait_recv()
                self.to_x[:half, :] = total(1, 0).astype(BF)
                adds[6].start()

            return carry

        lax.fori_loop(0, 4, step, 0)
        adds[3].wait_recv()
        self.to_across[:half, :] = total(3, 0).astype(BF)
        adds[4].start()
        self.to_across[half:, :] = total(3, half).astype(BF)
        adds[5].start()
        adds[2].wait_recv()
        self.to_z[half:, :] = total(2, half).astype(BF)
        adds[8].start()
        between()
        for copy in gather:
            copy.wait_send()
        adds[5].wait_recv()
        self.to_x[half:, :] = (total(1, half) + self.from_across[1].astype(F32)).astype(BF)
        adds[7].start()
        adds[4].wait_recv()
        self.to_z[:half, :] = (total(2, 0) + self.from_across[0].astype(F32)).astype(BF)
        adds[9].start()
        adds[0].wait_recv()
        for number in (6, 7, 8, 9):
            adds[number].wait_recv()
        for first in (0, half):
            rows_here = slice(first, first + half)
            result[rows_here, :] = (
                total(0, first)
                + self.from_x[rows_here, :].astype(F32)
                + self.from_z[rows_here, :].astype(F32)
            )
        for copy in adds:
            copy.wait_send()


def split_pair(team, m, product, sums, part):
    rows = team.rows
    for first in range(0, sums.shape[2], 256):
        columns = slice(first, first + 256)
        value = product(columns)
        low, high = value[:rows], value[rows:]
        sums[m, :, columns] = jnp.where(team.core == 0, low, high)
        part[m, :, columns] = jnp.where(team.core == 0, high, low).astype(BF)


def hidden_units(block, both, hidden, first):
    gate = plain(block, both[:, first : first + 256])
    return gate, plain(block, both[:, hidden + first : hidden + first + 256])


def ffn_rows(block, both, down):
    hidden = down.shape[0]
    parts = []
    for first in range(0, hidden, 256):
        gate, up = hidden_units(block, both, hidden, first)
        parts.append((gate * jax.nn.sigmoid(gate) * up).astype(BF))
    gated = jnp.concatenate(parts, axis=1)
    return lambda columns: plain(gated, down[:, columns])


def ffn_forward_kernel(normed, both, down, everyone, result, sums, *scratch):
    rows = normed.shape[0]
    team = Team(rows, normed, everyone, sums, scratch)
    team.greet()

    def compute(m, start):
        block = everyone[pl.ds(start, 2 * rows), :]
        split_pair(team, m, ffn_rows(block, both, down), sums, team.part)

    team.run(compute, lambda: None, result)


def ffn_back_rows(block, normed, both, down, gated, d_both, here):
    hidden = down.shape[0]
    before = normed[here, :]
    for first in range(0, hidden, 256):
        columns = slice(first, first + 256)
        gate, up = hidden_units(before, both, hidden, first)
        d_gated = right_trans(block, down[columns, :])
        sig = jax.nn.sigmoid(gate)
        act = gate * sig
        gated[here, columns] = (act * up).astype(BF)
        d_both[here, columns] = (d_gated * up * sig * (1.0 + gate * (1.0 - sig))).astype(BF)
        d_both[here, hidden + first : hidden + first + 256] = (d_gated * act).astype(BF)


def ffn_backward_kernel(
    grad, both, down, normed, result, both_part, down_part, everyone, gated, d_both, sums, *scratch
):
    rows = grad.shape[0]
    team = Team(rows, grad, everyone, sums, scratch)
    team.greet()

    def compute(m, start):
        here = pl.ds(start, 2 * rows)
        ffn_back_rows(everyone[here, :], normed, both, down, gated, d_both, here)
        split_pair(team, m, lambda c: right_trans(d_both[here, :], both[c, :]), sums, team.part)

    def between():
        def down_step(i, carry):
            cols = pl.ds(pl.multiple_of(i * 256, 256), 256)
            down_part[:, cols] = left_trans(gated[...], everyone[:, cols])
            return carry

        def both_step(i, carry):
            cols = pl.ds(pl.multiple_of(i * 256, 256), 256)
            both_part[:, cols] = left_trans(normed[...], d_both[:, cols]).astype(BF)
            return carry

        lax.fori_loop(0, down_part.shape[1] // 256, down_step, 0)
        lax.fori_loop(0, both_part.shape[1] // 256, both_step, 0)

    team.run(compute, between, result)


def ffn_forward(normed, both, down):
    rows, width = normed.shape
    return pl.pallas_call(
        ffn_forward_kernel,
        out_shape=(
            jax.ShapeDtypeStruct((8 * rows, width), BF),
            jax.ShapeDtypeStruct((rows, width), F32),
        ),
        in_specs=in_vmem(3),
        out_specs=in_vmem(2),
        scratch_shapes=[pltpu.VMEM((4, rows, width), F32)] + Team.scratch(rows, width),
        compiler_params=pltpu.CompilerParams(
            collective_id=1, has_side_effects=True, vmem_limit_bytes=VMEM_LIMIT
        ),
        name="ffn_forward",
    )(normed, both, down)


def ffn_backward(grad, both, down, normed):
    rows, width = grad.shape
    hidden = down.shape[0]
    return pl.pallas_call(
        ffn_backward_kernel,
        out_shape=(
            jax.ShapeDtypeStruct((rows, width), F32),
            jax.ShapeDtypeStruct((width, 2 * hidden), BF),
            jax.ShapeDtypeStruct((hidden, width), F32),
        ),
        in_specs=in_vmem(4),
        out_specs=in_vmem(3),
        scratch_shapes=[
            pltpu.VMEM((8 * rows, width), BF),
            pltpu.VMEM((8 * rows, hidden), BF),
            pltpu.VMEM((8 * rows, 2 * hidden), BF),
            pltpu.VMEM((4, rows, width), F32),
        ]
        + Team.scratch(rows, width),
        compiler_params=pltpu.CompilerParams(
            collective_id=2, has_side_effects=True, vmem_limit_bytes=VMEM_LIMIT
        ),
        name="ffn_backward",
    )(grad, both, down, normed)


class Place:
    def __init__(self):
        self.index = lax.axis_index("frames")
        self.place = lax.axis_index("pos")
        self.core = lax.rem(self.index, 2)
        self.x = lax.rem(self.index // 2, 2)
        self.z = self.index // 4
        self.core_peer = self.index + 1 - 2 * self.core
        self.x_peer = self.index + 2 - 4 * self.x

    def greet_all(self):
        barrier = pltpu.get_barrier_semaphore()

        def signal(step, carry):
            peer = lax.rem(self.index + step, 16)
            pl.semaphore_signal(barrier, inc=1, device_id=(peer, self.place), device_id_type=MESH)
            return carry

        lax.fori_loop(1, 16, signal, 0)
        pl.semaphore_signal(
            barrier, inc=1, device_id=(self.index, 1 - self.place), device_id_type=MESH
        )
        pl.semaphore_wait(barrier, 16)


class Gather:
    def __init__(self, where, number, source, full, sent, got):
        self.where, self.source, self.full = where, source, full
        self.sent, self.got = sent.at[number], got.at[number]
        self.rows = source.shape[0]

    def shard(self, z, x, core):
        start = (z * 4 + x * 2 + core) * self.rows
        return self.full.at[pl.ds(pl.multiple_of(start, self.rows), self.rows)]

    def copy(self, source, target, sent, got, peer):
        return pltpu.make_async_remote_copy(
            src_ref=source,
            dst_ref=target,
            send_sem=self.sent.at[sent],
            recv_sem=self.got.at[got],
            device_id=(peer, self.where.place),
            device_id_type=MESH,
        )

    def z_copy(self, z, up, own=False):
        w = self.where
        target = self.shard(z, w.x, w.core)
        source = self.source if own else target
        if up:
            return self.copy(source, target, z, z, jnp.minimum(w.index + 4, 15))
        return self.copy(source, target, 4 + z, z, jnp.maximum(w.index - 4, 0))

    def x_copy(self, z, own=False):
        w = self.where
        target = self.shard(z, w.x, w.core)
        return self.copy(self.source if own else target, target, 8 + z, 4 + z, w.x_peer)

    def core_copy(self, z, other_x, own=False):
        w = self.where
        x = 1 - w.x if other_x else w.x
        target = self.shard(z, x, w.core)
        number = z * 2 + other_x
        return self.copy(
            self.source if own else target, target, 12 + number, 8 + number, w.core_peer
        )

    def local(self):
        w = self.where
        return pltpu.make_async_copy(
            self.source, self.shard(w.z, w.x, w.core), self.got.at[w.z]
        )

    def start(self):
        w = self.where
        pl.when(w.z < 3)(lambda: self.z_copy(w.z, True, True).start())
        pl.when(w.z > 0)(lambda: self.z_copy(w.z, False, True).start())
        self.x_copy(w.z, True).start()
        self.core_copy(w.z, 0, True).start()
        self.local().start()

    def pass_z(self, distance):
        w = self.where

        @pl.when(w.z >= distance)
        def _():
            z = w.z - distance
            self.z_copy(z, True).wait_recv()
            pl.when(w.z < 3)(lambda: self.z_copy(z, True).start())
            self.x_copy(z).start()
            self.core_copy(z, 0).start()

        @pl.when(w.z + distance <= 3)
        def _():
            z = w.z + distance
            self.z_copy(z, False).wait_recv()
            pl.when(w.z > 0)(lambda: self.z_copy(z, False).start())
            self.x_copy(z).start()
            self.core_copy(z, 0).start()

    def pass_x(self):
        w = self.where

        def hand(z):
            target = self.shard(z, 1 - w.x, w.core)
            self.copy(target, target, 8 + z, 4 + z, w.x_peer).wait_recv()
            self.core_copy(z, 1).start()

        hand(w.z)
        for distance in (1, 2, 3):
            pl.when(w.z >= distance)(lambda: hand(w.z - distance))
            pl.when(w.z + distance <= 3)(lambda: hand(w.z + distance))

    def finish(self):
        w = self.where
        for z in range(4):
            for other_x in (0, 1):
                x = 1 - w.x if other_x else w.x
                target = self.shard(z, x, 1 - w.core)
                number = z * 2 + other_x
                self.copy(target, target, 12 + number, 8 + number, w.core_peer).wait_recv()
        self.local().wait()

    def drain(self):
        w = self.where
        for z in range(4):
            pl.when((z <= w.z) & (w.z < 3))(lambda: self.z_copy(z, True).wait_send())
            pl.when((z >= w.z) & (w.z > 0))(lambda: self.z_copy(z, False).wait_send())
            self.x_copy(z).wait_send()
            self.core_copy(z, 0).wait_send()
            self.core_copy(z, 1).wait_send()


class Slices:
    def __init__(self, where, layer, gate, up, down, both, down_all, sent, got):
        self.where, self.both, self.down_all = where, both.at[layer], down_all.at[layer]
        self.gate, self.up, self.down = gate.at[layer], up.at[layer], down.at[layer]
        self.sent, self.got = sent.at[layer], got.at[layer]
        self.rows = self.gate.shape[0]
        self.hidden = self.down_all.shape[0]

    def piece(self, source, side, member):
        here = pl.ds(pl.multiple_of(self.where.index * self.rows, self.rows), self.rows)
        columns = pl.ds(pl.multiple_of(member * self.hidden, self.hidden), self.hidden)
        return source.at[:, columns], self.both.at[
            here, side * self.hidden : (side + 1) * self.hidden
        ]

    def remote(self, source, target, number, peer):
        return pltpu.make_async_remote_copy(
            src_ref=source,
            dst_ref=target,
            send_sem=self.sent.at[number],
            recv_sem=self.got.at[number],
            device_id=(peer, self.where.place),
            device_id_type=MESH,
        )

    def down_target(self):
        half = self.hidden // 2
        start = lax.rem(self.where.index, 2) * half
        return self.down_all.at[pl.ds(pl.multiple_of(start, half), half)]

    def start(self):
        index = self.where.index
        base = index - lax.rem(index, 8)

        def send(step, carry):
            member = lax.rem(index + step, 8)
            for side, source in ((0, self.gate), (1, self.up)):
                part, target = self.piece(source, side, member)
                self.remote(part, target, 0, base + member).start()
            return carry

        lax.fori_loop(1, 8, send, 0)
        for side, source in ((0, self.gate), (1, self.up)):
            part, target = self.piece(source, side, lax.rem(index, 8))
            pltpu.make_async_copy(part, target, self.got.at[0]).start()
        for team in (0, 1):
            peer = team * 8 + index // 2

            @pl.when(peer != index)
            def _():
                self.remote(self.down, self.down_target(), 1, peer).start()

            @pl.when(peer == index)
            def _():
                pltpu.make_async_copy(self.down, self.down_target(), self.got.at[1]).start()

    def team_rows(self, team):
        size = 8 * self.rows
        return self.both.at[pl.ds(pl.multiple_of(team * size, size), size)]

    def swap(self):
        mine = self.team_rows(self.where.index // 8)
        return self.remote(mine, mine, 2, lax.rem(self.where.index + 8, 16))

    def pass_on(self):
        mine = self.team_rows(self.where.index // 8)
        pltpu.make_async_copy(mine, mine, self.got.at[0]).wait()
        self.swap().start()

    def finish(self):
        theirs = self.team_rows(1 - self.where.index // 8)
        pltpu.make_async_copy(theirs, theirs, self.got.at[2]).wait()
        pltpu.make_async_copy(self.down_all, self.down_all, self.got.at[1]).wait()

    def drain(self):
        index = self.where.index
        most = self.both.at[pl.ds(0, 7 * self.rows)]
        pltpu.make_async_copy(most, most, self.sent.at[0]).wait()
        self.swap().wait_send()
        ends = (index == 0) | (index == 15)
        half = self.down_all.at[pl.ds(0, self.hidden // 2)]

        @pl.when(ends)
        def _():
            pltpu.make_async_copy(half, half, self.sent.at[1]).wait()

        @pl.when(jnp.logical_not(ends))
        def _():
            pltpu.make_async_copy(self.down_all, self.down_all, self.sent.at[1]).wait()


def two_parts(values):
    high = values.astype(BF)
    return high, (values - high.astype(F32)).astype(BF)


def heads_summed(values, heads):
    high, low = two_parts(values)
    return plain(high, heads[...]) + plain(low, heads[...])


def heads_spread(values, heads):
    high, low = two_parts(values)
    return right_trans(high, heads[...]) + right_trans(low, heads[...])


def fill_heads(heads):
    rows = lax.broadcasted_iota(jnp.int32, heads.shape, 0) // HD
    columns = lax.broadcasted_iota(jnp.int32, heads.shape, 1)
    heads[...] = jnp.where(rows == columns, 1.0, 0.0).astype(BF)


def probabilities(q, k, k0, heads, place):
    own = heads_summed(q * k, heads) / math.sqrt(HD)
    past = jnp.where(place > 0, heads_summed(q * k0, heads) / math.sqrt(HD), -1e30)
    return softmax_pair(own, past)


def softmax_pair(own, past):
    largest = jnp.maximum(own, past)
    own, past = jnp.exp(own - largest), jnp.exp(past - largest)
    total = own + past
    return own / total, past / total


def forward_kernel(
    frames, onehot, gain_shard, table, qkv0, qkv1, out0, out1, gate, up, down, *refs
):
    (act, stream, middle, qkv, other, attended, everyone, gain_rows) = refs[:8]
    (qkv0_out, qkv1_out, outs_out, both_out, down_out) = refs[8:13]
    (gains, table_all, qkv0_all, qkv1_all, outs_all, both, down_all) = refs[13:20]
    (heads, normed, result, sums, gather_sent, gather_got, slice_sent, slice_got) = refs[20:28]
    (y_sent, y_got, saved, scores, scores_in) = refs[28:33]
    team_scratch = refs[33:41]
    team_sent, team_got = refs[41:43]
    rows, width = frames.shape
    where = Place()

    def gather(number, source, full):
        return Gather(where, number, source, full, gather_sent, gather_got)

    gain_gather = gather(0, gain_shard, gains)
    table_gather = gather(1, table, table_all)
    qkv_gathers = [gather(2, qkv0, qkv0_all), gather(3, qkv1, qkv1_all)]
    out_gathers = [gather(4, out0, outs_all.at[0]), gather(5, out1, outs_all.at[1])]
    slices = [
        Slices(where, layer, gate, up, down, both, down_all, slice_sent, slice_got)
        for layer in range(LAYERS)
    ]
    where.greet_all()
    for item in (gain_gather, table_gather, qkv_gathers[0], out_gathers[0]):
        item.start()
    slices[0].start()
    fill_heads(heads)
    first = (gain_gather, table_gather, qkv_gathers[0], out_gathers[0])
    for item in first:
        for distance in (1, 2, 3):
            item.pass_z(distance)
    slices[0].pass_on()
    for item in first:
        item.pass_x()
    gain_gather.finish()
    for block in range(8):
        first, second = block * 16, block * 16 + 8
        gain_rows[:, block * 128 : (block + 1) * 128] = (
            gains[first : first + 8, :] + gains[second : second + 8, :]
        )
    table_gather.finish()
    for first in range(0, width, 256):
        columns = slice(first, first + 256)
        stream[0, :, columns] = frames[:, columns].astype(F32) + plain(
            onehot[...], table_all[:, columns]
        )
    saves = []
    second = (qkv_gathers[1], out_gathers[1])

    def save(source, target, number):
        copy = pltpu.make_async_copy(source, target, saved.at[number])
        copy.start()
        saves.append(copy)

    for layer in range(LAYERS):
        value = stream[layer]
        normed[...] = (value * inverse_rms(value) * gain_rows[layer : layer + 1, :]).astype(BF)
        qkv_gathers[layer].finish()
        weights = (qkv0_all, qkv1_all)[layer]
        if layer == 0:
            for item in second:
                item.start()
        save(weights, (qkv0_out, qkv1_out)[layer], layer)
        def to_other(source, target, number):
            return pltpu.make_async_remote_copy(
                src_ref=source,
                dst_ref=target,
                send_sem=y_sent.at[3 * layer + number],
                recv_sem=y_got.at[3 * layer + number],
                device_id=(where.index, 1 - where.place),
                device_id_type=MESH,
            )

        first = pl.multiple_of(2 * width * (1 - where.place), 128)
        exchange = [
            to_other(
                qkv.at[layer, :, pl.ds(first, width)], other.at[layer, :, pl.ds(width, width)], 0
            ),
            to_other(scores, scores_in.at[layer], 1),
            to_other(
                qkv.at[layer, :, pl.ds(width, width)], other.at[layer, :, pl.ds(0, width)], 2
            ),
        ]
        for first in list(range(0, width, 512)) + list(range(2 * width, 3 * width, 512)):
            columns = slice(first, first + 512)
            qkv[layer, :, columns] = plain(normed[...], weights[:, columns]).astype(BF)
        exchange[0].start()
        for first in range(width, 2 * width, 512):
            columns = slice(first, first + 512)
            qkv[layer, :, columns] = plain(normed[...], weights[:, columns]).astype(BF)
        if layer == 0:
            slices[1].start()
        k = qkv[layer, :, width : 2 * width].astype(F32)
        own = heads_summed(qkv[layer, :, :width].astype(F32) * k, heads) / math.sqrt(HD)
        exchange[0].wait_recv()
        scores[...] = heads_summed(other[layer, :, width:].astype(F32) * k, heads)
        exchange[1].start()
        exchange[2].start()
        exchange[1].wait_recv()
        past = jnp.where(where.place > 0, scores_in[layer] / math.sqrt(HD), -1e30)
        own, past = softmax_pair(own, past)
        attended[layer] = (
            heads_spread(own, heads) * qkv[layer, :, 2 * width :].astype(F32)
            + heads_spread(past, heads) * other[layer, :, width:].astype(F32)
        ).astype(BF)
        out_gathers[layer].finish()
        for first in range(0, width, 512):
            columns = slice(first, first + 512)
            middle[layer, :, columns] = stream[layer, :, columns] + plain(
                attended[layer], outs_all[layer, :, columns]
            )
        value = middle[layer]
        normed[...] = (value * inverse_rms(value) * gain_rows[2 + layer : 3 + layer, :]).astype(BF)
        if layer == 0:
            for item in second:
                item.pass_z(1)
        slices[layer].finish()
        save(both.at[layer], both_out.at[layer], 2 + layer)
        save(down_all.at[layer], down_out.at[layer], 4 + layer)
        team = Team(
            rows,
            normed,
            everyone.at[layer],
            sums,
            tuple(team_scratch) + (team_sent.at[layer], team_got.at[layer]),
        )

        def compute(m, start):
            block = everyone[layer, pl.ds(start, 2 * rows), :]
            rows_out = ffn_rows(block, both.at[layer], down_all.at[layer])
            split_pair(team, m, rows_out, sums, team.part)

        later = None
        if layer == 0:

            def later(m):
                pl.when(m == 1)(lambda: slices[1].pass_on())
                for step in (2, 3):

                    @pl.when(m == step)
                    def _():
                        for item in second:
                            item.pass_z(step)

        def between():
            if layer == 0:
                for item in second:
                    item.pass_x()

        team.run(compute, lambda: None, result, later)
        between()
        if layer == 0:
            stream[1] = middle[0] + result[...]
        else:
            act[...] = (middle[1] + result[...]).astype(BF)
        exchange[2].wait_recv()
        for copy in exchange:
            copy.wait_send()
    save(outs_all, outs_out, 6)
    for item in [gain_gather, table_gather] + qkv_gathers + out_gathers + slices:
        item.drain()
    for copy in saves:
        copy.wait()


def forward(frames, onehot, gain_shard, table, w_qkv, w_out, gate, up, down):
    rows, width = frames.shape
    hidden = gate.shape[2] // 8
    vocab = table.shape[0] * 16
    shape = jax.ShapeDtypeStruct
    hbm = pl.BlockSpec(memory_space=pl.ANY)
    return pl.pallas_call(
        forward_kernel,
        out_shape=(
            shape((rows, width), BF),
            shape((2, rows, width), F32),
            shape((2, rows, width), F32),
            shape((2, rows, 3 * width), BF),
            shape((2, rows, 2 * width), BF),
            shape((2, rows, width), BF),
            shape((2, 8 * rows, width), BF),
            shape((8, width), F32),
            shape((width, 3 * width), BF),
            shape((width, 3 * width), BF),
            shape((2, width, width), BF),
            shape((2, width, 2 * hidden), BF),
            shape((2, hidden, width), BF),
        ),
        in_specs=in_vmem(2) + [hbm] * 9,
        out_specs=tuple(in_vmem(8) + [hbm] * 5),
        scratch_shapes=[
            pltpu.VMEM((8 * 16, 128), F32),
            pltpu.VMEM((vocab, width), BF),
            pltpu.VMEM((width, 3 * width), BF),
            pltpu.VMEM((width, 3 * width), BF),
            pltpu.VMEM((2, width, width), BF),
            pltpu.VMEM((2, width, 2 * hidden), BF),
            pltpu.VMEM((2, hidden, width), BF),
            pltpu.VMEM((width, 128), BF),
            pltpu.VMEM((rows, width), BF),
            pltpu.VMEM((rows, width), F32),
            pltpu.VMEM((4, rows, width), F32),
            pltpu.SemaphoreType.DMA((6, 20)),
            pltpu.SemaphoreType.DMA((6, 16)),
            pltpu.SemaphoreType.DMA((2, 3)),
            pltpu.SemaphoreType.DMA((2, 3)),
            pltpu.SemaphoreType.DMA((6,)),
            pltpu.SemaphoreType.DMA((6,)),
            pltpu.SemaphoreType.DMA((7,)),
            pltpu.VMEM((rows, 128), F32),
            pltpu.VMEM((2, rows, 128), F32),
        ]
        + Team.scratch(rows, width)[:8]
        + [
            pltpu.SemaphoreType.DMA((2, Team.SCRATCH_COPIES)),
            pltpu.SemaphoreType.DMA((2, Team.SCRATCH_COPIES)),
        ],
        compiler_params=pltpu.CompilerParams(
            collective_id=3, has_side_effects=True, vmem_limit_bytes=63 * 2**20
        ),
        name="forward_pass",
    )(
        frames,
        onehot,
        gain_shard,
        table,
        w_qkv[0],
        w_qkv[1],
        w_out[0],
        w_out[1],
        gate,
        up,
        down,
    )


def own_half(values, core, other):
    rows, width = values.shape
    parts = []
    for first in range(0, width, 256):
        low, high = values[:, first : first + 128], values[:, first + 128 : first + 256]
        lane = lax.broadcasted_iota(jnp.int32, low.shape, 1)
        even = jnp.where(lane < 64, low, pltpu.roll(high, 64, 1))
        odd = jnp.where(lane < 64, pltpu.roll(low, 64, 1), high)
        first_core = (core == 0) != other
        parts.append(jnp.where(first_core, even, odd))
    return jnp.concatenate(parts, axis=1)


def backward_kernel(
    cotangent, codes, codes_theirs, gain_rows, stream, middle, qkv, other, attended, normed, qkv0,
    qkv1, outs, both, down, *refs
):
    (input_grad, both_got, pair_got, down_got, attn_got, table_got, gain_got) = refs[:7]
    refs = refs[1:]
    (v_stream, v_middle, v_qkv, v_other, v_attended, v_normed, w_qkv, w_out, w_both, w_down) = refs[
        6:16
    ]
    (grad, d_middle, rounded, normed2, attended2, d_qkv2, d_middle2, for_core, d_other, y_in) = refs[
        16:26
    ]
    (codes2, grad2, part, from_x, everyone, gated, d_both, sums, both_part, down_part) = refs[26:36]
    (gain_sums, heads, loaded, core_sent, core_got, y_sent, y_got, x_sent, x_got) = refs[36:45]
    (z_sent, z_got, f_sent, f_got, f_kept, g_sent, g_got, d_scores, s_in) = refs[45:54]
    team_scratch = refs[54:62]
    team_sent, team_got = refs[62:64]
    rows, width = cotangent.shape
    share = both_part.shape[0] // 16
    where = Place()
    own, theirs = pl.ds(0, rows), pl.ds(rows, rows)
    chunk, small = rows // 2, 32

    def load(source, target, number):
        return pltpu.make_async_copy(source, target, loaded.at[number])

    def loads_of(layer):
        return [
            load(normed.at[layer], v_normed, 0),
            load(both.at[layer], w_both, 1),
            load(down.at[layer], w_down, 2),
            load(middle.at[layer], v_middle, 3),
            load(outs.at[layer], w_out, 4),
            load(qkv.at[layer], v_qkv, 5),
            load(other.at[layer], v_other, 6),
            load(stream.at[layer], v_stream, 7),
            load(attended.at[layer], v_attended, 8),
            load((qkv0, qkv1)[layer], w_qkv, 9),
        ]

    def remote(source, target, sent, got, peer, place=None):
        return pltpu.make_async_remote_copy(
            src_ref=source,
            dst_ref=target,
            send_sem=sent,
            recv_sem=got,
            device_id=(peer, where.place if place is None else place),
            device_id_type=MESH,
        )

    def wait_bytes(like, semaphore):
        pltpu.make_async_copy(like, like, semaphore).wait()

    def to_core(source, target, number):
        return remote(source, target, core_sent.at[number], core_got.at[number], where.core_peer)

    def team_rows(ref, team):
        return ref.at[pl.ds(pl.multiple_of(team * 8 * share, 8 * share), 8 * share)]

    def swap(layer):
        team = where.index // 8
        return remote(
            team_rows(both_part, 1 - team),
            pair_got.at[layer],
            f_sent.at[3 * layer],
            f_got.at[3 * layer],
            lax.rem(where.index + 8, 16),
        )

    def share_ffn(layer, spare):
        index = where.index
        team, member = index // 8, lax.rem(index, 8)
        swap(layer).wait_recv()
        fetch = load(pair_got.at[layer], spare, 12 + layer)
        fetch.start()
        fetch.wait()
        start = pl.multiple_of(team * 8 * share, 8 * share)

        def add(i, carry):
            first = pl.multiple_of(i * 32, 32)
            here = pl.ds(pl.multiple_of(start + first, 32), 32)
            both_part[here, :] = (
                both_part[here, :].astype(F32) + spare[pl.ds(first, 32), :].astype(F32)
            ).astype(BF)
            return carry

        lax.fori_loop(0, 8 * share // 32, add, 0)

        def piece(owner):
            first = pl.multiple_of(start + owner * share, share)
            return both_part.at[pl.ds(first, share)]

        def send(step, carry):
            owner = lax.rem(member + step, 8)
            remote(
                piece(owner),
                both_got.at[layer, member],
                f_sent.at[3 * layer + 2],
                f_got.at[3 * layer + 2],
                team * 8 + owner,
            ).start()
            return carry

        lax.fori_loop(1, 8, send, 0)
        pltpu.make_async_copy(
            piece(member), both_got.at[layer, member], f_kept.at[2 * layer]
        ).start()

    def send_ffn(layer):
        index = where.index
        swap(layer).start()
        half = down_part.shape[0] // 2
        for side in (0, 1):
            owner = 2 * lax.rem(index, 8) + side
            piece = down_part.at[pl.ds(side * half, half)]
            target = down_got.at[layer, index // 8]

            @pl.when(owner != index)
            def _():
                remote(
                    piece, target, f_sent.at[3 * layer + 1], f_got.at[3 * layer + 1], owner
                ).start()

            @pl.when(owner == index)
            def _():
                pltpu.make_async_copy(piece, target, f_kept.at[2 * layer + 1]).start()

    def drain_ffn(layer):
        index = where.index
        swap(layer).wait_send()
        wait_bytes(both_part.at[pl.ds(0, 7 * share)], f_sent.at[3 * layer + 2])
        wait_bytes(both_part.at[pl.ds(0, share)], f_kept.at[2 * layer])
        ends = (index == 0) | (index == 15)
        half = down_part.shape[0] // 2
        semaphore = f_sent.at[3 * layer + 1]

        @pl.when(ends)
        def _():
            wait_bytes(down_part.at[pl.ds(0, half)], semaphore)
            wait_bytes(down_part.at[pl.ds(0, half)], f_kept.at[2 * layer + 1])

        @pl.when(jnp.logical_not(ends))
        def _():
            wait_bytes(down_part, semaphore)

    def landing(layer):
        return from_x if layer == 1 else everyone.at[pl.ds(0, 16 * share)]

    def send_x(layer, piece):
        for z in range(4):
            start = (z * 2 + 1 - where.x) * share
            remote(
                part.at[piece, pl.ds(pl.multiple_of(start, share), share)],
                landing(layer).at[pl.ds((z * 4 + piece) * share, share)],
                x_sent.at[4 * layer + piece],
                x_got.at[4 * layer + piece],
                where.x_peer,
            ).start()

    def attention_grads(piece):
        def step(i, carry):
            here = pl.ds(pl.multiple_of(i * 256, 256), 256)
            if piece < 3:
                right = d_qkv2[:, piece * width : (piece + 1) * width]
                value = left_trans(normed2[:, here], right)
            else:
                value = left_trans(attended2[:, here], d_middle2[...])
            part[piece, here, :] = value.astype(BF)
            return carry

        lax.fori_loop(0, normed2.shape[1] // 256, step, 0)

    def send_z(source, target, number, size, stride, first=0):
        for z in range(4):
            piece = source.at[pl.ds(z * stride + first, size)]
            peer = z * 4 + where.x * 2 + where.core

            @pl.when(where.z != z)
            def _():
                remote(piece, target, z_sent.at[number], z_got.at[number], peer).start()

            @pl.when(where.z == z)
            def _():
                pltpu.make_async_copy(piece, target, z_got.at[number]).start()

    def finish_x(layer, pieces):
        arrived = landing(layer)
        for piece in pieces:
            wait_bytes(arrived.at[pl.ds(0, 4 * share)], x_got.at[4 * layer + piece])
            for z in range(4):
                start = pl.multiple_of((z * 2 + where.x) * share, share)
                here = pl.ds((z * 4 + piece) * share, share)
                arrived[here, :] = (
                    arrived[here, :].astype(F32)
                    + part[piece, pl.ds(start, share), :].astype(F32)
                ).astype(BF)
            target = attn_got.at[layer, where.z, pl.ds(piece * share, share)]
            send_z(arrived, target, layer, share, 4 * share, piece * share)

    first_loads = loads_of(1)
    starting = [load(cotangent, rounded, 10), load(codes, codes2.at[own], 11)]
    for copy in starting + first_loads:
        copy.start()
    where.greet_all()
    codes_copy = to_core(codes_theirs, codes2.at[theirs], 10)
    codes_copy.start()
    starting[0].wait()
    grad[...] = rounded[...].astype(F32)
    gain_sums[...] = jnp.zeros_like(gain_sums)
    fill_heads(heads)
    waiting = {1: first_loads, 0: loads_of(0)}

    for layer in (1, 0):
        copies = waiting[layer]
        team = Team(
            rows,
            rounded,
            everyone,
            sums,
            tuple(team_scratch) + (team_sent.at[layer], team_got.at[layer]),
        )

        def compute(m, start):
            here = pl.ds(start, 2 * rows)
            ffn_back_rows(everyone[here, :], v_normed, w_both, w_down, gated, d_both, here)
            split_pair(
                team, m, lambda c: right_trans(d_both[here, :], w_both[c, :]), sums, team.part
            )

        def between():
            if layer == 0:
                drain_ffn(1)

            def down_step(i, carry):
                here = pl.ds(pl.multiple_of(i * 256, 256), 256)
                down_part[here, :] = left_trans(gated[:, here], everyone[...]).astype(BF)
                return carry

            def both_step(i, carry):
                here = pl.ds(pl.multiple_of(i * 256, 256), 256)
                both_part[here, :] = left_trans(v_normed[:, here], d_both[...]).astype(BF)
                return carry

            lax.fori_loop(0, down_part.shape[0] // 256, down_step, 0)
            lax.fori_loop(0, width // 256, both_step, 0)
            if layer == 1:
                for copy in waiting[0][:3]:
                    copy.start()

        def early():
            for copy in copies[:3]:
                copy.wait()
            if layer == 0:
                share_ffn(1, d_both.at[pl.ds(0, 8 * share)])
                for piece in (1, 2):
                    attention_grads(piece)

        team.run(compute, between, d_middle, early=early)
        if layer == 0:
            send_x(1, 1)
            send_x(1, 2)
        copies[3].wait()

        def norm_step(i, carry):
            here = pl.ds(pl.multiple_of(i * chunk, 16), chunk)
            value = v_middle[here, :]
            back, gain_grad = norm_back(
                d_middle[here, :], value, inverse_rms(value), gain_rows[2 + layer : 3 + layer, :]
            )
            gain_sums[2 + layer : 3 + layer, :] += gain_grad[None]
            gradient = grad[here, :] + back
            d_middle[here, :] = gradient
            d_middle2[here, :] = gradient.astype(BF)
            return carry

        lax.fori_loop(0, rows // chunk, norm_step, 0)
        shared = [to_core(d_middle2.at[own], d_middle2.at[theirs], 5 * layer)]
        shared[0].start()
        for copy in copies[4:9]:
            copy.wait()

        for first in range(0, width, 256):
            columns = slice(first, first + 256)
            sums[2, :, columns] = right_trans(d_middle2[:rows, :], w_out[columns, :])

        def attention_step(i, carry):
            here = pl.ds(pl.multiple_of(i * small, small), small)
            d_attended = sums[2, here, :].astype(BF).astype(F32)
            q = v_qkv[here, :width].astype(F32)
            k = v_qkv[here, width : 2 * width].astype(F32)
            k0 = v_other[here, :width].astype(F32)
            mine, past = probabilities(q, k, k0, heads, where.place)
            d_mine = heads_summed(d_attended * v_qkv[here, 2 * width :].astype(F32), heads)
            d_past = heads_summed(d_attended * v_other[here, width:].astype(F32), heads)
            inner = mine * d_mine + past * d_past
            s_past = past * (d_past - inner) / math.sqrt(HD)
            d_scores[here, :] = s_past
            s_past = heads_spread(s_past, heads)
            d_other[here, :] = (heads_spread(past, heads) * d_attended).astype(BF)
            s_mine = heads_spread(mine * (d_mine - inner) / math.sqrt(HD), heads)
            d_qkv2[here, :width] = (s_mine * k + s_past * k0).astype(BF)
            sums[0, here, :] = s_mine * q
            sums[1, here, :] = heads_spread(mine, heads) * d_attended
            return carry

        lax.fori_loop(0, rows // small, attention_step, 0)
        exchange = [
            remote(
                source,
                target.at[layer],
                y_sent.at[2 * layer + number],
                y_got.at[2 * layer + number],
                where.index,
                1 - where.place,
            )
            for number, (source, target) in enumerate(((d_scores, s_in), (d_other, y_in)))
        ]
        for copy in exchange:
            copy.start()
        send_ffn(layer)

        def operand_step(i, carry):
            here = pl.ds(pl.multiple_of(i * chunk, 16), chunk)
            value = v_stream[here, :]
            value = value * inverse_rms(value) * gain_rows[layer : layer + 1, :]
            for number, item, target in (
                (0, value.astype(BF).astype(F32), normed2),
                (1, v_attended[here, :].astype(F32), attended2),
            ):
                for_core[number, here, :] = own_half(item, where.core, True).astype(BF)
                target[here, :] = own_half(item, where.core, False).astype(BF)
            return carry

        lax.fori_loop(0, rows // chunk, operand_step, 0)
        shared.append(to_core(for_core.at[0], normed2.at[theirs], 5 * layer + 1))
        shared.append(to_core(for_core.at[1], attended2.at[theirs], 5 * layer + 2))
        queries, others = pl.ds(0, width), pl.ds(width, 2 * width)
        shared.append(
            to_core(d_qkv2.at[own, queries], d_qkv2.at[theirs, queries], 5 * layer + 3)
        )
        for copy in shared[1:]:
            copy.start()
        for copy in shared:
            copy.wait_recv()
        for piece in (3, 0):
            if layer == 0:
                finish_x(1, (piece,))
                wait_bytes(part.at[piece, pl.ds(0, 4 * share)], x_sent.at[4 + piece])
            attention_grads(piece)
            send_x(layer, piece)
        for copy in exchange:
            copy.wait_recv()

        def arrival_step(i, carry):
            here = pl.ds(pl.multiple_of(i * chunk, 16), chunk)
            spread = heads_spread(s_in[layer, here, :], heads)
            d_qkv2[here, width : 2 * width] = (
                sums[0, here, :] + spread * v_other[here, width:].astype(F32)
            ).astype(BF)
            d_qkv2[here, 2 * width :] = (
                sums[1, here, :] + y_in[layer, here, :].astype(F32)
            ).astype(BF)
            return carry

        lax.fori_loop(0, rows // chunk, arrival_step, 0)
        last = to_core(d_qkv2.at[own, others], d_qkv2.at[theirs, others], 5 * layer + 4)
        last.start()
        shared.append(last)
        if layer == 0:
            finish_x(1, (1, 2))
            for piece in (1, 2):
                wait_bytes(part.at[piece, pl.ds(0, 4 * share)], x_sent.at[4 + piece])
            last.wait_recv()
            for piece in (1, 2):
                attention_grads(piece)
                send_x(0, piece)
        copies[9].wait()
        for first in range(0, width, 256):
            columns = slice(first, first + 256)
            sums[2, :, columns] = right_trans(d_qkv2[:rows, :], w_qkv[columns, :])

        def stream_step(i, carry):
            here = pl.ds(pl.multiple_of(i * chunk, 16), chunk)
            value = v_stream[here, :]
            back, gain_grad = norm_back(
                sums[2, here, :], value, inverse_rms(value), gain_rows[layer : layer + 1, :]
            )
            gain_sums[layer : layer + 1, :] += gain_grad[None]
            gradient = d_middle[here, :] + back
            grad[here, :] = gradient
            rounded_to = rounded if layer == 1 else grad2
            rounded_to[here, :] = gradient.astype(BF)
            return carry

        lax.fori_loop(0, rows // chunk, stream_step, 0)
        for copy in shared:
            copy.wait_send()
        for copy in exchange:
            copy.wait_send()
        if layer == 1:
            last.wait_recv()
            for copy in waiting[0][3:]:
                copy.start()

    grad_out = load(grad, input_grad, 14)
    grad_out.start()
    grad_copy = to_core(grad2.at[own], grad2.at[theirs], 11)
    grad_copy.start()
    index = where.index

    def gain_columns(device):
        return gain_sums.at[:, pl.ds(pl.multiple_of(device // 2 * 128, 128), 128)]

    def send_gain(step, carry):
        peer = lax.rem(index + step, 16)
        remote(gain_columns(peer), gain_got.at[index], g_sent.at[0], g_got.at[0], peer).start()
        return carry

    lax.fori_loop(1, 16, send_gain, 0)
    pltpu.make_async_copy(gain_columns(index), gain_got.at[index], g_got.at[0]).start()
    grad_copy.wait()
    codes_copy.wait()
    starting[1].wait()
    vocab = codes2.shape[1] // 8

    def table_step(i, carry):
        here = pl.ds(pl.multiple_of(i * 256, 256), 256)
        d_both[here, :] = left_trans(codes2[:, here], grad2[...]).astype(BF)
        return carry

    lax.fori_loop(0, 8 * vocab // 256, table_step, 0)
    table_in = everyone.at[pl.ds(16 * share, 4 * vocab)]
    for z in range(4):
        start = pl.multiple_of((z * 2 + 1 - where.x) * vocab, vocab)
        remote(
            d_both.at[pl.ds(start, vocab)],
            table_in.at[pl.ds(z * vocab, vocab)],
            x_sent.at[8],
            x_got.at[8],
            where.x_peer,
        ).start()
    share_ffn(0, d_both.at[pl.ds(8 * vocab, 8 * share)])
    finish_x(0, (3, 0, 1, 2))
    wait_bytes(table_in, x_got.at[8])
    for z in range(4):
        start = pl.multiple_of((z * 2 + where.x) * vocab, vocab)
        here = pl.ds(z * vocab, vocab)
        table_in[here, :] = (
            table_in[here, :].astype(F32) + d_both[pl.ds(start, vocab), :].astype(F32)
        ).astype(BF)
    send_z(table_in, table_got.at[where.z], 2, vocab, vocab)

    drain_ffn(0)
    for layer in (0, 1):
        wait_bytes(both_got.at[layer, pl.ds(0, 7)], f_got.at[3 * layer + 2])
        arrived, ends = f_got.at[3 * layer + 1], (index == 0) | (index == 15)
        pl.when(ends)(lambda: wait_bytes(down_got.at[layer, 0], arrived))
        pl.when(jnp.logical_not(ends))(lambda: wait_bytes(down_got.at[layer], arrived))
        wait_bytes(attn_got.at[layer], z_got.at[layer])
        wait_bytes(everyone.at[pl.ds(0, 12 * share)], z_sent.at[layer])
    for piece in range(4):
        wait_bytes(part.at[piece, pl.ds(0, 4 * share)], x_sent.at[piece])
    wait_bytes(table_got, z_got.at[2])
    wait_bytes(everyone.at[pl.ds(0, 3 * vocab)], z_sent.at[2])
    wait_bytes(d_both.at[pl.ds(0, 4 * vocab)], x_sent.at[8])
    grad_out.wait()
    wait_bytes(gain_got, g_got.at[0])
    wait_bytes(gain_got.at[pl.ds(0, 15)], g_sent.at[0])


def backward(
    cotangent, codes, codes_theirs, gain_rows, stream, middle, qkv, other, attended, normed, qkv0,
    qkv1, outs, both, down
):
    rows, width = cotangent.shape
    hidden = down.shape[1]
    share = width // 16
    vocab = codes.shape[1] // 8
    shape = jax.ShapeDtypeStruct
    hbm = pl.BlockSpec(memory_space=pl.ANY)
    vmem = pltpu.VMEM
    dma = pltpu.SemaphoreType.DMA
    return pl.pallas_call(
        backward_kernel,
        out_shape=(
            shape((rows, width), F32),
            shape((2, 8, share, 2 * hidden), BF),
            shape((2, 8 * share, 2 * hidden), BF),
            shape((2, 2, hidden // 2, width), BF),
            shape((2, 4, 4 * share, width), BF),
            shape((4, vocab, width), BF),
            shape((16, 8, 128), F32),
        ),
        in_specs=[hbm] * 3 + in_vmem(1) + [hbm] * 11,
        out_specs=tuple([hbm] * 7),
        scratch_shapes=[
            vmem((rows, width), F32),
            vmem((rows, width), F32),
            vmem((rows, 3 * width), BF),
            vmem((rows, 2 * width), BF),
            vmem((rows, width), BF),
            vmem((8 * rows, width), BF),
            vmem((width, 3 * width), BF),
            vmem((width, width), BF),
            vmem((width, 2 * hidden), BF),
            vmem((hidden, width), BF),
            vmem((rows, width), F32),
            vmem((rows, width), F32),
            vmem((rows, width), BF),
            vmem((2 * rows, width // 2), BF),
            vmem((2 * rows, width // 2), BF),
            vmem((2 * rows, 3 * width), BF),
            vmem((2 * rows, width), BF),
            vmem((2, rows, width // 2), BF),
            vmem((rows, width), BF),
            vmem((2, rows, width), BF),
            vmem((2 * rows, 8 * vocab), BF),
            vmem((2 * rows, width), BF),
            vmem((4, width // 2, width), BF),
            vmem((16 * share, width), BF),
            vmem((8 * rows, width), BF),
            vmem((8 * rows, hidden), BF),
            vmem((8 * rows, 2 * hidden), BF),
            vmem((4, rows, width), F32),
            vmem((width, 2 * hidden), BF),
            vmem((hidden, width), BF),
            vmem((8, width), F32),
            vmem((width, 128), BF),
            dma((15,)),
            dma((12,)),
            dma((12,)),
            dma((4,)),
            dma((4,)),
            dma((9,)),
            dma((9,)),
            dma((3,)),
            dma((3,)),
            dma((6,)),
            dma((6,)),
            dma((4,)),
            dma((1,)),
            dma((1,)),
            vmem((rows, 128), F32),
            vmem((2, rows, 128), F32),
        ]
        + Team.scratch(rows, width)[:8]
        + [dma((2, Team.SCRATCH_COPIES)), dma((2, Team.SCRATCH_COPIES))],
        compiler_params=pltpu.CompilerParams(
            collective_id=4, has_side_effects=True, vmem_limit_bytes=63 * 2**20
        ),
        name="backward_pass",
    )(
        cotangent,
        codes,
        codes_theirs,
        gain_rows,
        stream,
        middle,
        qkv,
        other,
        attended,
        normed,
        qkv0,
        qkv1,
        outs,
        both,
        down,
    )


def finish_kernel(both, down, attn, table, table_grad, qkv_grad, out_grad, gate_grad, up_grad, down_grad):
    hidden = both.shape[3] // 2
    share, width = both.shape[2], attn.shape[3]
    for layer in range(LAYERS):
        for member in range(8):
            columns = slice(member * hidden, (member + 1) * hidden)
            gate_grad[layer, 0, :, columns] = both[layer, member, :, :hidden].astype(F32)
            up_grad[layer, 0, :, columns] = both[layer, member, :, hidden:].astype(F32)
        down_grad[layer, 0] = down[layer, 0].astype(F32) + down[layer, 1].astype(F32)
        for piece in range(4):
            rows = slice(piece * share, (piece + 1) * share)
            value = sum(attn[layer, z, rows, :].astype(F32) for z in range(4))
            if piece < 3:
                qkv_grad[layer, 0, :, piece * width : (piece + 1) * width] = value
            else:
                out_grad[layer, 0] = value
    table_grad[0] = sum(table[z].astype(F32) for z in range(4))


def finish(both, down, attn, table):
    share, width = both.shape[2], attn.shape[3]
    hidden = both.shape[3] // 2
    shape = jax.ShapeDtypeStruct
    return pl.pallas_call(
        finish_kernel,
        out_shape=(
            shape((1,) + table.shape[1:], F32),
            shape((LAYERS, 1, share, 3 * width), F32),
            shape((LAYERS, 1, share, width), F32),
            shape((LAYERS, 1, share, 8 * hidden), F32),
            shape((LAYERS, 1, share, 8 * hidden), F32),
            shape((LAYERS, 1, hidden // 2, width), F32),
        ),
        in_specs=in_vmem(4),
        out_specs=tuple(in_vmem(6)),
        compiler_params=pltpu.CompilerParams(vmem_limit_bytes=48 * 2**20),
        name="finish",
    )(both, down, attn, table)


class Plan:
    def __init__(self, count):
        self.count = count
        self.team = 8
        self.teams = count // self.team
        self.across = [[g * self.team + t for g in range(self.teams)] for t in range(self.team)]

    def ffn_weights(self, gate, up, down):
        rows = gate.shape[0]
        both = jnp.stack([gate, up], axis=1).reshape(rows, 2, self.teams, self.team, -1)
        parts = both.transpose(3, 0, 1, 2, 4).reshape(self.team, rows, -1)
        parts = jnp.broadcast_to(parts[None], (self.teams,) + parts.shape)
        parts = parts.reshape((self.count,) + parts.shape[2:])
        mine = lax.all_to_all(parts, "frames", split_axis=0, concat_axis=0, tiled=True)
        return mine.reshape(self.count * rows, -1), self.gather_across(down)

    def gather_across(self, rows):
        if self.teams != 2:
            return lax.all_gather(rows, "frames", axis=0, tiled=True, axis_index_groups=self.across)
        theirs = lax.ppermute(rows, "frames", self.partners())
        first = lax.axis_index("frames") < self.team
        return jnp.concatenate([jnp.where(first, rows, theirs), jnp.where(first, theirs, rows)])

    def scatter_across(self, rows):
        if self.teams != 2:
            part = lax.psum_scatter(
                rows.astype(BF),
                "frames",
                scatter_dimension=0,
                tiled=True,
                axis_index_groups=self.across,
            )
            return part.astype(F32)
        half = rows.shape[0] // 2
        first = lax.axis_index("frames") < self.team
        mine = jnp.where(first, rows[:half], rows[half:])
        sent = jnp.where(first, rows[half:], rows[:half]).astype(BF)
        return mine + lax.ppermute(sent, "frames", self.partners()).astype(F32)

    def partners(self):
        return [(i, (i + self.team) % self.count) for i in range(self.count)]

    def ffn_grads(self, both_part, down_part):
        parts = both_part.astype(BF).reshape(self.count, -1, both_part.shape[1])
        parts = lax.all_to_all(parts, "frames", split_axis=0, concat_axis=0, tiled=True)
        rows = parts.shape[1]
        parts = parts.astype(F32).reshape(self.teams, self.team, rows, -1).sum(axis=0)
        down = self.scatter_across(down_part)
        parts = parts.reshape(self.team, rows, 2, self.teams, -1)
        both = parts.transpose(1, 2, 3, 0, 4).reshape(rows, 2, -1)
        return both[:, 0], both[:, 1], down


def attend(qkv, other):
    width = HEADS * HD
    position = lax.axis_index("pos")
    q, k, v = (qkv[:, i * width : (i + 1) * width].astype(F32) for i in range(3))
    k0, v0 = (other[:, i * width : (i + 1) * width].astype(F32) for i in range(2))
    own = head_sum(q * k) / math.sqrt(HD)
    past = jnp.where(position > 0, head_sum(q * k0) / math.sqrt(HD), -1e30)
    largest = jnp.maximum(own, past)
    own, past = jnp.exp(own - largest), jnp.exp(past - largest)
    total = own + past
    own, past = own / total, past / total
    attended = head_spread(own) * v + head_spread(past) * v0
    return attended.astype(BF), own, past


def attend_back(grad, qkv, other, own, past):
    width = HEADS * HD
    q, k, v = (qkv[:, i * width : (i + 1) * width].astype(F32) for i in range(3))
    k0, v0 = (other[:, i * width : (i + 1) * width].astype(F32) for i in range(2))
    grad = grad.astype(F32)
    d_own, d_past = head_sum(grad * v), head_sum(grad * v0)
    inner = own * d_own + past * d_past
    s_own = head_spread(own * (d_own - inner) / math.sqrt(HD))
    s_past = head_spread(past * (d_past - inner) / math.sqrt(HD))
    own, past = head_spread(own), head_spread(past)
    d_q = s_own * k + s_past * k0
    d_k = s_own * q
    d_v = own * grad
    d_other = jnp.concatenate([s_past * q, past * grad], axis=1)
    return d_q, d_k, d_v, d_other


def plain_forward(
    plan, onward, frames_in, onehot, code_table, w_qkv, w_out, w_gate, w_up, w_down, gain_attn, gain_ffn
):
    width = frames_in.shape[-1]
    gains = jnp.stack([gain_attn[0, 0], gain_attn[1, 0], gain_ffn[0, 0], gain_ffn[1, 0]], axis=1)
    gains = jnp.pad(gains, ((0, 0), (0, 124)))
    full_table = lax.all_gather(code_table[0], "frames", axis=0, tiled=True)
    first_qkv = lax.all_gather(
        jnp.concatenate([w_qkv[0, 0], gains], axis=1), "frames", axis=0, tiled=True
    )
    gain_rows = first_qkv[:, 3 * width : 3 * width + 4].astype(F32).T
    qkv_all = [first_qkv[:, : 3 * width], None]
    out_all = [lax.all_gather(w_out[0, 0], "frames", axis=0, tiled=True), None]
    ffn_all = [plan.ffn_weights(w_gate[0, 0], w_up[0, 0], w_down[0, 0]), None]
    qkv_all[1] = lax.all_gather(w_qkv[1, 0], "frames", axis=0, tiled=True)
    out_all[1] = lax.all_gather(w_out[1, 0], "frames", axis=0, tiled=True)
    ffn_all[1] = plan.ffn_weights(w_gate[1, 0], w_up[1, 0], w_down[1, 0])

    stream = frames_in[:, 0].astype(F32) + plain(onehot, full_table)
    kept = []
    for layer in range(LAYERS):
        inv_attn = inverse_rms(stream)
        normed_attn = (stream * inv_attn * gain_rows[layer]).astype(BF)
        qkv = plain(normed_attn, qkv_all[layer]).astype(BF)
        other = lax.ppermute(qkv[:, width:], "pos", onward)
        attended, own, past = attend(qkv, other)
        middle = stream + plain(attended, out_all[layer])
        inv_ffn = inverse_rms(middle)
        normed_ffn = (middle * inv_ffn * gain_rows[2 + layer]).astype(BF)
        both_all, down_all = ffn_all[layer]
        team_normed, summed = ffn_forward(normed_ffn, both_all, down_all)
        new_stream = middle + summed
        kept.append(
            (
                stream,
                inv_attn,
                normed_attn,
                qkv,
                other,
                own,
                past,
                attended,
                middle,
                inv_ffn,
                team_normed,
            )
        )
        stream = new_stream
    return kept, stream, gain_rows, qkv_all, out_all, ffn_all


def fused_body(
    onehot, frames_in, code_table, w_qkv, w_out, w_gate, w_up, w_down, gain_attn, gain_ffn, cotangent
):
    share = gain_attn.shape[-1]
    width = frames_in.shape[-1]
    gains = jnp.concatenate([gain_attn[:, 0], gain_ffn[:, 0]], axis=0).astype(F32)
    gains = jnp.pad(gains, ((0, 4), (0, share)))
    odd = lax.rem(lax.axis_index("frames"), 2) == 1
    gains = jnp.where(odd, jnp.roll(gains, share, axis=1), gains)
    act, *saved = forward(
        frames_in[:, 0],
        onehot,
        gains,
        code_table[0],
        w_qkv[:, 0],
        w_out[:, 0],
        w_gate[:, 0],
        w_up[:, 0],
        w_down[:, 0],
    )
    stream, middle, qkv, other, attended, normed, gain_rows, qkv0, qkv1, outs, both, down = saved
    blocks = onehot.reshape(onehot.shape[0], 8, 2, -1)
    first, second = (blocks[:, :, i].reshape(onehot.shape[0], -1) for i in (0, 1))
    codes, codes_theirs = jnp.where(odd, second, first), jnp.where(odd, first, second)
    input_grad, both_got, pair_got, down_got, attn_got, table_got, gain_got = backward(
        cotangent[:, 0],
        codes,
        codes_theirs,
        gain_rows,
        stream,
        middle,
        qkv,
        other,
        attended,
        normed,
        qkv0,
        qkv1,
        outs,
        both,
        down,
    )
    table, qkv_grad, out_grad, gate_grad, up_grad, down_grad = finish(
        both_got, down_got, attn_got, table_got
    )
    sums = gain_got.sum(axis=0)
    sums = jnp.where(odd, sums[:4, 64:], sums[:4, :64]).reshape(2, LAYERS, 1, share)
    return (
        act[:, None, :],
        input_grad[:, None, :],
        table,
        qkv_grad,
        out_grad,
        gate_grad,
        up_grad,
        down_grad,
        sums[0],
        sums[1],
    )


def body(
    frames_in,
    code_table,
    code_ids,
    delays,
    item_lengths,
    w_qkv,
    w_out,
    w_gate,
    w_up,
    w_down,
    gain_attn,
    gain_ffn,
    cotangent,
):
    count = lax.axis_size("frames")
    plan = Plan(count)
    positions = lax.axis_size("pos")
    onward = [(i, i + 1) for i in range(positions - 1)]
    backward = [(i + 1, i) for i in range(positions - 1)]
    local_frames = frames_in.shape[0]
    item_count = item_lengths.shape[0]
    width = frames_in.shape[-1]

    neighbours = [(i, i + 1) for i in range(count - 1)]
    earlier = lax.ppermute(code_ids[local_frames - 2 :], "frames", neighbours)
    extended = jnp.concatenate([earlier, code_ids], axis=0)[:, 0]
    global_frame = lax.axis_index("frames") * local_frames + jnp.arange(
        local_frames, dtype=jnp.int32
    )
    item_ends = jnp.cumsum(item_lengths)
    starts = item_ends - item_lengths
    item_index = jnp.sum((starts[None, :] <= global_frame[:, None]).astype(jnp.int32), axis=1) - 1
    chosen = item_index[:, None] == jnp.arange(item_count, dtype=jnp.int32)[None, :]
    item_begin = jnp.sum(jnp.where(chosen, starts[None, :], 0), axis=1)
    delay_rows = jnp.sum(jnp.where(chosen, delays[:, 0][None, :], 0), axis=1)
    one_back = extended[1 : local_frames + 1]
    two_back = extended[:local_frames]
    code_rows = jnp.where(delay_rows == 1, one_back, two_back)
    is_valid = global_frame - delay_rows >= item_begin
    vocab_size = code_table.shape[1] * count
    matches = code_rows[:, None] == jnp.arange(vocab_size, dtype=jnp.int32)[None, :]
    onehot = (matches & is_valid[:, None]).astype(BF)

    if count == 16:
        return fused_body(
            onehot, frames_in, code_table, w_qkv, w_out, w_gate, w_up, w_down, gain_attn, gain_ffn,
            cotangent,
        )
    kept, stream, gain_rows, qkv_all, out_all, ffn_all = plain_forward(
        plan, onward, frames_in, onehot, code_table, w_qkv, w_out, w_gate, w_up, w_down,
        gain_attn, gain_ffn,
    )
    output = stream.astype(BF)[:, None, :]

    gradient = cotangent[:, 0].astype(F32)
    collected = [None] * LAYERS
    gain_parts = [None] * (2 * LAYERS)
    for layer in reversed(range(LAYERS)):
        (
            stream,
            inv_attn,
            normed_attn,
            qkv,
            other,
            own,
            past,
            attended,
            middle,
            inv_ffn,
            team_normed,
        ) = kept[layer]
        both_all, down_all = ffn_all[layer]
        grad_normed, both_part, down_part = ffn_backward(
            gradient.astype(BF), both_all, down_all, team_normed
        )
        ffn_shares = plan.ffn_grads(both_part, down_part)
        grad_middle, gain_parts[2 + layer] = norm_back(
            grad_normed, middle, inv_ffn, gain_rows[2 + layer]
        )
        grad_middle = gradient + grad_middle
        grad_attn = grad_middle.astype(BF)
        grad_attended = right_trans(grad_attn, out_all[layer]).astype(BF)
        d_q, d_k, d_v, d_other = attend_back(grad_attended, qkv, other, own, past)
        arrived = lax.ppermute(d_other.astype(BF), "pos", backward).astype(F32)
        grad_qkv = jnp.concatenate([d_q, d_k + arrived[:, :width], d_v + arrived[:, width:]], axis=1)
        grad_qkv = grad_qkv.astype(BF)
        out_part = left_trans(attended, grad_attn).astype(BF)
        out_share = lax.psum_scatter(out_part, "frames", scatter_dimension=0, tiled=True)
        grad_normed_attn = right_trans(grad_qkv, qkv_all[layer])
        grad_stream, gain_parts[layer] = norm_back(
            grad_normed_attn, stream, inv_attn, gain_rows[layer]
        )
        gradient = grad_middle + grad_stream
        qkv_part = left_trans(normed_attn, grad_qkv).astype(BF)
        if layer == 0:
            tail = jnp.stack(gain_parts, axis=1).astype(BF)
            qkv_part = jnp.concatenate([qkv_part, jnp.pad(tail, ((0, 0), (0, 124)))], axis=1)
        qkv_share = lax.psum_scatter(qkv_part, "frames", scatter_dimension=0, tiled=True)
        collected[layer] = (qkv_share.astype(F32), out_share.astype(F32)) + ffn_shares
    table_part = left_trans(onehot, gradient.astype(BF)).astype(BF)
    table_share = lax.psum_scatter(table_part, "frames", scatter_dimension=0, tiled=True)
    gain_shares = collected[0][0][:, 3 * width : 3 * width + 4].T
    collected[0] = (collected[0][0][:, : 3 * width],) + collected[0][1:]
    stacked = [
        jnp.stack([collected[layer][slot] for layer in range(LAYERS)], axis=0)[:, None]
        for slot in range(5)
    ]
    return (
        output,
        gradient[:, None, :],
        table_share.astype(F32)[None],
        stacked[0],
        stacked[1],
        stacked[2],
        stacked[3],
        stacked[4],
        gain_shares[:2][:, None],
        gain_shares[2:][:, None],
    )


def solution(mesh):
    return jax.shard_map(
        body,
        mesh=mesh,
        in_specs=(
            P("frames", "pos", None),
            P("pos", "frames", None),
            P("frames", "pos"),
            P(None, "pos"),
            P(),
            P(None, "pos", "frames", None),
            P(None, "pos", "frames", None),
            P(None, "pos", "frames", None),
            P(None, "pos", "frames", None),
            P(None, "pos", "frames", None),
            P(None, "pos", "frames"),
            P(None, "pos", "frames"),
            P("frames", "pos", None),
        ),
        out_specs=(
            P("frames", "pos", None),
            P("frames", "pos", None),
            P("pos", "frames", None),
            P(None, "pos", "frames", None),
            P(None, "pos", "frames", None),
            P(None, "pos", "frames", None),
            P(None, "pos", "frames", None),
            P(None, "pos", "frames", None),
            P(None, "pos", "frames"),
            P(None, "pos", "frames"),
        ),
        check_vma=False,
    )
```
